32 devices in a mesh: shard: 4 (over z), ctx: 2 (over x), tp: 4 (over y, core).
Axes of the slice: x: 2, y: 2, z: 4, core: 2. Of those that a mesh axis runs over, the one named last changes fastest.
Arguments:
- video_tokens: bfloat16 [4, 1568, 1024], P('shard', 'ctx'), may hold values from -6 to 6
- qkv_weight: bfloat16 [1024, 3, 1024], P(('shard', 'ctx'), None, 'tp'), may hold values from -0.1875 to 0.1875
- q_bias: bfloat16 [1024], P('tp'), may hold values from -3 to 3
- v_bias: bfloat16 [1024], P('tp'), may hold values from -0.59765625 to 0.59765625
- proj_weight: bfloat16 [1024, 1024], P('tp', ('shard', 'ctx')), may hold values from -0.75 to 0.75
- proj_bias: bfloat16 [1024], replicated, may hold values from -2 to 2
- norm1_gain: bfloat16 [1024], replicated, may hold values from 0.5 to 1.5
- norm1_shift: bfloat16 [1024], replicated, may hold values from -2 to 2
- norm2_gain: bfloat16 [1024], replicated, may hold values from 0.5 to 1.5
- norm2_shift: bfloat16 [1024], replicated, may hold values from -2 to 2
- fc1_weight: bfloat16 [1024, 4096], P(('shard', 'ctx'), 'tp'), may hold values from -0.1875 to 0.1875
- fc1_bias: bfloat16 [4096], P('tp'), may hold values from -3 to 3
- fc2_weight: bfloat16 [4096, 1024], P('tp', ('shard', 'ctx')), may hold values from -0.09375 to 0.09375
- fc2_bias: bfloat16 [1024], replicated, may hold values from -2 to 2
- out_grad: bfloat16 [4, 1568, 1024], P('shard', 'ctx'), may hold values from -6 to 6
Outputs:
- layer_out: bfloat16 [4, 1568, 1024], P('shard', 'ctx')
- input_grad: bfloat16 [4, 1568, 1024], P('shard', 'ctx')
- grad_qkv_weight: float32 [1024, 3, 1024], P(('shard', 'ctx'), None, 'tp')
- grad_q_bias: float32 [1024], P('tp')
- grad_v_bias: float32 [1024], P('tp')
- grad_proj_weight: float32 [1024, 1024], P('tp', ('shard', 'ctx'))
- grad_proj_bias: float32 [1024], replicated
- grad_norm1_gain: float32 [1024], replicated
- grad_norm1_shift: float32 [1024], replicated
- grad_norm2_gain: float32 [1024], replicated
- grad_norm2_shift: float32 [1024], replicated
- grad_fc1_weight: float32 [1024, 4096], P(('shard', 'ctx'), 'tp')
- grad_fc1_bias: float32 [4096], P('tp')
- grad_fc2_weight: float32 [4096, 1024], P('tp', ('shard', 'ctx'))
- grad_fc2_bias: float32 [1024], replicated
The draws below stay inside these ranges and needn't reach their ends.
All inputs are finite; a program needn't handle non-finite values.
Results may differ from the reference program's by a relative error of at most 0.014.
Values may be sent and summed in bfloat16 or wider, within the bound.
No kernel may reach another device: no remote copies, remote signals or barrier semaphores. Data moves between devices by JAX's collectives and lax.ppermute only.
A program may use at most 128 MiB of HBM per device.

```python
import jax
import jax.numpy as jnp
from jax import lax

D = 1024
HEADS = 16
FF = 4096
CLIP = 1568
HD = 64
CLIPS = 4


def block_scale(stream_key, extent, shards, least, largest):
    loudness, own = 1.0, jax.random.fold_in(stream_key, 6)
    for axis_at, parts in shards:
        steps = jnp.exp(jax.random.uniform(jax.random.fold_in(own, axis_at), (parts,), jnp.float32, least / len(shards), largest / len(shards)))
        loudness = loudness * jnp.repeat(steps, extent[axis_at] // parts).reshape([-1 if axis == axis_at else 1 for axis in range(len(extent))])
    return loudness


def noise(own_key, shape, deviation, limit, pieces=(), held_as=jnp.bfloat16):
    loudness = block_scale(own_key, shape, pieces, -0.22, 0.18) if pieces else 1.0
    drawn = jax.random.normal(own_key, shape, jnp.float32) * deviation * loudness
    return jnp.minimum(jnp.maximum(drawn, -limit), limit).astype(held_as)


def setup_inputs(seed: int = 0) -> dict:
    key_of = jax.random.split(jax.random.key(seed), 16)
    return {
        "video_tokens": noise(key_of[0], (CLIPS, CLIP, D), 1.0, 6.0, ((0, 4), (1, 2))),
        "qkv_weight": noise(key_of[1], (D, 3, D), D ** -0.5, 0.1875, ((0, 8), (2, 4))),
        "q_bias": noise(key_of[2], (D,), 0.5, 3.0, ((0, 4),)),
        "v_bias": noise(key_of[3], (D,), 0.1, 0.59765625, ((0, 4),)),
        "proj_weight": noise(key_of[4], (D, D), (max(D // 16, 1)) ** -0.5, 0.75, ((0, 4), (1, 8))),
        "proj_bias": noise(key_of[5], (D,), 0.3, 2.0),
        "norm1_gain": jnp.clip(1.0 + 0.1 * jax.random.normal(key_of[6], (D,), jnp.float32), 0.5, 1.5).astype(jnp.bfloat16),
        "norm1_shift": noise(key_of[7], (D,), 0.3, 2.0),
        "norm2_gain": jnp.clip(1.0 + 0.1 * jax.random.normal(key_of[8], (D,), jnp.float32), 0.5, 1.5).astype(jnp.bfloat16),
        "norm2_shift": noise(key_of[9], (D,), 0.3, 2.0),
        "fc1_weight": noise(key_of[10], (D, FF), D ** -0.5, 0.1875, ((0, 8), (1, 4))),
        "fc1_bias": noise(key_of[11], (FF,), 0.5, 3.0, ((0, 4),)),
        "fc2_weight": noise(key_of[12], (FF, D), FF ** -0.5, 0.09375, ((0, 4), (1, 8))),
        "fc2_bias": noise(key_of[13], (D,), 0.3, 2.0),
        "out_grad": noise(key_of[14], (CLIPS, CLIP, D), 1.0, 6.0, ((0, 4), (1, 2))),
    }


norm_eps = 1e-06
highest = lax.Precision.HIGHEST

@jax.custom_vjp
def low(v):
    return lax.optimization_barrier(v.astype(jnp.bfloat16)).astype(jnp.float32)

@jax.custom_vjp
def low_back(v):
    return v

def low_keep(v):
    return (low(v), None)

def low_pass(kept, grad):
    return (grad,)

def back_keep(v):
    return (v, None)

def back_low(kept, grad):
    return (low(grad),)
low.defvjp(low_keep, low_pass)
low_back.defvjp(back_keep, back_low)

def norm_rows(values, gain, shift):
    row_mean = lax.optimization_barrier(jnp.mean(values, axis=-1, keepdims=True))
    centered = values - row_mean
    variance = lax.optimization_barrier(jnp.mean(centered * centered, axis=-1, keepdims=True))
    return centered * lax.rsqrt(variance + norm_eps) * gain + shift

def matmul(left, right):
    return jnp.dot(left, right, precision=highest, preferred_element_type=jnp.float32)

def clip_layer(params, clip_in):
    qkv_weight, q_bias, v_bias, proj_weight, proj_bias, norm1_gain, norm1_shift, norm2_gain, norm2_shift, fc1_weight, fc1_bias, fc2_weight, fc2_bias = params
    score_scale = HD ** (-0.5)
    normed = low(norm_rows(clip_in, norm1_gain, norm1_shift))
    queries = low_back(low(matmul(normed, qkv_weight[:, 0, :]) + q_bias))
    key_rows = low_back(low(matmul(normed, qkv_weight[:, 1, :])))
    value_rows = low_back(low(matmul(normed, qkv_weight[:, 2, :]) + v_bias))
    head_q = queries.reshape(CLIP, HEADS, HD)
    head_k = key_rows.reshape(CLIP, HEADS, HD)
    head_v = value_rows.reshape(CLIP, HEADS, HD)
    scores = jnp.einsum('qhd,khd->hqk', head_q, head_k, precision=highest) * score_scale
    scores = low_back(scores)
    probs_low = low(jax.nn.softmax(scores, axis=-1))
    mixture = jnp.einsum('hqk,khd->qhd', probs_low, head_v, precision=highest).reshape(CLIP, D)
    mixture = low_back(low(mixture))
    attention = low_back(matmul(mixture, proj_weight) + proj_bias)
    middle = clip_in + attention
    second = low(norm_rows(middle, norm2_gain, norm2_shift))
    pre_act = low_back(matmul(second, fc1_weight) + fc1_bias)
    hidden = low(jax.nn.gelu(pre_act, approximate=False))
    branch = low_back(matmul(hidden, fc2_weight) + fc2_bias)
    return middle + branch

def reference(video_tokens, qkv_weight, q_bias, v_bias, proj_weight, proj_bias, norm1_gain, norm1_shift, norm2_gain, norm2_shift, fc1_weight, fc1_bias, fc2_weight, fc2_bias, out_grad):
    params = tuple((param.astype(jnp.float32) for param in (qkv_weight, q_bias, v_bias, proj_weight, proj_bias, norm1_gain, norm1_shift, norm2_gain, norm2_shift, fc1_weight, fc1_bias, fc2_weight, fc2_bias)))

    def one_clip(grad_sums, clip_pair):
        clip_in, clip_grad = clip_pair
        clip_out, pullback = jax.vjp(clip_layer, params, clip_in.astype(jnp.float32))
        param_grads, in_grad = pullback(clip_grad.astype(jnp.float32))
        grad_sums = jax.tree.map(lambda left, right: left + right, grad_sums, param_grads)
        return (grad_sums, (clip_out.astype(jnp.bfloat16), in_grad.astype(jnp.bfloat16)))
    zeros_start = tuple((jnp.zeros_like(param) for param in params))
    grad_sums, (layer_out, input_grad) = lax.scan(one_clip, zeros_start, (video_tokens, out_grad))
    return (layer_out, input_grad, grad_sums[0], grad_sums[1], grad_sums[2], grad_sums[3], grad_sums[4], grad_sums[5], grad_sums[6], grad_sums[7], grad_sums[8], grad_sums[9], grad_sums[10], grad_sums[11], grad_sums[12])
```

```python
import functools

import jax
import jax.numpy as jnp
from jax import lax
from jax.experimental import pallas as pl
from jax.experimental.pallas import tpu as pltpu
from jax.sharding import PartitionSpec as P

HD = 64
HEADS = 4
WIDTH = HEADS * HD
QTILE = 112
KTILE = 112

norm_eps = 1e-06
bf16, f32 = jnp.bfloat16, jnp.float32
VMEM_LIMIT = 32 * 1024 * 1024

CTX_PAIRS = [(0, 1), (1, 0)]
CORE_PAIRS = [(0, 1), (1, 0), (2, 3), (3, 2)]
FAR_PAIRS = [(0, 2), (2, 0), (1, 3), (3, 1)]


def params(**more):
    return pltpu.CompilerParams(vmem_limit_bytes=VMEM_LIMIT, **more)


def norm_rows(values, gain, shift):
    row_mean = jnp.mean(values, axis=-1, keepdims=True)
    centered = values - row_mean
    variance = jnp.mean(centered * centered, axis=-1, keepdims=True)
    return centered * lax.rsqrt(variance + norm_eps) * gain + shift


def dot_nn(left, right):
    return jnp.dot(left, right, preferred_element_type=f32)


def dot_tn(left, right):
    return lax.dot_general(left, right, (((0,), (0,)), ((), ())), preferred_element_type=f32)


def dot_nt(left, right):
    return lax.dot_general(left, right, (((1,), (1,)), ((), ())), preferred_element_type=f32)


def ctx_swap(value):
    return lax.ppermute(value, "ctx", CTX_PAIRS)


def ring_gather(piece, count):
    down = [(i, (i - 1) % count) for i in range(count)]
    pieces = [piece]
    for _ in range(count - 1):
        pieces.append(lax.ppermute(pieces[-1], "shard", down))
    return pieces


def ring_scatter(kept, count):
    up = [(i, (i + 1) % count) for i in range(count)]
    me = lax.axis_index("shard")

    def block(step):
        return lax.dynamic_index_in_dim(kept, (me + step) % count, 0, keepdims=False)

    if count == 1:
        return block(0).astype(f32)
    total = block(count - 1).astype(bf16)
    for step in range(count - 2, -1, -1):
        arrived = lax.ppermute(total, "shard", up)
        total = block(step).astype(f32) + arrived.astype(f32)
        if step:
            total = total.astype(bf16)
    return total


def assemble_kernel(count, rows, *refs):
    pieces, out = refs[: 2 * count], refs[2 * count]
    shard, ctx = lax.axis_index("shard"), lax.axis_index("ctx")
    for side in range(2):
        for step in range(count):
            owner = lax.rem(shard + step, count) * 2 + (ctx + side) % 2
            out[pl.ds(pl.multiple_of(owner * rows, rows), rows), :] = pieces[side * count + step][...]


def assemble(own, other):
    count = len(own)
    rows, columns = own[0].shape
    return pl.pallas_call(
        functools.partial(assemble_kernel, count, rows),
        out_shape=jax.ShapeDtypeStruct((2 * count * rows, columns), bf16),
        compiler_params=params(),
        name="assemble",
    )(*own, *other)


def tp_sum(terms):
    core = lax.axis_index("tp") % 2
    half = terms.shape[0] // 2
    keep = lax.dynamic_slice_in_dim(terms, core * half, half, 0)
    send = lax.dynamic_slice_in_dim(terms, (1 - core) * half, half, 0)
    near = (keep.astype(f32) + lax.ppermute(send, "tp", CORE_PAIRS).astype(f32)).astype(bf16)
    near = lax.optimization_barrier(near)
    total = (near.astype(f32) + lax.ppermute(near, "tp", FAR_PAIRS).astype(f32)).astype(bf16)
    total = lax.optimization_barrier(total)
    other = lax.ppermute(total, "tp", CORE_PAIRS)
    return jnp.where(core == 0, jnp.concatenate([total, other]), jnp.concatenate([other, total]))


def small_sum(vector, count):
    vector = vector + ctx_swap(vector)
    step = 1
    while step < count:
        vector = vector + lax.ppermute(vector, "shard", [(i, i ^ step) for i in range(count)])
        step *= 2
    return vector


def head_mask(shape, head):
    lane = lax.broadcasted_iota(jnp.int32, shape, len(shape) - 1)
    return (lane >= head * HD) & (lane < (head + 1) * HD)


def fwd_near_kernel(q_ref, kv_ref, o_ref, m_ref, l_ref):
    q = q_ref[...]
    keys, values = kv_ref[:, :WIDTH], kv_ref[:, WIDTH:]
    rows = q.shape[0]
    o = jnp.zeros((rows, WIDTH), f32)
    m = jnp.zeros((rows, WIDTH), f32)
    total = jnp.zeros((rows, WIDTH), f32)
    for head in range(HEADS):
        mask = head_mask((rows, WIDTH), head)
        scores = dot_nt(jnp.where(mask, q, jnp.zeros_like(q)), keys)
        top = jnp.max(scores, axis=-1, keepdims=True)
        weights = jnp.exp(scores - top)
        row_sum = jnp.sum(weights, axis=-1, keepdims=True)
        mixed = dot_nn(weights.astype(bf16), values)
        o = jnp.where(mask, mixed, o)
        m = jnp.where(mask, top, m)
        total = jnp.where(mask, row_sum, total)
    o_ref[...] = o
    m_ref[...] = m
    l_ref[...] = total


def fwd_far_kernel(q_ref, kv_ref, o_ref, m_ref, l_ref, mix_ref, lse_ref):
    q = q_ref[...]
    keys, values = kv_ref[:, :WIDTH], kv_ref[:, WIDTH:]
    rows = q.shape[0]
    o, m, total = o_ref[...], m_ref[...], l_ref[...]
    o_out = jnp.zeros((rows, WIDTH), f32)
    lse = jnp.zeros((rows, 128), f32)
    lane = lax.broadcasted_iota(jnp.int32, (rows, 128), 1)
    for head in range(HEADS):
        mask = head_mask((rows, WIDTH), head)
        scores = dot_nt(jnp.where(mask, q, jnp.zeros_like(q)), keys)
        before = m[:, head * HD : head * HD + 1]
        top = jnp.maximum(jnp.max(scores, axis=-1, keepdims=True), before)
        weights = jnp.exp(scores - top)
        carry = jnp.exp(before - top)
        row_sum = jnp.sum(weights, axis=-1, keepdims=True) + carry * total[:, head * HD : head * HD + 1]
        mixed = dot_nn(weights.astype(bf16), values) + carry * o
        o_out = jnp.where(mask, mixed / row_sum, o_out)
        lse = jnp.where(lane == head, top + jnp.log(row_sum), lse)
    mix_ref[...] = o_out.astype(bf16)
    lse_ref[...] = lse


def attention_near(q, kv):
    rows, keys = q.shape[0], kv.shape[0]
    tile = pl.BlockSpec((QTILE, WIDTH), lambda i: (i, 0))
    return pl.pallas_call(
        fwd_near_kernel,
        grid=(rows // QTILE,),
        out_shape=[jax.ShapeDtypeStruct((rows, WIDTH), f32)] * 3,
        in_specs=[tile, pl.BlockSpec((keys, 2 * WIDTH), lambda i: (0, 0))],
        out_specs=[tile] * 3,
        compiler_params=params(),
        cost_estimate=pl.CostEstimate(flops=16 * rows * keys * WIDTH, bytes_accessed=1 << 22, transcendentals=0),
        name="attention_near",
    )(q, kv)


def attention_far(q, kv, o, m, total):
    rows, keys = q.shape[0], kv.shape[0]
    tile = pl.BlockSpec((QTILE, WIDTH), lambda i: (i, 0))
    return pl.pallas_call(
        fwd_far_kernel,
        grid=(rows // QTILE,),
        out_shape=[jax.ShapeDtypeStruct((rows, WIDTH), bf16), jax.ShapeDtypeStruct((rows, 128), f32)],
        in_specs=[tile, pl.BlockSpec((keys, 2 * WIDTH), lambda i: (0, 0)), tile, tile, tile],
        out_specs=[tile, pl.BlockSpec((QTILE, 128), lambda i: (i, 0))],
        compiler_params=params(),
        cost_estimate=pl.CostEstimate(flops=16 * rows * keys * WIDTH, bytes_accessed=1 << 22, transcendentals=0),
        name="attention_far",
    )(q, kv, o, m, total)


def bwd_kernel(k_ref, v_ref, q_ref, do_ref, lse_ref, delta_ref, dkv_ref, dq_ref):
    @pl.when(pl.program_id(0) == 0)
    def _():
        dq_ref[...] = jnp.zeros_like(dq_ref)

    q, d_out = q_ref[...], do_ref[...]
    keys, values = k_ref[...], v_ref[...]
    rows = keys.shape[0]
    dk = jnp.zeros((rows, WIDTH), f32)
    dv = jnp.zeros((rows, WIDTH), f32)
    dq = dq_ref[...]
    for head in range(HEADS):
        mask = head_mask((rows, WIDTH), head)
        head_k = jnp.where(mask, keys, jnp.zeros_like(keys))
        head_v = jnp.where(mask, values, jnp.zeros_like(values))
        probs = jnp.exp(dot_nt(head_k, q) - lse_ref[head : head + 1, :])
        d_probs = dot_nt(head_v, d_out)
        dv = jnp.where(mask, dot_nn(probs.astype(bf16), d_out), dv)
        d_scores = (probs * (d_probs - delta_ref[head : head + 1, :])).astype(bf16)
        dk = jnp.where(mask, dot_nn(d_scores, q), dk)
        dq = dq + dot_tn(d_scores, head_k)
    dkv_ref[:, :WIDTH] = dk
    dkv_ref[:, WIDTH:] = dv
    dq_ref[...] = dq


def attention_back(q, kv, d_out, lse, delta):
    rows, keys = q.shape[0], kv.shape[0]
    whole = pl.BlockSpec((rows, WIDTH), lambda i: (0, 0))
    line = pl.BlockSpec(lse.shape, lambda i: (0, 0))
    return pl.pallas_call(
        bwd_kernel,
        grid=(keys // KTILE,),
        out_shape=[jax.ShapeDtypeStruct((keys, 2 * WIDTH), f32), jax.ShapeDtypeStruct((rows, WIDTH), f32)],
        in_specs=[
            pl.BlockSpec((KTILE, WIDTH), lambda i: (i, 0)),
            pl.BlockSpec((KTILE, WIDTH), lambda i: (i, 1)),
            whole,
            whole,
            line,
            line,
        ],
        out_specs=[pl.BlockSpec((KTILE, 2 * WIDTH), lambda i: (i, 0)), whole],
        compiler_params=params(),
        cost_estimate=pl.CostEstimate(flops=40 * rows * keys * WIDTH, bytes_accessed=1 << 22, transcendentals=0),
        name="attention_back",
    )(kv, kv, q, d_out, lse, delta)


def layer(
    count,
    video_tokens,
    qkv_weight,
    q_bias,
    v_bias,
    proj_weight,
    proj_bias,
    norm1_gain,
    norm1_shift,
    norm2_gain,
    norm2_shift,
    fc1_weight,
    fc1_bias,
    fc2_weight,
    fc2_bias,
    out_grad,
):
    score_scale = HD ** (-0.5)
    inputs = video_tokens[0].astype(f32)
    ctx = lax.axis_index("ctx")
    (q_bias_f, v_bias_f, proj_bias_f, gain_one, shift_one, gain_two, shift_two, fc1_bias_f, fc2_bias_f) = (
        param.astype(f32)
        for param in (q_bias, v_bias, proj_bias, norm1_gain, norm1_shift, norm2_gain, norm2_shift, fc1_bias, fc2_bias)
    )
    piece_a = jnp.concatenate([qkv_weight[:, 0], qkv_weight[:, 1], qkv_weight[:, 2], proj_weight.T], axis=1)
    own_a = ring_gather(piece_a, count)
    other_a = [ctx_swap(piece) for piece in own_a]
    piece_1, piece_2, _ = lax.optimization_barrier((fc1_weight, fc2_weight.T, own_a[-1]))
    own_1 = ring_gather(piece_1, count)
    own_2 = ring_gather(piece_2, count)
    weight_a = assemble(own_a, other_a)
    qkv_w, proj_t = weight_a[:, : 3 * WIDTH], weight_a[:, 3 * WIDTH :]

    normed, norm1_pull = jax.vjp(norm_rows, inputs, gain_one, shift_one)
    normed_b = normed.astype(bf16)
    projected = dot_nn(normed_b, qkv_w)
    queries = ((projected[:, :WIDTH] + q_bias_f).astype(bf16).astype(f32) * score_scale).astype(bf16)
    kv = jnp.concatenate(
        [projected[:, WIDTH : 2 * WIDTH].astype(bf16), (projected[:, 2 * WIDTH :] + v_bias_f).astype(bf16)], axis=1
    )
    kv_far = ctx_swap(kv)
    partial = attention_near(queries, kv)
    own_1, own_2, kv_far = lax.optimization_barrier((own_1, own_2, kv_far))
    other_1 = [ctx_swap(piece) for piece in own_1]
    other_2 = [ctx_swap(piece) for piece in own_2]
    mixture_b, lse = attention_far(queries, kv_far, *partial)
    attn_sum = tp_sum(dot_nt(mixture_b, proj_t).astype(bf16))
    weight_1 = assemble(own_1, other_1)
    weight_2 = assemble(own_2, other_2)

    middle = inputs + attn_sum.astype(f32) + proj_bias_f
    second, norm2_pull = jax.vjp(norm_rows, middle, gain_two, shift_two)
    second_b = second.astype(bf16)
    pre_act = dot_nn(second_b, weight_1) + fc1_bias_f
    hidden_f, gelu_pull = jax.vjp(lambda v: jax.nn.gelu(v, approximate=False), pre_act)
    hidden_b = hidden_f.astype(bf16)
    grad_b = out_grad[0]
    grad_f = grad_b.astype(f32)
    d_hidden = dot_nn(grad_b, weight_2)
    d_pre_b = gelu_pull(d_hidden)[0].astype(bf16)
    d_second = tp_sum(dot_nt(d_pre_b, weight_1).astype(bf16)).astype(f32)
    mlp_sum = tp_sum(dot_nt(hidden_b, weight_2).astype(bf16))
    out_rows = (middle + mlp_sum.astype(f32) + fc2_bias_f).astype(bf16)

    def scatter(grads):
        width, columns = grads.shape
        rows = width // (2 * count)
        split = grads.reshape(count, 2, rows, columns)
        keep = lax.dynamic_index_in_dim(split, ctx, 1, keepdims=False)
        send = lax.dynamic_index_in_dim(split, 1 - ctx, 1, keepdims=False).astype(bf16)
        kept = keep.astype(f32) + ctx_swap(send).astype(f32)
        return ring_scatter(kept, count)

    d_fc1 = dot_tn(second_b, d_pre_b)
    d_fc2_t = dot_tn(grad_b, hidden_b)
    grad_fc1 = scatter(d_fc1)
    grad_fc2 = scatter(d_fc2_t).T
    d_fc1_bias = jnp.sum(d_pre_b.astype(f32), axis=0)
    d_fc2_bias = jnp.sum(grad_f, axis=0)

    d_mid_norm, d_gain_two, d_shift_two = norm2_pull(d_second)
    d_middle = grad_f + d_mid_norm
    d_middle_b = d_middle.astype(bf16)
    d_proj_t = dot_tn(d_middle_b, mixture_b)
    d_proj_bias = jnp.sum(d_middle_b.astype(f32), axis=0)
    d_mixture_b = dot_nn(d_middle_b, proj_t).astype(bf16)
    early = small_sum(jnp.concatenate([d_fc1_bias, d_fc2_bias, d_gain_two, d_shift_two, d_proj_bias]), count)

    rows = d_mixture_b.shape[0]
    delta = jnp.sum((d_mixture_b.astype(f32) * mixture_b.astype(f32)).reshape(rows, HEADS, HD), axis=-1)
    delta_t, lse_t = delta.T, lse[:, :HEADS].T
    dkv_away, dq_away = attention_back(queries, kv_far, d_mixture_b, lse_t, delta_t)
    dkv_back = ctx_swap(dkv_away.astype(bf16))
    dkv_here, dq_here = attention_back(queries, kv, d_mixture_b, lse_t, delta_t)
    d_query_b = ((dq_away + dq_here) * score_scale).astype(bf16)
    d_kv_b = (dkv_here + dkv_back.astype(f32)).astype(bf16)
    d_projected = jnp.concatenate([d_query_b, d_kv_b], axis=1)
    d_q_bias = jnp.sum(d_query_b.astype(f32), axis=0)
    d_v_bias = jnp.sum(d_kv_b[:, WIDTH:].astype(f32), axis=0)
    d_normed = tp_sum(dot_nt(d_projected, qkv_w).astype(bf16)).astype(f32)
    d_qkv = dot_tn(normed_b, d_projected)
    grad_a = scatter(jnp.concatenate([d_qkv, d_proj_t], axis=1))
    grad_qkv = grad_a[:, : 3 * WIDTH].reshape(-1, 3, WIDTH)
    grad_proj = grad_a[:, 3 * WIDTH :].T
    d_in_norm, d_gain_one, d_shift_one = norm1_pull(d_normed)
    input_grad = (d_middle + d_in_norm).astype(bf16)
    late = small_sum(jnp.concatenate([d_q_bias, d_v_bias, d_gain_one, d_shift_one]), count)
    width, hidden = inputs.shape[1], fc1_bias.shape[0]
    g_fc1_bias, g_fc2_bias, g_gain_two, g_shift_two, g_proj_bias = (
        early[:hidden],
        *(early[hidden + i * width : hidden + (i + 1) * width] for i in range(4)),
    )
    return (
        out_rows[None],
        input_grad[None],
        grad_qkv,
        late[:WIDTH],
        late[WIDTH : 2 * WIDTH],
        grad_proj,
        g_proj_bias,
        late[2 * WIDTH : 2 * WIDTH + width],
        late[2 * WIDTH + width :],
        g_gain_two,
        g_shift_two,
        grad_fc1,
        g_fc1_bias,
        grad_fc2,
        g_fc2_bias,
    )


def solution(mesh):
    split = ("shard", "ctx")
    tokens, rows, columns = P("shard", "ctx", None), P(split, "tp"), P("tp", split)
    stack = P(split, None, "tp")
    own, copied = P("tp"), P()
    in_specs = (
        tokens,
        stack,
        own,
        own,
        columns,
        copied,
        copied,
        copied,
        copied,
        copied,
        rows,
        own,
        columns,
        copied,
        tokens,
    )
    out_specs = (
        tokens,
        tokens,
        stack,
        own,
        own,
        columns,
        copied,
        copied,
        copied,
        copied,
        copied,
        rows,
        own,
        columns,
        copied,
    )
    return jax.shard_map(
        functools.partial(layer, mesh.shape["shard"]),
        mesh=mesh,
        in_specs=in_specs,
        out_specs=out_specs,
        check_vma=False,
    )
```

```python
import functools

import jax
import jax.numpy as jnp
from jax import lax
from jax.experimental import pallas as pl
from jax.experimental.pallas import tpu as pltpu
from jax.sharding import PartitionSpec as P

HD = 64
HEADS = 4
WIDTH = HEADS * HD
QTILE = 112

norm_eps = 1e-06
bf16, f32 = jnp.bfloat16, jnp.float32
VMEM_LIMIT = 24 * 1024 * 1024
SPLITS = ((0, 336), (336, 448))

CTX_PAIRS = [(0, 1), (1, 0)]
CORE_PAIRS = [(0, 1), (1, 0), (2, 3), (3, 2)]
FAR_PAIRS = [(0, 2), (2, 0), (1, 3), (3, 1)]


def cost(micros):
    return pl.CostEstimate(flops=int(micros * 1e7), bytes_accessed=0, transcendentals=0)


def call(kernel, outs, micros, name, scratch=()):
    return pl.pallas_call(
        kernel,
        out_shape=[jax.ShapeDtypeStruct(shape, dtype) for shape, dtype in outs],
        scratch_shapes=scratch,
        compiler_params=pltpu.CompilerParams(vmem_limit_bytes=VMEM_LIMIT),
        cost_estimate=cost(micros),
        name=name,
    )


def dot_nn(left, right):
    return jnp.dot(left, right, preferred_element_type=f32)


def dot_tn(left, right):
    return lax.dot_general(left, right, (((0,), (0,)), ((), ())), preferred_element_type=f32)


def dot_nt(left, right):
    return lax.dot_general(left, right, (((1,), (1,)), ((), ())), preferred_element_type=f32)


def tie(value, *before):
    return lax.optimization_barrier((value, *before))[0]


def ctx_swap(value):
    return lax.ppermute(value, "ctx", CTX_PAIRS)


def core_swap(value):
    return lax.ppermute(value, "tp", CORE_PAIRS)


def far_swap(value):
    return lax.ppermute(value, "tp", FAR_PAIRS)


def ring_down(value, count):
    return lax.ppermute(value, "shard", [(i, (i - 1) % count) for i in range(count)])


def ring_up(value, count):
    return lax.ppermute(value, "shard", [(i, (i + 1) % count) for i in range(count)])


class Order:
    def __init__(self):
        self.last = None

    def __call__(self, work, *values):
        if self.last is not None:
            values = lax.optimization_barrier((*values, self.last))[:-1]
        result = work(*values)
        self.last = min(jax.tree.leaves(result), key=lambda leaf: leaf.size)
        return result

    def wait(self, value):
        value, self.last = lax.optimization_barrier((value, self.last))
        return value


def add_low(left, right):
    return (left.astype(f32) + right.astype(f32)).astype(bf16)


class TpSum:
    def __init__(self, order, keep, send):
        self.order, self.keep = order, keep
        self.arrived = core_swap(send)

    def far(self):
        self.near = lax.optimization_barrier(self.order(add_low, self.keep, self.arrived))
        self.arrived = far_swap(self.near)

    def back(self):
        total = lax.optimization_barrier(self.order(add_low, self.near, self.arrived))
        self.result = (total, core_swap(total))


class SwapScatter:
    def __init__(self, order, count, keep, high, low):
        self.order, self.count, self.keep = order, count, keep
        self.high, self.low = ctx_swap(high), ctx_swap(low)
        self.rows, self.at, self.arrived = keep.shape[0] // count, count - 1, None

    def step(self):
        rows, half, at = self.rows, self.count // 2, self.at
        other, first = (self.high, half) if at >= half else (self.low, 0)

        def total(keep, other, *arrived):
            here = keep[at * rows : (at + 1) * rows].astype(f32)
            there = other[(at - first) * rows : (at - first + 1) * rows].astype(f32)
            value = here + there + sum(part.astype(f32) for part in arrived)
            return value.astype(bf16) if at else value

        arrived = [] if self.arrived is None else [self.arrived]
        value = self.order(total, self.keep, other, *arrived)
        if at:
            self.arrived, self.at = ring_up(value, self.count), at - 1
        else:
            self.result = value


class RingScatter:
    def __init__(self, order, count, grads, last):
        self.order, self.count, self.grads = order, count, grads
        self.rows, self.at = grads.shape[0] // count, count - 2
        self.arrived = ring_up(last, count)

    def step(self):
        rows, at, side = self.rows, self.at, self.rows // 2

        def total(grads, arrived):
            return (grads[at * rows : (at + 1) * rows].astype(f32) + arrived.astype(f32)).astype(bf16)

        def ends(grads, arrived):
            value = grads[:rows].astype(f32) + arrived.astype(f32)
            return value[:side], value[side:].astype(bf16)

        if at > 0:
            self.arrived = ring_up(self.order(total, self.grads, self.arrived), self.count)
        elif at == 0:
            self.own, other = self.order(ends, self.grads, self.arrived)
            self.arrived = ctx_swap(other)
        else:
            self.result = self.order(lambda own, arrived: own + arrived.astype(f32), self.own, self.arrived)
        self.at = at - 1


def exchanges(count):
    steps = [1 << i for i in range(count.bit_length() - 1)]
    swaps = [lambda value, step=step: lax.ppermute(value, "shard", [(i, i ^ step) for i in range(count)]) for step in steps]
    return [ctx_swap, *swaps]


def place(count, rows, step, side):
    shard, ctx = lax.axis_index("shard"), lax.axis_index("ctx")
    owner = lax.rem(shard + step, count) * 2 + (ctx + side) % 2
    return pl.ds(pl.multiple_of(owner * rows, rows), rows)


def core_columns(width, side):
    half = width // 2
    core = (lax.axis_index("tp") + side) % 2
    return pl.ds(pl.multiple_of(core * half, half), half)


def normalize(values):
    centered = values - jnp.mean(values, axis=-1, keepdims=True)
    inverse = lax.rsqrt(jnp.mean(centered * centered, axis=-1, keepdims=True) + norm_eps)
    return centered * inverse, inverse


def normalize_back(unit, inverse, d_unit):
    mean = jnp.mean(d_unit, axis=-1, keepdims=True)
    along = jnp.mean(d_unit * unit, axis=-1, keepdims=True)
    return inverse * (d_unit - mean - unit * along)


def column_sum(values):
    return jnp.sum(values, axis=0, keepdims=True)


def assemble_kernel(count, rows, *refs):
    own, other, out = refs[:count], refs[count:-1], refs[-1]
    each = count // len(other)
    for step in range(count):
        at = (step % each) * rows
        out[place(count, rows, step, 0), :] = own[step][...]
        out[place(count, rows, step, 1), :] = other[step // each][at : at + rows, :]


def assemble(own, other):
    count = len(own)
    rows, columns = own[0].shape
    shape = (2 * count * rows, columns)
    return call(functools.partial(assemble_kernel, count, rows), [(shape, bf16)], 1.5, "assemble")(*own, *other)[0]


def assemble_pairs_kernel(count, rows, *refs):
    pairs, out = refs[:count], refs[count]
    for step in range(count):
        for side in range(2):
            out[place(count, rows, step, side), :] = pairs[step][side * rows : (side + 1) * rows, :]


def assemble_pairs(pairs):
    count = len(pairs)
    rows, columns = pairs[0].shape[0] // 2, pairs[0].shape[1]
    shape = (2 * count * rows, columns)
    return call(functools.partial(assemble_pairs_kernel, count, rows), [(shape, bf16)], 1.5, "assemble_pairs")(*pairs)[0]


def lines(out, row, values):
    for i in range(values.shape[0]):
        out[row : row + 1, i * 128 : (i + 1) * 128] = values[i : i + 1, :].astype(f32)


def norm1_kernel(x_ref, *refs):
    vectors, vec_ref, out_ref = refs[:9], refs[9], refs[10]

    @pl.when(pl.program_id(0) == 0)
    def _():
        vec_ref[...] = jnp.zeros_like(vec_ref)
        for row, ref in enumerate(vectors[:7]):
            lines(vec_ref, row + (row == 6), ref[...])
        for i, ref in enumerate(vectors[7:]):
            for part in range(WIDTH // 128):
                at = i * WIDTH + part * 128
                vec_ref[6:7, at : at + 128] = ref[part : part + 1, :].astype(f32)

    unit, _ = normalize(x_ref[...].astype(f32))
    out_ref[...] = (unit * vec_ref[1:2, :] + vec_ref[2:3, :]).astype(bf16)


def norm1(x, vectors):
    rows, width = x.shape
    tile = pl.BlockSpec((QTILE, width), lambda i: (i, 0))
    vectors = [vector.reshape(-1, 128) for vector in vectors]
    vec = pl.BlockSpec((8, width), lambda i: (0, 0))
    return pl.pallas_call(
        norm1_kernel,
        grid=(rows // QTILE,),
        out_shape=[jax.ShapeDtypeStruct((8, width), f32), jax.ShapeDtypeStruct((rows, width), bf16)],
        in_specs=[tile, *(pl.BlockSpec(vector.shape, lambda i: (0, 0)) for vector in vectors)],
        out_specs=[vec, tile],
        compiler_params=pltpu.CompilerParams(vmem_limit_bytes=VMEM_LIMIT),
        cost_estimate=cost(3),
        name="norm1",
    )(x, *vectors)


def pack_kernel(qkv_ref, proj_ref, fc2_ref, a_ref, t_ref):
    for i in range(3):
        a_ref[:, i * WIDTH : (i + 1) * WIDTH] = qkv_ref[i]
    a_ref[:, 3 * WIDTH :] = proj_ref[...].T
    t_ref[...] = fc2_ref[...].T


def pack(qkv_weight, proj_weight, fc2_weight):
    rows, hidden = fc2_weight.shape[1], fc2_weight.shape[0]
    if rows % 128:
        columns = [qkv_weight[:, 0], qkv_weight[:, 1], qkv_weight[:, 2], proj_weight.T]
        return jnp.concatenate(columns, axis=1), fc2_weight.T
    outs = [((rows, 4 * WIDTH), bf16), ((rows, hidden), bf16)]
    return call(pack_kernel, outs, 1, "pack")(qkv_weight.transpose(1, 0, 2), proj_weight, fc2_weight)


def qkv_kernel(count, rows, *refs):
    pieces = refs[: 2 * count]
    normed_ref, vec_ref, w_ref, p_ref, q_ref, kv_ref, sems = refs[2 * count :]
    copies = []
    for side in range(2):
        for step in range(count):
            at, index = place(count, rows, step, side), side * count + step
            left = pltpu.make_async_copy(pieces[index].at[:, pl.ds(0, 3 * WIDTH)], w_ref.at[at], sems.at[2 * index])
            right = pltpu.make_async_copy(pieces[index].at[:, pl.ds(3 * WIDTH, WIDTH)], p_ref.at[at], sems.at[2 * index + 1])
            copies += [left, right]
    for copy in copies:
        copy.start()
    for copy in copies:
        copy.wait()
    for start, size in SPLITS:
        at = slice(start, start + size)
        projected = dot_nn(normed_ref[at, :], w_ref[...])
        queries = (projected[:, :WIDTH] + vec_ref[6:7, :WIDTH]).astype(bf16)
        q_ref[at, :] = (queries.astype(f32) * HD ** (-0.5)).astype(bf16)
        kv_ref[at, :WIDTH] = projected[:, WIDTH : 2 * WIDTH].astype(bf16)
        kv_ref[at, WIDTH:] = (projected[:, 2 * WIDTH :] + vec_ref[6:7, WIDTH : 2 * WIDTH]).astype(bf16)


def qkv(count, pieces, normed, vec):
    rows = pieces[0].shape[0]
    tokens, width = normed.shape
    whole = pl.BlockSpec(memory_space=pltpu.VMEM)
    return pl.pallas_call(
        functools.partial(qkv_kernel, count, rows),
        out_shape=[
            jax.ShapeDtypeStruct((width, 3 * WIDTH), bf16),
            jax.ShapeDtypeStruct((width, WIDTH), bf16),
            jax.ShapeDtypeStruct((tokens, WIDTH), bf16),
            jax.ShapeDtypeStruct((tokens, 2 * WIDTH), bf16),
        ],
        in_specs=[pl.BlockSpec(memory_space=pl.ANY)] * (2 * count) + [whole, whole],
        out_specs=[whole] * 4,
        scratch_shapes=[pltpu.SemaphoreType.DMA((4 * count,))],
        compiler_params=pltpu.CompilerParams(vmem_limit_bytes=VMEM_LIMIT),
        cost_estimate=cost(4),
        name="qkv",
    )(*pieces, normed, vec)


def head_mask(shape, head):
    lane = lax.broadcasted_iota(jnp.int32, shape, len(shape) - 1)
    return (lane >= head * HD) & (lane < (head + 1) * HD)


def fwd_near_kernel(start, size, q_ref, kv_ref, o_ref, m_ref, l_ref):
    q = q_ref[start : start + size, :]
    keys, values = kv_ref[:, :WIDTH], kv_ref[:, WIDTH:]
    o = jnp.zeros((size, WIDTH), f32)
    m = jnp.zeros((size, WIDTH), f32)
    total = jnp.zeros((size, WIDTH), f32)
    for head in range(HEADS):
        mask = head_mask((size, WIDTH), head)
        scores = dot_nt(jnp.where(mask, q, jnp.zeros_like(q)), keys)
        top = jnp.max(scores, axis=-1, keepdims=True)
        weights = jnp.exp(scores - top)
        row_sum = jnp.sum(weights, axis=-1, keepdims=True)
        mixed = dot_nn(weights.astype(bf16), values)
        o = jnp.where(mask, mixed, o)
        m = jnp.where(mask, top, m)
        total = jnp.where(mask, row_sum, total)
    o_ref[...] = o
    m_ref[...] = m
    l_ref[...] = total


def fwd_far_kernel(start, size, q_ref, kv_ref, o_ref, m_ref, l_ref, p_ref, mix_ref, lse_ref, keep_ref, send_ref):
    q = q_ref[start : start + size, :]
    keys, values = kv_ref[:, :WIDTH], kv_ref[:, WIDTH:]
    o, m, total = o_ref[...], m_ref[...], l_ref[...]
    o_out = jnp.zeros((size, WIDTH), f32)
    lse = jnp.zeros((size, 128), f32)
    lane = lax.broadcasted_iota(jnp.int32, (size, 128), 1)
    for head in range(HEADS):
        mask = head_mask((size, WIDTH), head)
        scores = dot_nt(jnp.where(mask, q, jnp.zeros_like(q)), keys)
        before = m[:, head * HD : head * HD + 1]
        top = jnp.maximum(jnp.max(scores, axis=-1, keepdims=True), before)
        weights = jnp.exp(scores - top)
        carry = jnp.exp(before - top)
        row_sum = jnp.sum(weights, axis=-1, keepdims=True) + carry * total[:, head * HD : head * HD + 1]
        mixed = dot_nn(weights.astype(bf16), values) + carry * o
        o_out = jnp.where(mask, mixed / row_sum, o_out)
        lse = jnp.where(lane == head, top + jnp.log(row_sum), lse)
    mixture = o_out.astype(bf16)
    mix_ref[...] = mixture
    lse_ref[...] = lse
    width = p_ref.shape[0]
    keep_ref[...] = dot_nt(mixture, p_ref[core_columns(width, 0), :]).astype(bf16)
    send_ref[...] = dot_nt(mixture, p_ref[core_columns(width, 1), :]).astype(bf16)


def attention_near(start, size, q, kv):
    kernel = functools.partial(fwd_near_kernel, start, size)
    return call(kernel, [((size, WIDTH), f32)] * 3, 8 * size / 784, "attention_near")(q, kv)


def attention_far(start, size, q, kv, o, m, total, proj_t):
    half = proj_t.shape[0] // 2
    outs = [((size, WIDTH), bf16), ((size, 128), f32), ((size, half), bf16), ((size, half), bf16)]
    kernel = functools.partial(fwd_far_kernel, start, size)
    return call(kernel, outs, 9 * size / 784, "attention_far")(q, kv, o, m, total, proj_t)


def merge(out, mine, other):
    width = out.shape[1]
    out[:, core_columns(width, 0)] = mine[...].astype(out.dtype)
    out[:, core_columns(width, 1)] = other[...].astype(out.dtype)


def mlp_kernel(
    start, size, mine_ref, other_ref, x_ref, g_ref, vec_ref, w1_ref, w2_ref,
    mid_ref, second_ref, hidden_ref, d_pre_ref, keep_ref, send_ref, bias_sum_ref, g_sum_ref,
):
    at = slice(start, start + size)
    width = x_ref.shape[1]
    merge(mid_ref, mine_ref, other_ref)
    middle = mid_ref[...] + x_ref[at, :].astype(f32) + vec_ref[0:1, :]
    mid_ref[...] = middle
    unit, _ = normalize(middle)
    second = (unit * vec_ref[3:4, :] + vec_ref[4:5, :]).astype(bf16)
    second_ref[...] = second
    grad = g_ref[at, :]
    g_sum_ref[...] = jnp.broadcast_to(column_sum(grad.astype(f32)), g_sum_ref.shape)
    pre = dot_nn(second, w1_ref[...]) + vec_ref[7:8, :]
    upper = 0.5 + 0.5 * lax.erf(pre * (0.5**0.5))
    hidden_ref[...] = (pre * upper).astype(bf16)
    slope = upper + pre * (jnp.exp(-0.5 * pre * pre) * 0.3989422804014327)
    d_pre = (slope * dot_nn(grad, w2_ref[...])).astype(bf16)
    d_pre_ref[...] = d_pre
    bias_sum_ref[...] = jnp.broadcast_to(column_sum(d_pre.astype(f32)), bias_sum_ref.shape)
    keep_ref[...] = dot_nt(d_pre, w1_ref[core_columns(width, 0), :]).astype(bf16)
    send_ref[...] = dot_nt(d_pre, w1_ref[core_columns(width, 1), :]).astype(bf16)


def mlp(start, size, mine, other, x, g, vec, w1, w2):
    width, hidden = w1.shape
    outs = [
        ((size, width), f32),
        ((size, width), bf16),
        ((size, hidden), bf16),
        ((size, hidden), bf16),
        ((size, width // 2), bf16),
        ((size, width // 2), bf16),
        ((8, hidden), f32),
        ((8, width), f32),
    ]
    return call(functools.partial(mlp_kernel, start, size), outs, 14 * size / 784, "mlp")(mine, other, x, g, vec, w1, w2)


def mlp_out_kernel(hidden_a, hidden_b, w2_ref, keep_ref, send_ref):
    width = w2_ref.shape[0]
    for (start, size), hidden in zip(SPLITS, (hidden_a, hidden_b)):
        at = slice(start, start + size)
        keep_ref[at, :] = dot_nt(hidden[...], w2_ref[core_columns(width, 0), :]).astype(bf16)
        send_ref[at, :] = dot_nt(hidden[...], w2_ref[core_columns(width, 1), :]).astype(bf16)


def mlp_out(tokens, hidden_a, hidden_b, w2):
    half = ((tokens, w2.shape[0] // 2), bf16)
    return call(mlp_out_kernel, [half, half], 2, "mlp_out")(hidden_a, hidden_b, w2)


def layer_out_kernel(mine, other, mid_a, mid_b, vec_ref, out_ref, work_ref):
    merge(work_ref, mine, other)
    for (start, size), middle in zip(SPLITS, (mid_a, mid_b)):
        at = slice(start, start + size)
        out_ref[at, :] = (middle[...] + work_ref[at, :] + vec_ref[5:6, :]).astype(bf16)


def spread(count, grads_ref, keep_ref, high_ref, low_ref):
    rows, half = grads_ref.shape[0] // (2 * count), count // 2
    for step in range(count):
        at = slice(step * rows, (step + 1) * rows)
        keep_ref[at, :] = grads_ref[place(count, rows, step, 0), :]
        out, first = (high_ref, half) if step >= half else (low_ref, 0)
        out[(step - first) * rows : (step - first + 1) * rows, :] = grads_ref[place(count, rows, step, 1), :].astype(bf16)


def grad_1_kernel(count, left_a, left_b, right_a, right_b, out_ref, last_ref, grads_ref):
    grads_ref[...] = dot_tn(left_a[...], right_a[...]) + dot_tn(left_b[...], right_b[...])
    rows = grads_ref.shape[0] // (2 * count)
    for step in range(count):
        for side in range(2):
            block = grads_ref[place(count, rows, step, side), :]
            out_ref[(2 * step + side) * rows : (2 * step + side + 1) * rows, :] = block
            if step == count - 1:
                last_ref[side * rows : (side + 1) * rows, :] = block.astype(bf16)


def grad_1(count, width, columns, *arrays):
    scratch = [pltpu.VMEM((width, columns), f32)]
    outs = [((width, columns), f32), ((width // count, columns), bf16)]
    return call(functools.partial(grad_1_kernel, count), outs, 3, "grad_1", scratch)(*arrays)


def grad_2_kernel(count, left, right_a, right_b, keep_ref, high_ref, low_ref, grads_ref):
    (a, size_a), (b, size_b) = SPLITS
    grads_ref[...] = dot_tn(left[a : a + size_a, :], right_a[...]) + dot_tn(left[b : b + size_b, :], right_b[...])
    spread(count, grads_ref, keep_ref, high_ref, low_ref)


def grad_a_kernel(count, normed, d_proj, mid_a, mid_b, mix_a, mix_b, keep_ref, high_ref, low_ref, grads_ref):
    grads_ref[:, : 3 * WIDTH] = dot_tn(normed[...], d_proj[...])
    grads_ref[:, 3 * WIDTH :] = dot_tn(mid_a[...], mix_a[...]) + dot_tn(mid_b[...], mix_b[...])
    spread(count, grads_ref, keep_ref, high_ref, low_ref)


def weight_grad(kernel, count, width, columns, micros, *arrays):
    scratch = [pltpu.VMEM((width, columns), f32)]
    outs = [((width // 2, columns), f32), ((width // 4, columns), bf16), ((width // 4, columns), bf16)]
    return call(functools.partial(kernel, count), outs, micros, kernel.__name__, scratch)(*arrays)


def norm2_back_kernel(
    start, size, mine_ref, other_ref, mid_ref, g_ref, vec_ref, p_ref, mix_ref, lse_ref,
    d_mid_ref, low_ref, d_mix_ref, delta_ref, lse_out_ref, sums_ref,
):
    merge(d_mid_ref, mine_ref, other_ref)
    d_second = d_mid_ref[...]
    unit, inverse = normalize(mid_ref[...])
    sums_ref[...] = jnp.zeros_like(sums_ref)
    sums_ref[0:1, :] = column_sum(d_second * unit)
    sums_ref[1:2, :] = column_sum(d_second)
    d_middle = g_ref[start : start + size, :].astype(f32) + normalize_back(unit, inverse, d_second * vec_ref[3:4, :])
    d_mid_ref[...] = d_middle
    low = d_middle.astype(bf16)
    low_ref[...] = low
    sums_ref[2:3, :] = column_sum(low.astype(f32))
    d_mix = dot_nn(low, p_ref[...]).astype(bf16)
    d_mix_ref[...] = d_mix
    head = lax.broadcasted_iota(jnp.int32, (8, WIDTH), 0)
    lane = lax.broadcasted_iota(jnp.int32, (8, WIDTH), 1)
    pick = (lane // HD == head).astype(f32)
    both = d_mix.astype(f32) * mix_ref[...].astype(f32)
    exact = dict(precision=lax.Precision.HIGHEST, preferred_element_type=f32)
    delta_ref[...] = lax.dot_general(pick, both, (((1,), (1,)), ((), ())), **exact)
    one = (lane == head).astype(f32)[:, :128]
    lse_out_ref[...] = lax.dot_general(one, lse_ref[...], (((1,), (1,)), ((), ())), **exact)


def norm2_back(start, size, mine, other, middle, g, vec, proj_t, mixture, lse):
    width = proj_t.shape[0]
    outs = [
        ((size, width), f32),
        ((size, width), bf16),
        ((size, WIDTH), bf16),
        ((8, size), f32),
        ((8, size), f32),
        ((8, width), f32),
    ]
    kernel = functools.partial(norm2_back_kernel, start, size)
    return call(kernel, outs, 6 * size / 784, "norm2_back")(mine, other, middle, g, vec, proj_t, mixture, lse)


def bwd_kernel(start, size, kv_ref, q_ref, do_ref, lse_ref, delta_ref, dkv_ref, dq_ref):
    at = slice(start, start + size)
    for head in range(HEADS):
        low, high = slice(head * HD, (head + 1) * HD), slice(WIDTH + head * HD, WIDTH + (head + 1) * HD)
        keys, values = kv_ref[at, low], kv_ref[at, high]
        q, d_out = q_ref[:, low], do_ref[:, low]
        probs = jnp.exp(dot_nt(keys, q) - lse_ref[head : head + 1, :])
        d_probs = dot_nt(values, d_out)
        dkv_ref[:, high] = dot_nn(probs.astype(bf16), d_out).astype(dkv_ref.dtype)
        d_scores = (probs * (d_probs - delta_ref[head : head + 1, :])).astype(bf16)
        dkv_ref[:, low] = dot_nn(d_scores, q).astype(dkv_ref.dtype)
        dq_ref[low, :] = dot_tn(keys, d_scores)


def attention_back(start, size, q, kv, d_out, lse, delta, dtype):
    outs = [((size, 2 * WIDTH), dtype), ((WIDTH, q.shape[0]), f32)]
    kernel = functools.partial(bwd_kernel, start, size)
    return call(kernel, outs, 11 * size / 784, "attention_back")(kv, q, d_out, lse, delta)


def qkv_back_kernel(dq_1, dq_2, dq_3, dq_4, here_a, here_b, back_a, back_b, w_ref, d_proj_ref, keep_a, send_a, keep_b, send_b, sums_ref):
    width = w_ref.shape[0]
    d_query = ((dq_1[...] + dq_2[...] + dq_3[...] + dq_4[...]).T * HD ** (-0.5)).astype(bf16)
    d_proj_ref[:, :WIDTH] = d_query
    sums_ref[...] = jnp.zeros_like(sums_ref)
    sums_ref[0:1, :] = column_sum(d_query.astype(f32))
    parts = zip(SPLITS, (here_a, here_b), (back_a, back_b), (keep_a, keep_b), (send_a, send_b))
    value_sum = 0.0
    for (start, size), here, back, keep, send in parts:
        d_kv = (here[...] + back[...].astype(f32)).astype(bf16)
        d_proj_ref[start : start + size, WIDTH:] = d_kv
        value_sum = value_sum + column_sum(d_kv[:, WIDTH:].astype(f32))
        part = d_proj_ref[start : start + size, :]
        keep[...] = dot_nt(part, w_ref[core_columns(width, 0), :]).astype(bf16)
        send[...] = dot_nt(part, w_ref[core_columns(width, 1), :]).astype(bf16)
    sums_ref[1:2, :] = value_sum


def qkv_back(tokens, w, *arrays):
    width = w.shape[0]
    halves = [((size, width // 2), bf16) for _, size in SPLITS for _ in range(2)]
    outs = [((tokens, 3 * WIDTH), bf16), *halves, ((8, WIDTH), f32)]
    return call(qkv_back_kernel, outs, 3, "qkv_back")(*arrays, w)


def norm1_sums_kernel(d_proj_ref, w_ref, x_ref, sums_ref):
    sums_ref[...] = jnp.zeros_like(sums_ref)
    gain, shift = 0.0, 0.0
    for start, size in SPLITS:
        at = slice(start, start + size)
        unit, _ = normalize(x_ref[at, :].astype(f32))
        terms = dot_nt(d_proj_ref[at, :], w_ref[...])
        gain, shift = gain + column_sum(terms * unit), shift + column_sum(terms)
    sums_ref[0:1, :] = gain
    sums_ref[1:2, :] = shift


def norm1_back_kernel(mine_a, other_a, mine_b, other_b, d_mid_a, d_mid_b, x_ref, vec_ref, out_ref, work_ref):
    for (start, size), mine, other, d_mid in zip(SPLITS, (mine_a, mine_b), (other_a, other_b), (d_mid_a, d_mid_b)):
        at = slice(start, start + size)
        work = work_ref.at[pl.ds(0, size)]
        merge(work, mine, other)
        unit, inverse = normalize(x_ref[at, :].astype(f32))
        d_in = normalize_back(unit, inverse, work[...] * vec_ref[1:2, :])
        out_ref[at, :] = (d_mid[...] + d_in).astype(bf16)


def layer(
    count,
    video_tokens,
    qkv_weight,
    q_bias,
    v_bias,
    proj_weight,
    proj_bias,
    norm1_gain,
    norm1_shift,
    norm2_gain,
    norm2_shift,
    fc1_weight,
    fc1_bias,
    fc2_weight,
    fc2_bias,
    out_grad,
):
    x, g = video_tokens[0], out_grad[0]
    tokens, width = x.shape
    hidden = fc1_bias.shape[0]
    order = Order()

    piece, piece_2 = pack(qkv_weight, proj_weight, fc2_weight)
    own_a, other_a = [piece], [ctx_swap(piece)]
    arrived_2 = ctx_swap(piece_2)
    for step in range(1, count):
        before = own_a[-1] if step == 1 else tie(own_a[-1], other_a[step - 2])
        own_a.append(ring_down(before, count))
        other_a.append(ctx_swap(own_a[-1]))
    own_1 = [tie(fc1_weight, own_a[-1])]
    pairs = [tie(jnp.concatenate([piece_2, arrived_2]), own_a[-1])]

    def next_1():
        own_1.append(ring_down(order.wait(own_1[-1]), count))

    def next_2():
        pairs.append(ring_down(order.wait(pairs[-1]), count))

    vec, normed = order(
        lambda x, *vectors: norm1(x, vectors),
        x, proj_bias, norm1_gain, norm1_shift, norm2_gain, norm2_shift, fc2_bias, fc1_bias, q_bias, v_bias,
    )
    next_1()
    next_2()
    for step in range(count // 2 - 1):
        next_1()
    qkv_w, proj_t, queries, kv = order(
        lambda *values: qkv(count, values[: 2 * count], *values[2 * count :]), *own_a, *other_a, normed, vec
    )
    kv_far = ctx_swap(kv)
    partials = [order(functools.partial(attention_near, *SPLITS[0]), queries, kv)]
    for step in range(count // 2 - 1):
        next_2()
    partials.append(order(functools.partial(attention_near, *SPLITS[1]), queries, kv))
    while len(own_1) < count:
        next_1()
    own_1 = order.wait(own_1)
    half = count // 2
    other_1 = [ctx_swap(tie(jnp.concatenate(own_1[:half]), kv_far)), ctx_swap(tie(jnp.concatenate(own_1[half:]), kv_far))]
    attn, mixtures, lses = [], [], []
    for split, partial in zip(SPLITS, partials):
        mixture, lse, keep, send = order(functools.partial(attention_far, *split), queries, kv_far, *partial, proj_t)
        mixtures.append(mixture)
        lses.append(lse)
        attn.append(TpSum(order, keep, send))
        if split == SPLITS[0]:
            next_2()
    attn[0].far()
    attn[1].far()
    while len(pairs) < count:
        next_2()
    attn[0].back()
    w1 = order(lambda *pieces: assemble(pieces[:count], pieces[count:]), *own_1, *other_1)
    w2 = order(lambda *pieces: assemble_pairs(pieces), *pairs)
    attn[1].back()

    middles, seconds, hiddens, d_pres, d_seconds, bias_sums, g_sums = [], [], [], [], [], [], []
    for (start, size), part in zip(SPLITS, attn):
        middle, second, hidden_b, d_pre, keep, send, bias_sum, g_sum = order(
            functools.partial(mlp, start, size), *part.result, x, g, vec, w1, w2
        )
        middles.append(middle)
        seconds.append(second)
        hiddens.append(hidden_b)
        d_pres.append(d_pre)
        bias_sums.append(bias_sum[0])
        g_sums.append(g_sum[0])
        d_seconds.append(TpSum(order, keep, send))
    d_seconds[0].far()
    d_seconds[1].far()
    parts_1 = order(functools.partial(grad_1, count, width, hidden), *seconds, *d_pres)
    grad_fc1 = RingScatter(order, count, *parts_1)
    parts_2 = order(functools.partial(weight_grad, grad_2_kernel, count, width, hidden, 3), g, *hiddens)
    grad_fc2 = SwapScatter(order, count, *parts_2)

    d_mids, lows, d_mixes, deltas, lse_rows, norm2_sums = [], [], [], [], [], []
    for i, (start, size) in enumerate(SPLITS):
        d_seconds[i].back()
    for i, (start, size) in enumerate(SPLITS):
        d_mid, low, d_mix, delta, lse_row, sums = order(
            functools.partial(norm2_back, start, size),
            *d_seconds[i].result, middles[i], g, vec, proj_t, mixtures[i], lses[i],
        )
        d_mids.append(d_mid)
        lows.append(low)
        d_mixes.append(d_mix)
        deltas.append(delta)
        lse_rows.append(lse_row)
        norm2_sums.append(sums)
    norm2_sums = sum(norm2_sums)
    out_sum = TpSum(order, *order(functools.partial(mlp_out, tokens), *hiddens, w2))
    d_mix, delta, lse_row = jnp.concatenate(d_mixes), jnp.concatenate(deltas, axis=1), jnp.concatenate(lse_rows, axis=1)

    def turn(keys, split, dtype):
        return order(
            lambda *values: attention_back(*split, *values, dtype), queries, keys, d_mix, lse_row, delta
        )

    grad_fc1.step()
    away_a = turn(kv_far, SPLITS[0], bf16)
    back_a = ctx_swap(away_a[0])
    out_sum.far()
    grad_fc2.step()
    away_b = turn(kv_far, SPLITS[1], bf16)
    back_b = ctx_swap(away_b[0])
    for _ in range(1, half):
        grad_fc1.step()
    here_a = turn(kv, SPLITS[0], f32)
    for _ in range(1, half):
        grad_fc2.step()
    out_sum.back()
    here_b = turn(kv, SPLITS[1], f32)
    for _ in range(half, count - 1):
        grad_fc1.step()
    for _ in range(half, count - 1):
        grad_fc2.step()

    d_proj, keep_a, send_a, keep_b, send_b, qv_sums = order(
        lambda *values: qkv_back(tokens, values[-1], *values[:-1]),
        away_a[1], away_b[1], here_a[1], here_b[1], here_a[0], here_b[0], back_a, back_b, qkv_w,
    )
    d_normed = [TpSum(order, keep_a, send_a), TpSum(order, keep_b, send_b)]
    parts_a = order(
        functools.partial(weight_grad, grad_a_kernel, count, width, 4 * WIDTH, 4), normed, d_proj, *lows, *mixtures
    )
    grad_a = SwapScatter(order, count, *parts_a)
    d_normed[0].far()
    d_normed[1].far()
    norm1_sums = order(call(norm1_sums_kernel, [((8, width), f32)], 3, "norm1_sums"), d_proj, qkv_w, x)[0]
    norm1_sums = norm1_sums[:2].reshape(-1)
    scratch = [pltpu.VMEM((tokens, width), f32)]
    out_rows = order(
        call(layer_out_kernel, [((tokens, width), bf16)], 2, "layer_out", scratch), *out_sum.result, *middles, vec
    )[0]
    grad_fc1.step()
    grad_fc2.step()
    norm1_sums = order(jnp.add, norm1_sums, core_swap(norm1_sums))
    d_normed[0].back()
    grad_a.step()
    norm1_sums = order(jnp.add, norm1_sums, far_swap(norm1_sums))
    terms = [sum(bias_sums), sum(g_sums), norm2_sums[0], norm2_sums[1], norm2_sums[2], norm1_sums, qv_sums[0], qv_sums[1]]
    sums = jnp.concatenate(terms)
    swaps = exchanges(count)
    d_normed[1].back()
    for _ in range(1, half):
        grad_a.step()
    sums = order(jnp.add, sums, swaps[0](sums))
    scratch = [pltpu.VMEM((max(size for _, size in SPLITS), width), f32)]
    input_grad = order(
        call(norm1_back_kernel, [((tokens, width), bf16)], 4, "norm1_back", scratch),
        *d_normed[0].result, *d_normed[1].result, *d_mids, x, vec,
    )[0]
    for swap in swaps[1:-1]:
        sums = order(jnp.add, sums, swap(sums))
    for _ in range(half, count - 1):
        grad_a.step()
    for swap in swaps[-1:]:
        sums = order(jnp.add, sums, swap(sums))
    grad_a.step()
    grad_qkv = grad_a.result[:, : 3 * WIDTH].reshape(-1, 3, WIDTH)
    grad_proj = grad_a.result[:, 3 * WIDTH :].T
    ends = [hidden, width, width, width, width, width, width, WIDTH, WIDTH]
    ends = [sum(ends[: i + 1]) for i in range(len(ends))]
    g_fc1_bias, g_fc2_bias, g_gain_two, g_shift_two, g_proj_bias, g_gain_one, g_shift_one, g_q_bias, g_v_bias = (
        sums[begin:end] for begin, end in zip([0, *ends], ends)
    )
    return (
        out_rows[None],
        input_grad[None],
        grad_qkv,
        g_q_bias,
        g_v_bias,
        grad_proj,
        g_proj_bias,
        g_gain_one,
        g_shift_one,
        g_gain_two,
        g_shift_two,
        grad_fc1.result,
        g_fc1_bias,
        grad_fc2.result.T,
        g_fc2_bias,
    )


def solution(mesh):
    split = ("shard", "ctx")
    tokens, rows, columns = P("shard", "ctx", None), P(split, "tp"), P("tp", split)
    stack = P(split, None, "tp")
    own, copied = P("tp"), P()
    in_specs = (
        tokens,
        stack,
        own,
        own,
        columns,
        copied,
        copied,
        copied,
        copied,
        copied,
        rows,
        own,
        columns,
        copied,
        tokens,
    )
    out_specs = (
        tokens,
        tokens,
        stack,
        own,
        own,
        columns,
        copied,
        copied,
        copied,
        copied,
        copied,
        rows,
        own,
        columns,
        copied,
    )
    return jax.shard_map(
        functools.partial(layer, mesh.shape["shard"]),
        mesh=mesh,
        in_specs=in_specs,
        out_specs=out_specs,
        check_vma=False,
    )
```

```python
import functools

import jax
import jax.numpy as jnp
from jax import lax
from jax.experimental import pallas as pl
from jax.experimental.pallas import tpu as pltpu
from jax.sharding import PartitionSpec as P

HD = 64
HEADS = 4
WIDTH = HEADS * HD

norm_eps = 1e-06
bf16, f32 = jnp.bfloat16, jnp.float32
VMEM_LIMIT, VMEM_MLP, VMEM_MOST = 24 * 1024 * 1024, 36 * 1024 * 1024, 58 * 1024 * 1024
PARTS = (slice(0, 336), slice(336, 784))

CTX_PAIRS = [(0, 1), (1, 0)]
CORE_PAIRS = [(0, 1), (1, 0), (2, 3), (3, 2)]
FAR_PAIRS = [(0, 2), (2, 0), (1, 3), (3, 1)]


def cost(micros):
    return pl.CostEstimate(flops=int(micros * 1e5), bytes_accessed=1024, transcendentals=0)


class Order:
    def __init__(self):
        self.tokens = []

    def __call__(self, work, *values):
        CHAIN[:] = [self.tokens]
        result = work(*values)
        self.tokens = [CHAIN.pop()]
        return result

    def wait(self, value):
        self.tokens.extend(jax.tree.leaves(value))
        return value


CHAIN = []
WHOLE, PLACED = pl.BlockSpec(memory_space=pltpu.VMEM), pl.BlockSpec(memory_space=pl.ANY)
TOKEN = jax.ShapeDtypeStruct((8, 128), f32)


def launch(kernel, outs, micros, name, in_specs, out_specs, grid=(), scratch=(), limit=VMEM_LIMIT):
    def run(*values):
        tokens = [token for token in CHAIN.pop() if not any(token is value for value in values)]
        first, last = len(values), len(values) + len(tokens)
        end = last + len(outs)

        def ordered(*refs):
            kernel(*refs[:first], *refs[last:end], *refs[end + 1 :])
            refs[end][...] = jnp.zeros_like(refs[end])

        *results, token = pl.pallas_call(
            ordered,
            grid=grid,
            out_shape=[*(jax.ShapeDtypeStruct(shape, dtype) for shape, dtype in outs), TOKEN],
            in_specs=[*in_specs(len(values)), *[WHOLE] * len(tokens)],
            out_specs=[*out_specs, WHOLE],
            scratch_shapes=scratch,
            compiler_params=pltpu.CompilerParams(vmem_limit_bytes=limit),
            cost_estimate=cost(micros),
            name=name,
        )(*values, *tokens)
        CHAIN.append(token)
        return results

    return run


def call(kernel, outs, micros, name, scratch=(), far=(), limit=VMEM_LIMIT):
    def in_specs(count):
        return [PLACED if place in far else WHOLE for place in range(count)]

    return launch(kernel, outs, micros, name, in_specs, [WHOLE] * len(outs), (), scratch, limit)


def fetch(pairs, sems):
    copies = [pltpu.make_async_copy(source, target, sems.at[i]) for i, (source, target) in enumerate(pairs)]
    for copy in copies:
        copy.start()
    return copies


def dot_nn(left, right):
    return jnp.dot(left, right, preferred_element_type=f32)


def dot_tn(left, right):
    return lax.dot_general(left, right, (((0,), (0,)), ((), ())), preferred_element_type=f32)


def dot_nt(left, right):
    return lax.dot_general(left, right, (((1,), (1,)), ((), ())), preferred_element_type=f32)


def tie(value, *before):
    return lax.optimization_barrier((value, *before))[0]


def ctx_swap(value):
    return lax.ppermute(value, "ctx", CTX_PAIRS)


def core_swap(value):
    return lax.ppermute(value, "tp", CORE_PAIRS)


def far_swap(value):
    return lax.ppermute(value, "tp", FAR_PAIRS)


def ring_down(value, count):
    return lax.ppermute(value, "shard", [(i, (i - 1) % count) for i in range(count)])


def ring_up(value, count):
    return lax.ppermute(value, "shard", [(i, (i + 1) % count) for i in range(count)])


def relay(value):
    return call(relay_kernel, [(value.shape, value.dtype)], 1, "relay")(value)[0]


def relay_kernel(value_ref, out_ref):
    out_ref[...] = value_ref[...]


def add_kernel(left, *refs):
    out, at = refs[-1], 0
    for right in refs[:-1]:
        part = slice(at, at + right.shape[1])
        out[:, part] = (left[:, part].astype(f32) + right[...].astype(f32)).astype(out.dtype)
        at += right.shape[1]


def add(left, *rights):
    return call(add_kernel, [(left.shape, left.dtype)], 1, "add")(left, *rights)[0]


def add_apart_kernel(left, *refs):
    rights, outs = refs[: len(refs) // 2], refs[len(refs) // 2 :]
    for i, (right, out) in enumerate(zip(rights, outs)):
        part = slice(i * out.shape[1], (i + 1) * out.shape[1])
        out[...] = (left[:, part].astype(f32) + right[...].astype(f32)).astype(out.dtype)


def add_apart(left, *rights):
    return call(add_apart_kernel, [(right.shape, right.dtype) for right in rights], 1, "add_apart")(left, *rights)


def add_halves_kernel(left, right, *outs):
    for i, out in enumerate(outs):
        part = slice(i * out.shape[1], (i + 1) * out.shape[1])
        out[...] = (left[:, part].astype(f32) + right[:, part].astype(f32)).astype(out.dtype)


def add_halves(left, right):
    half = (left.shape[0], left.shape[1] // 2)
    return call(add_halves_kernel, [(half, left.dtype)] * 2, 1, "add_halves")(left, right)


class TpSum:
    def __init__(self, order, apart, keep, *sends):
        self.order, self.apart, self.keep = order, apart, keep
        self.arrived = [core_swap(send) for send in sends]

    def far(self):
        if self.apart:
            self.near = self.order(add_apart, self.keep, *self.arrived)
        else:
            self.near = [self.order(add, self.keep, *self.arrived)]
        self.arrived = [far_swap(piece) for piece in self.near]

    def back(self):
        if self.apart:
            total = [self.order(add, *pair) for pair in zip(self.near, self.arrived)]
        else:
            total = self.order(add_halves, *self.near, *self.arrived)
        self.result = [*total, *(core_swap(piece) for piece in total)]


class SwapScatter:
    def __init__(self, order, count, keep, sends):
        self.order, self.count, self.keep = order, count, keep
        self.other, self.later = ctx_swap(sends[0]), list(sends[1:])
        self.rows, self.first = keep[0].shape[0], (count // 2 if self.later else 0)
        self.at, self.arrived = count - 1, None

    def step(self, finish=None):
        at = self.at
        if at < self.first:
            self.other, self.first = self.lower, 0
        terms, places = [self.keep[at], self.other], [0, at - self.first]
        if self.arrived is not None:
            terms, places = [*terms, self.arrived], [*places, 0]
        if finish:
            self.result = self.order(finish, *(term[place * self.rows : (place + 1) * self.rows] for term, place in zip(terms, places)))
            return
        extra = self.later.pop() if self.later else None
        value, *copied = self.order(
            lambda *values: block_sum(values, self.rows, places, bf16 if at else f32, extra), *terms
        )
        if copied:
            self.lower = ctx_swap(copied[0])
        if at:
            self.arrived, self.at = ring_up(value, self.count), at - 1
        else:
            self.result = value


class PairScatter:
    def __init__(self, order, count, blocks, keep, sends):
        self.order, self.count, self.blocks, self.keep = order, count, blocks, keep
        self.other, self.rows, self.at = ctx_swap(sends[0]), keep[0].shape[0], count - 2
        self.arrived = ring_up(blocks[-1], count)

    def joint(self):
        at, rows = self.at, self.rows
        value = self.order(
            lambda *values: joint_sum(rows, at + 1, *values), self.blocks[at], self.arrived, self.keep[at + 1], self.other
        )
        self.arrived, self.at = ring_up(value, self.count), at - 1

    def ends(self):
        rows = self.rows
        self.own, other, value = self.order(
            lambda *values: ends_sum(rows, *values), self.blocks[0], self.arrived, self.keep[1], self.other
        )
        self.swapped, self.arrived = ctx_swap(other), ring_up(value, self.count)

    def last_second(self, finish):
        self.second = self.order(finish, self.keep[0], self.other[: self.rows], self.arrived)

    def last_first(self):
        self.first = self.order(lambda *values: block_sum(values, self.rows, [0, 0], f32), self.own, self.swapped)[0]


def joint_sum(rows, at, block, arrived, keep, other):
    def kernel(block_ref, arrived_ref, keep_ref, other_ref, out_ref):
        pair, third = slice(0, 2 * rows), slice(2 * rows, 3 * rows)
        out_ref[pair, :] = (block_ref[...] + arrived_ref[pair, :].astype(f32)).astype(bf16)
        value = keep_ref[...] + other_ref[at * rows : (at + 1) * rows, :].astype(f32)
        if arrived_ref.shape[0] > 2 * rows:
            value = value + arrived_ref[third, :].astype(f32)
        out_ref[third, :] = value.astype(bf16)

    return call(kernel, [((3 * rows, block.shape[1]), bf16)], 1, "joint_sum")(block, arrived, keep, other)[0]


def ends_sum(rows, block, arrived, keep, other):
    def kernel(block_ref, arrived_ref, keep_ref, other_ref, own_ref, away_ref, out_ref):
        own, away, third = slice(0, rows), slice(rows, 2 * rows), slice(2 * rows, 3 * rows)
        own_ref[...] = block_ref[own, :] + arrived_ref[own, :].astype(f32)
        away_ref[...] = (block_ref[away, :] + arrived_ref[away, :].astype(f32)).astype(bf16)
        value = keep_ref[...] + other_ref[away, :].astype(f32) + arrived_ref[third, :].astype(f32)
        out_ref[...] = value.astype(bf16)

    shape = (rows, block.shape[1])
    return call(kernel, [(shape, f32), (shape, bf16), (shape, bf16)], 1, "ends_sum")(block, arrived, keep, other)


def split_sum_kernel(left, right, own_ref, other_ref):
    side = own_ref.shape[0]
    own_ref[...] = left[:side, :].astype(f32) + right[:side, :].astype(f32)
    other_ref[...] = (left[side:, :].astype(f32) + right[side:, :].astype(f32)).astype(bf16)


def split_sum(left, right):
    shape = (left.shape[0] // 2, left.shape[1])
    return call(split_sum_kernel, [(shape, f32), (shape, bf16)], 1, "split_sum")(left, right)


def block_sum(terms, rows, at, dtype, extra=None):
    columns = terms[0].shape[1]

    def kernel(*refs):
        ins, outs = refs[: len(terms)], refs[-1 if extra is None else -2 :]
        outs[0][...] = sum(ref[...].astype(f32) for ref in ins).astype(dtype)
        if extra is not None:
            outs[1][...] = refs[len(terms)][...]

    def spec(place):
        return pl.BlockSpec((rows, columns), lambda i: (place, 0))

    specs, outs, out_specs = [spec(place) for place in at], [((rows, columns), dtype)], [spec(0)]
    values = list(terms)
    if extra is not None:
        whole = pl.BlockSpec(extra.shape, lambda i: (0, 0))
        specs, outs, out_specs = [*specs, whole], [*outs, (extra.shape, extra.dtype)], [*out_specs, whole]
        values.append(extra)
    return launch(kernel, outs, 1, "block_sum", lambda count: specs, out_specs, (1,))(*values)


def finish_a_kernel(one, two, three, qkv_ref, proj_ref):
    total = one[...] + two[...].astype(f32) + three[...].astype(f32)
    for i in range(3):
        qkv_ref[i] = total[:, i * WIDTH : (i + 1) * WIDTH]
    right = total[:, 3 * WIDTH :]
    proj_ref[...] = right.T if proj_ref.shape[0] == WIDTH else right


def finish_a(one, two, three):
    rows = one.shape[0]
    shape = (WIDTH, rows) if rows % 128 == 0 else (rows, WIDTH)
    qkv, proj = call(finish_a_kernel, [((3, rows, WIDTH), f32), (shape, f32)], 1, "finish_a")(one, two, three)
    return qkv.transpose(1, 0, 2), proj if rows % 128 == 0 else proj.T


def finish_2_kernel(one, two, three, out_ref):
    out_ref[...] = (one[...] + two[...].astype(f32) + three[...].astype(f32)).T


def finish_2(one, two, three):
    rows, columns = one.shape
    if rows % 128:
        return block_sum((one, two, three), rows, (0, 0, 0), f32)[0].T
    return call(finish_2_kernel, [((columns, rows), f32)], 1, "finish_2")(one, two, three)[0]


def finish_sums_kernel(left, right, *outs):
    for i, out in enumerate(outs):
        row, first = (i, 0) if i < 7 else (7, (i - 7) * WIDTH)
        for part in range(out.shape[0]):
            at = slice(first + part * 128, first + (part + 1) * 128)
            out[part : part + 1, :] = left[row : row + 1, at] + right[row : row + 1, at]


def finish_sums(left, right):
    lines = left.shape[1] // 128
    outs = [((lines, 128), f32)] * 7 + [((WIDTH // 128, 128), f32)] * 2
    return [out.reshape(-1) for out in call(finish_sums_kernel, outs, 1, "finish_sums")(left, right)]


def exchanges(count):
    steps = [1 << i for i in range(count.bit_length() - 1)]
    swaps = [lambda value, step=step: lax.ppermute(value, "shard", [(i, i ^ step) for i in range(count)]) for step in steps]
    return [ctx_swap, *swaps]


def place(count, rows, step, side):
    shard, ctx = lax.axis_index("shard"), lax.axis_index("ctx")
    owner = lax.rem(shard + step, count) * 2 + (ctx + side) % 2
    return pl.ds(pl.multiple_of(owner * rows, rows), rows)


def core_columns(width, side, piece=None):
    half = width // 2
    core = (lax.axis_index("tp") + side) % 2
    if piece is None:
        return pl.ds(pl.multiple_of(core * half, half), half)
    return pl.ds(pl.multiple_of(core * half + piece * (half // 2), half // 2), half // 2)


def send_terms(at, left, right_ref, keep_ref, sends):
    width = right_ref.shape[0]
    keep_ref[at, :] = dot_nt(left, right_ref[core_columns(width, 0), :]).astype(bf16)
    terms = dot_nt(left, right_ref[core_columns(width, 1), :]).astype(bf16)
    for piece, out in enumerate(sends):
        out[at, :] = terms[:, piece * width // 4 : (piece + 1) * width // 4]


def term_shapes(rows, width):
    return [((rows, width // 2), bf16), ((rows, width // 4), bf16), ((rows, width // 4), bf16)]


def normalize(values):
    centered = values - jnp.mean(values, axis=-1, keepdims=True)
    inverse = lax.rsqrt(jnp.mean(centered * centered, axis=-1, keepdims=True) + norm_eps)
    return centered * inverse, inverse


def normalize_back(unit, inverse, d_unit):
    mean = jnp.mean(d_unit, axis=-1, keepdims=True)
    along = jnp.mean(d_unit * unit, axis=-1, keepdims=True)
    return inverse * (d_unit - mean - unit * along)


def column_sum(values):
    return jnp.sum(values, axis=0, keepdims=True)


def assemble_kernel(count, rows, *refs):
    own, other, out = refs[:count], refs[count:-1], refs[-1]
    each = count // len(other)
    for step in range(count):
        at = (step % each) * rows
        out[place(count, rows, step, 0), :] = own[step][...]
        out[place(count, rows, step, 1), :] = other[step // each][at : at + rows, :]


def assemble(own, other):
    count = len(own)
    rows, columns = own[0].shape
    shape = (2 * count * rows, columns)
    return call(functools.partial(assemble_kernel, count, rows), [(shape, bf16)], 1.5, "assemble")(*own, *other)[0]


def assemble_pairs_kernel(count, rows, *refs):
    pairs, out = refs[:count], refs[count]
    for step in range(count):
        for side in range(2):
            out[place(count, rows, step, side), :] = pairs[step][side * rows : (side + 1) * rows, :]


def assemble_pairs(pairs):
    count = len(pairs)
    rows, columns = pairs[0].shape[0] // 2, pairs[0].shape[1]
    shape = (2 * count * rows, columns)
    return call(functools.partial(assemble_pairs_kernel, count, rows), [(shape, bf16)], 1.5, "assemble_pairs")(*pairs)[0]


def norm1_kernel(x_hbm, *refs):
    sources, vec_ref, out_ref, x_ref, held, sems = refs[:8], *refs[8:]
    copies = fetch([(x_hbm, x_ref), *[(source, held.at[row]) for row, source in enumerate(sources)]], sems)
    for copy in copies[1:]:
        copy.wait()
    for row in range(8):
        for part in range(sources[0].shape[0]):
            vec_ref[row : row + 1, part * 128 : (part + 1) * 128] = held[row, part : part + 1, :].astype(f32)
    copies[0].wait()
    for at in PARTS:
        unit, _ = normalize(x_ref[at, :].astype(f32))
        out_ref[at, :] = (unit * vec_ref[1:2, :] + vec_ref[2:3, :]).astype(bf16)


def norm1(x, vectors):
    rows, width = x.shape
    vectors = [vector.reshape(-1, 128) for vector in vectors]
    outs = [((8, width), f32), ((rows, width), bf16)]
    scratch = [pltpu.VMEM((rows, width), bf16), pltpu.VMEM((8, *vectors[0].shape), bf16), pltpu.SemaphoreType.DMA((9,))]
    return call(norm1_kernel, outs, 3, "norm1", scratch, range(9), VMEM_MOST)(x, *vectors)


def pack_kernel(qkv_hbm, proj_hbm, fc2_hbm, a_ref, t_ref, qkv_ref, proj_ref, fc2_ref, sems):
    copies = fetch([(qkv_hbm, qkv_ref), (proj_hbm, proj_ref), (fc2_hbm, fc2_ref)], sems)
    copies[0].wait()
    for i in range(3):
        a_ref[:, i * WIDTH : (i + 1) * WIDTH] = qkv_ref[i]
    copies[1].wait()
    copies[2].wait()
    turned = proj_ref.shape[0] == WIDTH
    a_ref[:, 3 * WIDTH :] = proj_ref[...].T if turned else proj_ref[...]
    t_ref[...] = fc2_ref[...].T if turned else fc2_ref[...]


def pack(qkv_weight, proj_weight, fc2_weight):
    rows, hidden = fc2_weight.shape[1], fc2_weight.shape[0]
    outs = [((rows, 4 * WIDTH), bf16), ((rows, hidden), bf16)]
    if rows % 128:
        proj_weight, fc2_weight = proj_weight.T, fc2_weight.T
    scratch = [pltpu.VMEM((3, rows, WIDTH), bf16), pltpu.VMEM(proj_weight.shape, bf16), pltpu.VMEM(fc2_weight.shape, bf16)]
    scratch.append(pltpu.SemaphoreType.DMA((3,)))
    return call(pack_kernel, outs, 1, "pack", scratch, (0, 1, 2), VMEM_MOST)(qkv_weight.transpose(1, 0, 2), proj_weight, fc2_weight)


def qkv_kernel(count, rows, *refs):
    pieces = refs[: 2 * count]
    normed_hbm, vec_hbm, w_ref, p_ref, q_ref, k_ref, v_ref, normed_ref, vec_ref, sems = refs[2 * count :]
    pairs = [(normed_hbm, normed_ref), (vec_hbm, vec_ref)]
    for side in range(2):
        for step in range(count):
            at, index = place(count, rows, step, side), side * count + step
            pairs.append((pieces[index].at[:, pl.ds(0, 3 * WIDTH)], w_ref.at[at]))
            pairs.append((pieces[index].at[:, pl.ds(3 * WIDTH, WIDTH)], p_ref.at[at]))
    for copy in fetch(pairs, sems):
        copy.wait()
    for at in PARTS:
        projected = dot_nn(normed_ref[at, :], w_ref[...])
        queries = (projected[:, :WIDTH] + vec_ref[6:7, :WIDTH]).astype(bf16)
        q_ref[at, :] = (queries.astype(f32) * HD ** (-0.5)).astype(bf16)
        k_ref[at, :] = projected[:, WIDTH : 2 * WIDTH].astype(bf16)
        v_ref[at, :] = (projected[:, 2 * WIDTH :] + vec_ref[6:7, WIDTH : 2 * WIDTH]).astype(bf16)


def qkv(count, pieces, normed, vec):
    rows = pieces[0].shape[0]
    tokens, width = normed.shape
    outs = [((width, 3 * WIDTH), bf16), ((width, WIDTH), bf16), *[((tokens, WIDTH), bf16)] * 3]
    scratch = [pltpu.VMEM(normed.shape, bf16), pltpu.VMEM(vec.shape, f32), pltpu.SemaphoreType.DMA((4 * count + 2,))]
    kernel = functools.partial(qkv_kernel, count, rows)
    return call(kernel, outs, 4, "qkv", scratch, range(2 * count + 2))(*pieces, normed, vec)


def head_mask(shape, head):
    lane = lax.broadcasted_iota(jnp.int32, shape, len(shape) - 1)
    return (lane >= head * HD) & (lane < (head + 1) * HD)


def fwd_near_kernel(q_ref, k_ref, v_ref, o_ref, m_ref, l_ref):
    keys, values = k_ref[...], v_ref[...]
    for at in PARTS:
        q = q_ref[at, :]
        o, m, total = (jnp.zeros(q.shape, f32) for _ in range(3))
        for head in range(HEADS):
            mask = head_mask(q.shape, head)
            scores = dot_nt(jnp.where(mask, q, jnp.zeros_like(q)), keys)
            top = jnp.max(scores, axis=-1, keepdims=True)
            weights = jnp.exp(scores - top)
            row_sum = jnp.sum(weights, axis=-1, keepdims=True)
            mixed = dot_nn(weights.astype(bf16), values)
            o = jnp.where(mask, mixed, o)
            m = jnp.where(mask, top, m)
            total = jnp.where(mask, row_sum, total)
        o_ref[at, :] = o
        m_ref[at, :] = m
        l_ref[at, :] = total


def fwd_far_kernel(q_ref, k_ref, v_ref, o_ref, m_ref, l_ref, p_ref, mix_ref, lse_ref, keep_ref, *sends):
    keys, values = k_ref[...], v_ref[...]
    for at in PARTS:
        q = q_ref[at, :]
        o, m, total = o_ref[at, :], m_ref[at, :], l_ref[at, :]
        o_out = jnp.zeros(q.shape, f32)
        lse = jnp.zeros((q.shape[0], 128), f32)
        lane = lax.broadcasted_iota(jnp.int32, lse.shape, 1)
        for head in range(HEADS):
            mask = head_mask(q.shape, head)
            scores = dot_nt(jnp.where(mask, q, jnp.zeros_like(q)), keys)
            before = m[:, head * HD : head * HD + 1]
            top = jnp.maximum(jnp.max(scores, axis=-1, keepdims=True), before)
            weights = jnp.exp(scores - top)
            carry = jnp.exp(before - top)
            row_sum = jnp.sum(weights, axis=-1, keepdims=True) + carry * total[:, head * HD : head * HD + 1]
            mixed = dot_nn(weights.astype(bf16), values) + carry * o
            o_out = jnp.where(mask, mixed / row_sum, o_out)
            lse = jnp.where(lane == head, top + jnp.log(row_sum), lse)
        mixture = o_out.astype(bf16)
        mix_ref[at, :] = mixture
        lse_ref[at, :] = lse
        send_terms(at, mixture, p_ref, keep_ref, sends)


def attention_near(q, k, v):
    return call(fwd_near_kernel, [(q.shape, f32)] * 3, 6, "attention_near")(q, k, v)


def attention_far(q, k, v, o, m, total, proj_t):
    rows = q.shape[0]
    outs = [(q.shape, bf16), ((rows, 128), f32), *term_shapes(rows, proj_t.shape[0])]
    return call(fwd_far_kernel, outs, 8, "attention_far")(q, k, v, o, m, total, proj_t)


def merge(out, refs):
    width = out.shape[1]
    for i, ref in enumerate(refs):
        out[:, core_columns(width, i // 2, i % 2)] = ref[...].astype(out.dtype)


def mlp_kernel(
    sum_1, sum_2, sum_3, sum_4, x_ref, g_ref, vec_ref, w1_ref, w2_ref,
    mid_ref, second_ref, hidden_ref, d_pre_ref, sums_ref, keep_ref, send_1, send_2, x_held, g_held, sems,
):
    pairs = [pair for at in PARTS for pair in ((x_ref.at[at], x_held.at[at]), (g_ref.at[at], g_held.at[at]))]
    copies = fetch(pairs, sems)
    merge(mid_ref, (sum_1, sum_2, sum_3, sum_4))
    sums_ref[...] = jnp.zeros_like(sums_ref)
    for i, at in enumerate(PARTS):
        copies[2 * i].wait()
        middle = mid_ref[at, :] + x_held[at, :].astype(f32) + vec_ref[0:1, :]
        mid_ref[at, :] = middle
        unit, _ = normalize(middle)
        second = (unit * vec_ref[3:4, :] + vec_ref[4:5, :]).astype(bf16)
        second_ref[at, :] = second
        copies[2 * i + 1].wait()
        grad = g_held[at, :]
        sums_ref[1:2, :] += column_sum(grad.astype(f32))
        pre = dot_nn(second, w1_ref[...]) + vec_ref[7:8, :]
        upper = 0.5 + 0.5 * lax.erf(pre * (0.5**0.5))
        hidden_ref[at, :] = (pre * upper).astype(bf16)
        slope = upper + pre * (jnp.exp(-0.5 * pre * pre) * 0.3989422804014327)
        d_pre = (slope * dot_nn(grad, w2_ref[...])).astype(bf16)
        d_pre_ref[at, :] = d_pre
        sums_ref[0:1, :] += column_sum(d_pre.astype(f32))
        send_terms(at, d_pre, w1_ref, keep_ref, (send_1, send_2))


def mlp(sums, x, g, vec, w1, w2):
    (rows, width), hidden = x.shape, w1.shape[1]
    outs = [(x.shape, f32), (x.shape, bf16), ((rows, hidden), bf16), ((rows, hidden), bf16), ((8, width), f32)]
    outs += term_shapes(rows, width)
    scratch = [pltpu.VMEM(x.shape, bf16), pltpu.VMEM(x.shape, bf16), pltpu.SemaphoreType.DMA((4,))]
    return call(mlp_kernel, outs, 8, "mlp", scratch, (4, 5), VMEM_MLP)(*sums, x, g, vec, w1, w2)


def mlp_out_kernel(hidden_ref, w2_ref, keep_ref, *sends):
    for at in PARTS:
        send_terms(at, hidden_ref[at, :], w2_ref, keep_ref, sends)


def mlp_out(hidden, w2):
    return call(mlp_out_kernel, term_shapes(hidden.shape[0], w2.shape[0]), 2, "mlp_out")(hidden, w2)


def layer_out_kernel(sum_1, sum_2, sum_3, sum_4, mid_ref, vec_ref, out_ref, work_ref):
    merge(work_ref, (sum_1, sum_2, sum_3, sum_4))
    for at in PARTS:
        out_ref[at, :] = (mid_ref[at, :] + work_ref[at, :] + vec_ref[5:6, :]).astype(bf16)


def layer_out(sums, middle, vec):
    scratch = [pltpu.VMEM(middle.shape, f32)]
    return call(layer_out_kernel, [(middle.shape, bf16)], 2, "layer_out", scratch)(*sums, middle, vec)[0]


def spread(count, grads_ref, *outs):
    rows, sends = grads_ref.shape[0] // (2 * count), outs[count:]
    each = count // len(sends)
    for step in range(count):
        outs[step][...] = grads_ref[place(count, rows, step, 0), :]
        out, at = sends[len(sends) - 1 - step // each], (step % each) * rows
        out[at : at + rows, :] = grads_ref[place(count, rows, step, 1), :].astype(bf16)


def grad_1_kernel(count, left, right, *refs):
    outs, grads_ref = refs[:-1], refs[-1]
    grads_ref[...] = dot_tn(left[...], right[...])
    rows = grads_ref.shape[0] // (2 * count)
    for step, out in enumerate(outs):
        for side in range(2):
            out[side * rows : (side + 1) * rows, :] = grads_ref[place(count, rows, step, side), :].astype(out.dtype)


def grad_1(count, left, right):
    width, columns = left.shape[1], right.shape[1]
    scratch, shape = [pltpu.VMEM((width, columns), f32)], (width // count, columns)
    outs = [*[(shape, f32)] * (count - 1), (shape, bf16)]
    return call(functools.partial(grad_1_kernel, count), outs, 3, "grad_1", scratch)(left, right)


def grad_2_kernel(count, left, right, *refs):
    outs, grads_ref = refs[:-1], refs[-1]
    grads_ref[...] = dot_tn(left[...], right[...])
    spread(count, grads_ref, *outs)


def grad_a_kernel(count, normed, d_proj, low, mixture, *refs):
    outs, grads_ref = refs[:-1], refs[-1]
    grads_ref[:, : 3 * WIDTH] = dot_tn(normed[...], d_proj[...])
    grads_ref[:, 3 * WIDTH :] = dot_tn(low[...], mixture[...])
    spread(count, grads_ref, *outs)


def weight_grad(kernel, count, width, columns, micros, sends, *arrays):
    scratch = [pltpu.VMEM((width, columns), f32)]
    keep, send = ((width // 2 // count, columns), f32), ((width // 2 // sends, columns), bf16)
    results = call(functools.partial(kernel, count), [keep] * count + [send] * sends, micros, kernel.__name__, scratch)(*arrays)
    return results[:count], results[count:]


def norm2_back_kernel(
    sum_1, sum_2, sum_3, sum_4, mid_ref, g_ref, vec_ref, p_ref, mix_ref, lse_ref,
    low_ref, d_mix_ref, delta_ref, lse_out_ref, sums_ref, work_ref, both_ref,
):
    merge(work_ref, (sum_1, sum_2, sum_3, sum_4))
    sums_ref[...] = jnp.zeros_like(sums_ref)
    for at in PARTS:
        d_second = work_ref[at, :]
        unit, inverse = normalize(mid_ref[at, :])
        sums_ref[2:3, :] += column_sum(d_second * unit)
        sums_ref[3:4, :] += column_sum(d_second)
        d_middle = g_ref[at, :].astype(f32) + normalize_back(unit, inverse, d_second * vec_ref[3:4, :])
        low = d_middle.astype(bf16)
        low_ref[at, :] = low
        sums_ref[4:5, :] += column_sum(low.astype(f32))
        d_mix = dot_nn(low, p_ref[...]).astype(bf16)
        d_mix_ref[at, :] = d_mix
        both_ref[at, :] = d_mix.astype(f32) * mix_ref[at, :].astype(f32)
    head = lax.broadcasted_iota(jnp.int32, (8, WIDTH), 0)
    lane = lax.broadcasted_iota(jnp.int32, (8, WIDTH), 1)
    pick = (lane // HD == head).astype(f32)
    exact = dict(precision=lax.Precision.HIGHEST, preferred_element_type=f32)
    delta_ref[...] = lax.dot_general(pick, both_ref[...], (((1,), (1,)), ((), ())), **exact)
    one = (lane == head).astype(f32)[:, :128]
    lse_out_ref[...] = lax.dot_general(one, lse_ref[...], (((1,), (1,)), ((), ())), **exact)


def norm2_back(sums, middle, g, vec, proj_t, mixture, lse):
    rows, width = middle.shape
    outs = [((rows, width), bf16), ((rows, WIDTH), bf16), ((8, rows), f32), ((8, rows), f32), ((8, width), f32)]
    scratch = [pltpu.VMEM((rows, width), f32), pltpu.VMEM((rows, WIDTH), f32)]
    return call(norm2_back_kernel, outs, 6, "norm2_back", scratch)(*sums, middle, g, vec, proj_t, mixture, lse)


def bwd_kernel(q_ref, k_ref, v_ref, do_ref, lse_ref, delta_ref, dk_ref, dv_ref, dq_ref):
    for head in range(HEADS):
        at = slice(head * HD, (head + 1) * HD)
        keys, values, q, d_out = k_ref[:, at], v_ref[:, at], q_ref[:, at], do_ref[:, at]
        probs = jnp.exp(dot_nt(keys, q) - lse_ref[head : head + 1, :])
        d_probs = dot_nt(values, d_out)
        dv_ref[:, at] = dot_nn(probs.astype(bf16), d_out).astype(dv_ref.dtype)
        d_scores = (probs * (d_probs - delta_ref[head : head + 1, :])).astype(bf16)
        dk_ref[:, at] = dot_nn(d_scores, q).astype(dk_ref.dtype)
        dq_ref[at, :] = dot_tn(keys, d_scores)


def attention_back(q, k, v, d_out, lse, delta, dtype):
    outs = [(k.shape, dtype), (v.shape, dtype), ((WIDTH, q.shape[0]), f32)]
    return call(bwd_kernel, outs, 11, "attention_back")(q, k, v, d_out, lse, delta)


def qkv_back_kernel(away_ref, here_ref, dk_ref, dv_ref, dk_back, dv_back, w_ref, d_proj_ref, sums_ref, keep_ref, *sends):
    d_query = ((away_ref[...] + here_ref[...]).T * HD ** (-0.5)).astype(bf16)
    d_value = (dv_ref[...] + dv_back[...].astype(f32)).astype(bf16)
    d_proj_ref[:, :WIDTH] = d_query
    d_proj_ref[:, WIDTH : 2 * WIDTH] = (dk_ref[...] + dk_back[...].astype(f32)).astype(bf16)
    d_proj_ref[:, 2 * WIDTH :] = d_value
    for at in PARTS:
        send_terms(at, d_proj_ref[at, :], w_ref, keep_ref, sends)
    sums_ref[...] = jnp.zeros_like(sums_ref)
    sums_ref[7:8, :WIDTH] = column_sum(d_query.astype(f32))
    sums_ref[7:8, WIDTH : 2 * WIDTH] = column_sum(d_value.astype(f32))


def qkv_back(away, here, dk, dv, dk_back, dv_back, w):
    rows, width = dk.shape[0], w.shape[0]
    outs = [((rows, 3 * WIDTH), bf16), ((8, width), f32), *term_shapes(rows, width)]
    return call(qkv_back_kernel, outs, 3, "qkv_back")(away, here, dk, dv, dk_back, dv_back, w)


def norm1_back_kernel(
    sum_1, sum_2, sum_3, sum_4, low_ref, x_ref, vec_ref, sums_1, sums_2, sums_3, out_ref, sums_ref, work_ref, low_held, x_held, sems
):
    pairs = [pair for at in PARTS for pair in ((x_ref.at[at], x_held.at[at]), (low_ref.at[at], low_held.at[at]))]
    copies = fetch(pairs, sems)
    merge(work_ref, (sum_1, sum_2, sum_3, sum_4))
    sums_ref[...] = sums_1[...] + sums_2[...] + sums_3[...]
    for i, at in enumerate(PARTS):
        copies[2 * i].wait()
        unit, inverse = normalize(x_held[at, :].astype(f32))
        d_normed = work_ref[at, :]
        d_in = normalize_back(unit, inverse, d_normed * vec_ref[1:2, :])
        sums_ref[5:6, :] += column_sum(d_normed * unit)
        sums_ref[6:7, :] += column_sum(d_normed)
        copies[2 * i + 1].wait()
        out_ref[at, :] = (low_held[at, :].astype(f32) + d_in).astype(bf16)


def norm1_back(total, low, x, vec, *sums):
    scratch = [pltpu.VMEM(x.shape, f32), pltpu.VMEM(x.shape, bf16), pltpu.VMEM(x.shape, bf16)]
    outs, scratch = [(x.shape, bf16), (vec.shape, f32)], [*scratch, pltpu.SemaphoreType.DMA((4,))]
    return call(norm1_back_kernel, outs, 4, "norm1_back", scratch, (4, 5))(*total, low, x, vec, *sums)


def join_kernel(*refs):
    at = 0
    for ref in refs[:-1]:
        refs[-1][at : at + ref.shape[0], :] = ref[...]
        at += ref.shape[0]


def join(*pieces):
    rows = sum(piece.shape[0] for piece in pieces)
    return call(join_kernel, [((rows, pieces[0].shape[1]), bf16)], 1, "join")(*pieces)[0]


def layer(
    count,
    video_tokens,
    qkv_weight,
    q_bias,
    v_bias,
    proj_weight,
    proj_bias,
    norm1_gain,
    norm1_shift,
    norm2_gain,
    norm2_shift,
    fc1_weight,
    fc1_bias,
    fc2_weight,
    fc2_bias,
    out_grad,
):
    x, g = video_tokens[0], out_grad[0]
    tokens, width = x.shape
    hidden = fc1_bias.shape[0]
    order = Order()

    piece, piece_2 = order(pack, qkv_weight, proj_weight, fc2_weight)
    own_a, other_a = [piece], [ctx_swap(piece)]
    arrived_2 = ctx_swap(piece_2)
    qv_bias = jnp.concatenate([q_bias, v_bias, jnp.zeros((width - 2 * WIDTH,), bf16)])
    vec, normed = order(
        lambda x, *vectors: norm1(x, vectors),
        x, proj_bias, norm1_gain, norm1_shift, norm2_gain, norm2_shift, fc2_bias, qv_bias, fc1_bias,
    )
    pairs = []
    for step in range(1, count):
        before = own_a[-1]
        if step == 2:
            before = tie(before, other_a[0], normed)
        elif step > 2:
            before = tie(before, other_a[step - 2])
        if step == count - 1:
            pairs.append(order(join, piece_2, arrived_2))
            before = tie(before, pairs[0])
        own_a.append(ring_down(before, count))
        other_a.append(ctx_swap(own_a[-1]))
    half = count // 2

    own_1 = [tie(fc1_weight, own_a[-1], other_a[-2])]
    own_1.append(ring_down(own_1[-1], count))

    def next_1(until):
        while len(own_1) < until:
            own_1.append(ring_down(own_1[-1], count))

    def next_2(until):
        while len(pairs) < until:
            pairs.append(ring_down(pairs[-1], count))

    next_1(half)
    qkv_w, proj_t, queries, keys, values = order(
        lambda *values: qkv(count, values[: 2 * count], *values[2 * count :]), *own_a, *other_a, normed, vec
    )
    keys_far, values_far = ctx_swap(keys), ctx_swap(values)
    next_1(half + 1)
    next_2(half)
    partial = order(attention_near, queries, keys, values)
    own_1[-1] = order(relay, own_1[-1])
    next_1(count)
    pairs[-1] = order(relay, pairs[-1])
    next_2(half + 1)
    order.wait([keys_far, values_far])
    other_1 = [ctx_swap(order(join, *own_1[:half]))]
    order.wait(own_1[-1])
    mixture, lse, *terms = order(attention_far, queries, keys_far, values_far, *partial, proj_t)
    attn = TpSum(order, False, *terms)
    attn.far()
    order.wait(other_1[0])
    other_1.append(ctx_swap(order(join, *own_1[half:])))
    pairs[-1] = order(relay, pairs[-1])
    next_2(count)
    w1 = order(lambda *pieces: assemble(pieces[:count], pieces[count:]), *own_1, *other_1)
    w2 = order(lambda *pieces: assemble_pairs(pieces), *pairs)
    attn.back()

    middle, second, hidden_b, d_pre, sums_1, *terms = order(lambda *values: mlp(values[:4], *values[4:]), *attn.result, x, g, vec, w1, w2)
    d_second = TpSum(order, False, *terms)
    d_second.far()
    out_sum = TpSum(order, False, *order(mlp_out, hidden_b, w2))
    blocks_2 = order(functools.partial(weight_grad, grad_2_kernel, count, width, hidden, 3, 1), g, hidden_b)
    blocks_1 = order(functools.partial(grad_1, count), second, d_pre)
    grads = PairScatter(order, count, blocks_1, *blocks_2)
    order.wait(grads.arrived)
    d_second.back()
    out_sum.far()
    low, d_mix, delta, lse_row, sums_2 = order(
        lambda *values: norm2_back(values[:4], *values[4:]), *d_second.result, middle, g, vec, proj_t, mixture, lse
    )

    grads.joint()
    *away, d_q_away = order(
        lambda *values: attention_back(*values, bf16), queries, keys_far, values_far, d_mix, lse_row, delta
    )
    away = [ctx_swap(part) for part in away]
    *here, d_q_here = order(lambda *values: attention_back(*values, f32), queries, keys, values, d_mix, lse_row, delta)
    for _ in range(1, count - 2):
        grads.joint()
    order.wait(out_sum.arrived)
    d_proj, sums_3, *terms = order(qkv_back, d_q_away, d_q_here, *here, *away, qkv_w)
    d_normed = TpSum(order, True, *terms)
    blocks_a = order(
        functools.partial(weight_grad, grad_a_kernel, count, width, 4 * WIDTH, 4, 2), normed, d_proj, low, mixture
    )
    grad_a = SwapScatter(order, count, *blocks_a)
    d_normed.far()
    order.wait(grads.arrived)
    grad_a.step()
    order.wait(grad_a.arrived)
    d_normed.back()
    for _ in range(1, half):
        grad_a.step()
    grads.ends()
    order.wait(grad_a.lower)
    input_grad, sums = order(
        lambda *values: norm1_back(values[:4], *values[4:]), *d_normed.result, low, x, vec, sums_1, sums_2, sums_3
    )
    out_sum.back()
    swaps = exchanges(count)
    sums = order(add, sums, swaps[0](sums))
    for _ in range(half, count - 1):
        grad_a.step()
    out_rows = order(lambda *values: layer_out(values[:4], *values[4:]), *out_sum.result, middle, vec)
    for swap in swaps[1:-1]:
        order.wait(grad_a.arrived)
        sums = order(add, sums, swap(sums))
    grad_a.step(finish_a)
    grads.last_second(finish_2)
    grads.last_first()
    grad_qkv, grad_proj = grad_a.result
    sums = order(finish_sums, sums, swaps[-1](sums))
    g_fc1_bias, g_fc2_bias, g_gain_two, g_shift_two, g_proj_bias, g_gain_one, g_shift_one, g_q_bias, g_v_bias = sums
    return (
        out_rows[None],
        input_grad[None],
        grad_qkv,
        g_q_bias,
        g_v_bias,
        grad_proj,
        g_proj_bias,
        g_gain_one,
        g_shift_one,
        g_gain_two,
        g_shift_two,
        grads.first,
        g_fc1_bias,
        grads.second,
        g_fc2_bias,
    )


def solution(mesh):
    split = ("shard", "ctx")
    tokens, rows, columns = P("shard", "ctx", None), P(split, "tp"), P("tp", split)
    stack = P(split, None, "tp")
    own, copied = P("tp"), P()
    in_specs = (
        tokens,
        stack,
        own,
        own,
        columns,
        copied,
        copied,
        copied,
        copied,
        copied,
        rows,
        own,
        columns,
        copied,
        tokens,
    )
    out_specs = (
        tokens,
        tokens,
        stack,
        own,
        own,
        columns,
        copied,
        copied,
        copied,
        copied,
        copied,
        rows,
        own,
        columns,
        copied,
    )
    return jax.shard_map(
        functools.partial(layer, mesh.shape["shard"]),
        mesh=mesh,
        in_specs=in_specs,
        out_specs=out_specs,
        check_vma=False,
    )
```

```python
import functools

import jax
import jax.numpy as jnp
from jax import lax
from jax.experimental import pallas as pl
from jax.experimental.pallas import tpu as pltpu
from jax.sharding import PartitionSpec as P

HD = 64
HEADS = 4
WIDTH = HEADS * HD

norm_eps = 1e-06
bf16, f32 = jnp.bfloat16, jnp.float32
VMEM_LIMIT, VMEM_MLP, VMEM_MOST = 24 * 1024 * 1024, 36 * 1024 * 1024, 58 * 1024 * 1024
PARTS = (slice(0, 336), slice(336, 784))

CTX_PAIRS = [(0, 1), (1, 0)]
CORE_PAIRS = [(0, 1), (1, 0), (2, 3), (3, 2)]
FAR_PAIRS = [(0, 2), (2, 0), (1, 3), (3, 1)]


def cost(micros):
    return pl.CostEstimate(flops=int(micros * 1e5), bytes_accessed=1024, transcendentals=0)


class Order:
    def __init__(self):
        self.tokens = []

    def __call__(self, work, *values):
        CHAIN[:] = [self.tokens]
        result = work(*values)
        self.tokens = [CHAIN.pop()]
        return result

    def wait(self, value):
        self.tokens.extend(jax.tree.leaves(value))
        return value


CHAIN = []
WHOLE, PLACED = pl.BlockSpec(memory_space=pltpu.VMEM), pl.BlockSpec(memory_space=pl.ANY)
TOKEN = jax.ShapeDtypeStruct((8, 128), f32)


def launch(kernel, outs, micros, name, in_specs, out_specs, grid=(), scratch=(), limit=VMEM_LIMIT):
    def run(*values):
        tokens = [token for token in CHAIN.pop() if not any(token is value for value in values)]
        first, last = len(values), len(values) + len(tokens)
        end = last + len(outs)

        def ordered(*refs):
            kernel(*refs[:first], *refs[last:end], *refs[end + 1 :])
            refs[end][...] = jnp.zeros_like(refs[end])

        *results, token = pl.pallas_call(
            ordered,
            grid=grid,
            out_shape=[*(jax.ShapeDtypeStruct(shape, dtype) for shape, dtype in outs), TOKEN],
            in_specs=[*in_specs(len(values)), *[WHOLE] * len(tokens)],
            out_specs=[*out_specs, WHOLE],
            scratch_shapes=scratch,
            compiler_params=pltpu.CompilerParams(vmem_limit_bytes=limit),
            cost_estimate=cost(micros),
            name=name,
        )(*values, *tokens)
        CHAIN.append(token)
        return results

    return run


def call(kernel, outs, micros, name, scratch=(), far=(), limit=VMEM_LIMIT):
    def in_specs(count):
        return [PLACED if place in far else WHOLE for place in range(count)]

    return launch(kernel, outs, micros, name, in_specs, [WHOLE] * len(outs), (), scratch, limit)


def fetch(pairs, sems):
    copies = [pltpu.make_async_copy(source, target, sems.at[i]) for i, (source, target) in enumerate(pairs)]
    for copy in copies:
        copy.start()
    return copies


def dot_nn(left, right):
    return jnp.dot(left, right, preferred_element_type=f32)


def dot_tn(left, right):
    return lax.dot_general(left, right, (((0,), (0,)), ((), ())), preferred_element_type=f32)


def dot_nt(left, right):
    return lax.dot_general(left, right, (((1,), (1,)), ((), ())), preferred_element_type=f32)


def tie(value, *before):
    return lax.optimization_barrier((value, *before))[0]


def ctx_swap(value):
    return lax.ppermute(value, "ctx", CTX_PAIRS)


def core_swap(value):
    return lax.ppermute(value, "tp", CORE_PAIRS)


def far_swap(value):
    return lax.ppermute(value, "tp", FAR_PAIRS)


def ring_down(value, count):
    return lax.ppermute(value, "shard", [(i, (i - 1) % count) for i in range(count)])


def ring_up(value, count):
    return lax.ppermute(value, "shard", [(i, (i + 1) % count) for i in range(count)])


def relay(value):
    return call(relay_kernel, [(value.shape, value.dtype)], 1, "relay")(value)[0]


def relay_kernel(value_ref, out_ref):
    out_ref[...] = value_ref[...]


def add_kernel(left, *refs):
    out, at = refs[-1], 0
    for right in refs[:-1]:
        part = slice(at, at + right.shape[1])
        out[:, part] = (left[:, part].astype(f32) + right[...].astype(f32)).astype(out.dtype)
        at += right.shape[1]


def add(left, *rights):
    return call(add_kernel, [(left.shape, left.dtype)], 1, "add")(left, *rights)[0]


def add_apart_kernel(left, *refs):
    rights, outs = refs[: len(refs) // 2], refs[len(refs) // 2 :]
    for i, (right, out) in enumerate(zip(rights, outs)):
        part = slice(i * out.shape[1], (i + 1) * out.shape[1])
        out[...] = (left[:, part].astype(f32) + right[...].astype(f32)).astype(out.dtype)


def add_apart(left, *rights):
    return call(add_apart_kernel, [(right.shape, right.dtype) for right in rights], 1, "add_apart")(left, *rights)


def add_halves_kernel(left, right, *outs):
    for i, out in enumerate(outs):
        part = slice(i * out.shape[1], (i + 1) * out.shape[1])
        out[...] = (left[:, part].astype(f32) + right[:, part].astype(f32)).astype(out.dtype)


def add_halves(left, right):
    half = (left.shape[0], left.shape[1] // 2)
    return call(add_halves_kernel, [(half, left.dtype)] * 2, 1, "add_halves")(left, right)


class TpSum:
    def __init__(self, order, apart, keep, *sends):
        self.order, self.apart, self.keep = order, apart, keep
        self.arrived = [core_swap(send) for send in sends]

    def far(self):
        if self.apart:
            self.near = self.order(add_apart, self.keep, *self.arrived)
        else:
            self.near = [self.order(add, self.keep, *self.arrived)]
        self.arrived = [far_swap(piece) for piece in self.near]

    def back(self):
        if self.apart:
            total = [self.order(add, *pair) for pair in zip(self.near, self.arrived)]
        else:
            total = self.order(add_halves, *self.near, *self.arrived)
        self.result = [*total, *(core_swap(piece) for piece in total)]


class SwapScatter:
    def __init__(self, order, count, keep, sends):
        self.order, self.count, self.keep = order, count, keep
        self.other, self.later = ctx_swap(sends[0]), list(sends[1:])
        self.rows, self.first = keep[0].shape[0], (count // 2 if self.later else 0)
        self.at, self.arrived = count - 1, None

    def step(self, finish=None):
        at = self.at
        if at < self.first:
            self.other, self.first = self.lower, 0
        terms, places = [self.keep[at], self.other], [0, at - self.first]
        if self.arrived is not None:
            terms, places = [*terms, self.arrived], [*places, 0]
        if finish:
            self.result = self.order(finish, *(term[place * self.rows : (place + 1) * self.rows] for term, place in zip(terms, places)))
            return
        extra = self.later.pop() if self.later else None
        value, *copied = self.order(
            lambda *values: block_sum(values, self.rows, places, bf16 if at else f32, extra), *terms
        )
        if copied:
            self.lower = ctx_swap(copied[0])
        if at:
            self.arrived, self.at = ring_up(value, self.count), at - 1
        else:
            self.result = value


class PairScatter:
    def __init__(self, order, count, blocks, keep, sends):
        self.order, self.count, self.blocks, self.keep = order, count, blocks, keep
        self.other, self.rows, self.at = ctx_swap(sends[0]), keep[0].shape[0], count - 2
        self.arrived = ring_up(blocks[-1], count)

    def joint(self):
        at, rows = self.at, self.rows
        value = self.order(
            lambda *values: joint_sum(rows, at + 1, *values), self.blocks[at], self.arrived, self.keep[at + 1], self.other
        )
        self.arrived, self.at = ring_up(value, self.count), at - 1

    def ends(self):
        rows = self.rows
        self.own, other, value = self.order(
            lambda *values: ends_sum(rows, *values), self.blocks[0], self.arrived, self.keep[1], self.other
        )
        self.swapped, self.arrived = ctx_swap(other), ring_up(value, self.count)

    def last_second(self, finish):
        self.second = self.order(finish, self.keep[0], self.other[: self.rows], self.arrived)

    def last_first(self):
        self.first = self.order(lambda *values: block_sum(values, self.rows, [0, 0], f32), self.own, self.swapped)[0]


def joint_sum(rows, at, block, arrived, keep, other):
    def kernel(block_ref, arrived_ref, keep_ref, other_ref, out_ref):
        pair, third = slice(0, 2 * rows), slice(2 * rows, 3 * rows)
        out_ref[pair, :] = (block_ref[...] + arrived_ref[pair, :].astype(f32)).astype(bf16)
        value = keep_ref[...] + other_ref[at * rows : (at + 1) * rows, :].astype(f32)
        if arrived_ref.shape[0] > 2 * rows:
            value = value + arrived_ref[third, :].astype(f32)
        out_ref[third, :] = value.astype(bf16)

    return call(kernel, [((3 * rows, block.shape[1]), bf16)], 1, "joint_sum")(block, arrived, keep, other)[0]


def ends_sum(rows, block, arrived, keep, other):
    def kernel(block_ref, arrived_ref, keep_ref, other_ref, own_ref, away_ref, out_ref):
        own, away, third = slice(0, rows), slice(rows, 2 * rows), slice(2 * rows, 3 * rows)
        own_ref[...] = block_ref[own, :] + arrived_ref[own, :].astype(f32)
        away_ref[...] = (block_ref[away, :] + arrived_ref[away, :].astype(f32)).astype(bf16)
        value = keep_ref[...] + other_ref[away, :].astype(f32) + arrived_ref[third, :].astype(f32)
        out_ref[...] = value.astype(bf16)

    shape = (rows, block.shape[1])
    return call(kernel, [(shape, f32), (shape, bf16), (shape, bf16)], 1, "ends_sum")(block, arrived, keep, other)


def split_sum_kernel(left, right, own_ref, other_ref):
    side = own_ref.shape[0]
    own_ref[...] = left[:side, :].astype(f32) + right[:side, :].astype(f32)
    other_ref[...] = (left[side:, :].astype(f32) + right[side:, :].astype(f32)).astype(bf16)


def split_sum(left, right):
    shape = (left.shape[0] // 2, left.shape[1])
    return call(split_sum_kernel, [(shape, f32), (shape, bf16)], 1, "split_sum")(left, right)


def block_sum(terms, rows, at, dtype, extra=None):
    columns = terms[0].shape[1]

    def kernel(*refs):
        ins, outs = refs[: len(terms)], refs[-1 if extra is None else -2 :]
        outs[0][...] = sum(ref[...].astype(f32) for ref in ins).astype(dtype)
        if extra is not None:
            outs[1][...] = refs[len(terms)][...]

    def spec(place):
        return pl.BlockSpec((rows, columns), lambda i: (place, 0))

    specs, outs, out_specs = [spec(place) for place in at], [((rows, columns), dtype)], [spec(0)]
    values = list(terms)
    if extra is not None:
        whole = pl.BlockSpec(extra.shape, lambda i: (0, 0))
        specs, outs, out_specs = [*specs, whole], [*outs, (extra.shape, extra.dtype)], [*out_specs, whole]
        values.append(extra)
    return launch(kernel, outs, 1, "block_sum", lambda count: specs, out_specs, (1,))(*values)


def finish_a_kernel(one, two, three, qkv_ref, proj_ref):
    total = one[...] + two[...].astype(f32) + three[...].astype(f32)
    for i in range(3):
        qkv_ref[i] = total[:, i * WIDTH : (i + 1) * WIDTH]
    right = total[:, 3 * WIDTH :]
    proj_ref[...] = right.T if proj_ref.shape[0] == WIDTH else right


def finish_a(one, two, three):
    rows = one.shape[0]
    shape = (WIDTH, rows) if rows % 128 == 0 else (rows, WIDTH)
    qkv, proj = call(finish_a_kernel, [((3, rows, WIDTH), f32), (shape, f32)], 1, "finish_a")(one, two, three)
    return qkv.transpose(1, 0, 2), proj if rows % 128 == 0 else proj.T


def finish_2_kernel(one, two, three, out_ref):
    out_ref[...] = (one[...] + two[...].astype(f32) + three[...].astype(f32)).T


def finish_2(one, two, three):
    rows, columns = one.shape
    if rows % 128:
        return block_sum((one, two, three), rows, (0, 0, 0), f32)[0].T
    return call(finish_2_kernel, [((columns, rows), f32)], 1, "finish_2")(one, two, three)[0]


def finish_sums_kernel(left, right, *outs):
    for i, out in enumerate(outs):
        row, first = (i, 0) if i < 7 else (7, (i - 7) * WIDTH)
        for part in range(out.shape[0]):
            at = slice(first + part * 128, first + (part + 1) * 128)
            out[part : part + 1, :] = left[row : row + 1, at] + right[row : row + 1, at]


def finish_sums(left, right):
    lines = left.shape[1] // 128
    outs = [((lines, 128), f32)] * 7 + [((WIDTH // 128, 128), f32)] * 2
    return [out.reshape(-1) for out in call(finish_sums_kernel, outs, 1, "finish_sums")(left, right)]


def exchanges(count):
    steps = [1 << i for i in range(count.bit_length() - 1)]
    swaps = [lambda value, step=step: lax.ppermute(value, "shard", [(i, i ^ step) for i in range(count)]) for step in steps]
    return [ctx_swap, *swaps]


def place(count, rows, step, side):
    shard, ctx = lax.axis_index("shard"), lax.axis_index("ctx")
    owner = lax.rem(shard + step, count) * 2 + (ctx + side) % 2
    return pl.ds(pl.multiple_of(owner * rows, rows), rows)


def core_columns(width, side, piece=None):
    half = width // 2
    core = (lax.axis_index("tp") + side) % 2
    if piece is None:
        return pl.ds(pl.multiple_of(core * half, half), half)
    return pl.ds(pl.multiple_of(core * half + piece * (half // 2), half // 2), half // 2)


def send_terms(at, left, right_ref, keep_ref, sends):
    width = right_ref.shape[0]
    keep_ref[at, :] = dot_nt(left, right_ref[core_columns(width, 0), :]).astype(bf16)
    terms = dot_nt(left, right_ref[core_columns(width, 1), :]).astype(bf16)
    for piece, out in enumerate(sends):
        out[at, :] = terms[:, piece * width // 4 : (piece + 1) * width // 4]


def term_shapes(rows, width):
    return [((rows, width // 2), bf16), ((rows, width // 4), bf16), ((rows, width // 4), bf16)]


def normalize(values):
    centered = values - jnp.mean(values, axis=-1, keepdims=True)
    inverse = lax.rsqrt(jnp.mean(centered * centered, axis=-1, keepdims=True) + norm_eps)
    return centered * inverse, inverse


def normalize_back(unit, inverse, d_unit):
    mean = jnp.mean(d_unit, axis=-1, keepdims=True)
    along = jnp.mean(d_unit * unit, axis=-1, keepdims=True)
    return inverse * (d_unit - mean - unit * along)


def column_sum(values):
    return jnp.sum(values, axis=0, keepdims=True)


def assemble_kernel(count, rows, *refs):
    own, other, out = refs[:count], refs[count:-1], refs[-1]
    where = [(part, at) for part in other for at in range(0, part.shape[0], rows)]
    for step, (part, at) in enumerate(where):
        out[place(count, rows, step, 0), :] = own[step][...]
        out[place(count, rows, step, 1), :] = part[at : at + rows, :]


def assemble(own, other):
    count = len(own)
    rows, columns = own[0].shape
    shape = (2 * count * rows, columns)
    return call(functools.partial(assemble_kernel, count, rows), [(shape, bf16)], 1.5, "assemble")(*own, *other)[0]


def assemble_pairs_kernel(count, rows, *refs):
    pairs, out = refs[:count], refs[count]
    for step in range(count):
        for side in range(2):
            out[place(count, rows, step, side), :] = pairs[step][side * rows : (side + 1) * rows, :]


def assemble_pairs(pairs):
    count = len(pairs)
    rows, columns = pairs[0].shape[0] // 2, pairs[0].shape[1]
    shape = (2 * count * rows, columns)
    return call(functools.partial(assemble_pairs_kernel, count, rows), [(shape, bf16)], 1.5, "assemble_pairs")(*pairs)[0]


def norm1_kernel(x_hbm, *refs):
    sources, vec_ref, out_ref, x_ref, held, sems = refs[:8], *refs[8:]
    copies = fetch([(x_hbm, x_ref), *[(source, held.at[row]) for row, source in enumerate(sources)]], sems)
    for copy in copies[1:]:
        copy.wait()
    for row in range(8):
        for part in range(sources[0].shape[0]):
            vec_ref[row : row + 1, part * 128 : (part + 1) * 128] = held[row, part : part + 1, :].astype(f32)
    copies[0].wait()
    for at in PARTS:
        unit, _ = normalize(x_ref[at, :].astype(f32))
        out_ref[at, :] = (unit * vec_ref[1:2, :] + vec_ref[2:3, :]).astype(bf16)


def norm1(x, vectors):
    rows, width = x.shape
    vectors = [vector.reshape(-1, 128) for vector in vectors]
    outs = [((8, width), f32), ((rows, width), bf16)]
    scratch = [pltpu.VMEM((rows, width), bf16), pltpu.VMEM((8, *vectors[0].shape), bf16), pltpu.SemaphoreType.DMA((9,))]
    return call(norm1_kernel, outs, 3, "norm1", scratch, range(9), VMEM_MOST)(x, *vectors)


def pack_kernel(qkv_hbm, proj_hbm, fc2_hbm, a_ref, t_ref, qkv_ref, proj_ref, fc2_ref, sems):
    copies = fetch([(qkv_hbm, qkv_ref), (proj_hbm, proj_ref), (fc2_hbm, fc2_ref)], sems)
    copies[0].wait()
    for i in range(3):
        a_ref[:, i * WIDTH : (i + 1) * WIDTH] = qkv_ref[i]
    copies[1].wait()
    copies[2].wait()
    turned = proj_ref.shape[0] == WIDTH
    a_ref[:, 3 * WIDTH :] = proj_ref[...].T if turned else proj_ref[...]
    t_ref[...] = fc2_ref[...].T if turned else fc2_ref[...]


def pack(qkv_weight, proj_weight, fc2_weight):
    rows, hidden = fc2_weight.shape[1], fc2_weight.shape[0]
    outs = [((rows, 4 * WIDTH), bf16), ((rows, hidden), bf16)]
    if rows % 128:
        proj_weight, fc2_weight = proj_weight.T, fc2_weight.T
    scratch = [pltpu.VMEM((3, rows, WIDTH), bf16), pltpu.VMEM(proj_weight.shape, bf16), pltpu.VMEM(fc2_weight.shape, bf16)]
    scratch.append(pltpu.SemaphoreType.DMA((3,)))
    return call(pack_kernel, outs, 1, "pack", scratch, (0, 1, 2), VMEM_MOST)(qkv_weight.transpose(1, 0, 2), proj_weight, fc2_weight)


def qkv_kernel(count, rows, *refs):
    pieces = refs[: 2 * count]
    normed_hbm, vec_hbm, w_ref, p_ref, q_ref, k_ref, v_ref, normed_ref, vec_ref, sems = refs[2 * count :]
    pairs = [(normed_hbm, normed_ref), (vec_hbm, vec_ref)]
    for side in range(2):
        for step in range(count):
            at, index = place(count, rows, step, side), side * count + step
            pairs.append((pieces[index].at[:, pl.ds(0, 3 * WIDTH)], w_ref.at[at]))
            pairs.append((pieces[index].at[:, pl.ds(3 * WIDTH, WIDTH)], p_ref.at[at]))
    for copy in fetch(pairs, sems):
        copy.wait()
    for at in PARTS:
        projected = dot_nn(normed_ref[at, :], w_ref[...])
        queries = (projected[:, :WIDTH] + vec_ref[6:7, :WIDTH]).astype(bf16)
        q_ref[at, :] = (queries.astype(f32) * HD ** (-0.5)).astype(bf16)
        k_ref[at, :] = projected[:, WIDTH : 2 * WIDTH].astype(bf16)
        v_ref[at, :] = (projected[:, 2 * WIDTH :] + vec_ref[6:7, WIDTH : 2 * WIDTH]).astype(bf16)


def qkv(count, pieces, normed, vec):
    rows = pieces[0].shape[0]
    tokens, width = normed.shape
    outs = [((width, 3 * WIDTH), bf16), ((width, WIDTH), bf16), *[((tokens, WIDTH), bf16)] * 3]
    scratch = [pltpu.VMEM(normed.shape, bf16), pltpu.VMEM(vec.shape, f32), pltpu.SemaphoreType.DMA((4 * count + 2,))]
    kernel = functools.partial(qkv_kernel, count, rows)
    return call(kernel, outs, 4, "qkv", scratch, range(2 * count + 2))(*pieces, normed, vec)


def head_mask(shape, head):
    lane = lax.broadcasted_iota(jnp.int32, shape, len(shape) - 1)
    return (lane >= head * HD) & (lane < (head + 1) * HD)


def fwd_near_kernel(q_ref, k_ref, v_ref, o_ref, m_ref, l_ref):
    keys, values = k_ref[...], v_ref[...]
    for at in PARTS:
        q = q_ref[at, :]
        o, m, total = (jnp.zeros(q.shape, f32) for _ in range(3))
        for head in range(HEADS):
            mask = head_mask(q.shape, head)
            scores = dot_nt(jnp.where(mask, q, jnp.zeros_like(q)), keys)
            top = jnp.max(scores, axis=-1, keepdims=True)
            weights = jnp.exp(scores - top)
            row_sum = jnp.sum(weights, axis=-1, keepdims=True)
            mixed = dot_nn(weights.astype(bf16), values)
            o = jnp.where(mask, mixed, o)
            m = jnp.where(mask, top, m)
            total = jnp.where(mask, row_sum, total)
        o_ref[at, :] = o
        m_ref[at, :] = m
        l_ref[at, :] = total


def fwd_far_kernel(q_ref, k_ref, v_ref, o_ref, m_ref, l_ref, p_ref, mix_ref, lse_ref, keep_ref, *sends):
    keys, values = k_ref[...], v_ref[...]
    for at in PARTS:
        q = q_ref[at, :]
        o, m, total = o_ref[at, :], m_ref[at, :], l_ref[at, :]
        o_out = jnp.zeros(q.shape, f32)
        lse = jnp.zeros((q.shape[0], 128), f32)
        lane = lax.broadcasted_iota(jnp.int32, lse.shape, 1)
        for head in range(HEADS):
            mask = head_mask(q.shape, head)
            scores = dot_nt(jnp.where(mask, q, jnp.zeros_like(q)), keys)
            before = m[:, head * HD : head * HD + 1]
            top = jnp.maximum(jnp.max(scores, axis=-1, keepdims=True), before)
            weights = jnp.exp(scores - top)
            carry = jnp.exp(before - top)
            row_sum = jnp.sum(weights, axis=-1, keepdims=True) + carry * total[:, head * HD : head * HD + 1]
            mixed = dot_nn(weights.astype(bf16), values) + carry * o
            o_out = jnp.where(mask, mixed / row_sum, o_out)
            lse = jnp.where(lane == head, top + jnp.log(row_sum), lse)
        mixture = o_out.astype(bf16)
        mix_ref[at, :] = mixture
        lse_ref[at, :] = lse
        send_terms(at, mixture, p_ref, keep_ref, sends)


def attention_near(q, k, v):
    return call(fwd_near_kernel, [(q.shape, f32)] * 3, 6, "attention_near")(q, k, v)


def attention_far(q, k, v, o, m, total, proj_t):
    rows = q.shape[0]
    outs = [(q.shape, bf16), ((rows, 128), f32), *term_shapes(rows, proj_t.shape[0])]
    return call(fwd_far_kernel, outs, 8, "attention_far")(q, k, v, o, m, total, proj_t)


def merge(out, refs):
    width = out.shape[1]
    for i, ref in enumerate(refs):
        out[:, core_columns(width, i // 2, i % 2)] = ref[...].astype(out.dtype)


def mlp_kernel(
    sum_1, sum_2, sum_3, sum_4, x_ref, g_ref, vec_ref, w1_ref, w2_ref,
    mid_ref, second_ref, hidden_ref, d_pre_ref, sums_ref, keep_ref, send_1, send_2, x_held, g_held, sems,
):
    pairs = [pair for at in PARTS for pair in ((x_ref.at[at], x_held.at[at]), (g_ref.at[at], g_held.at[at]))]
    copies = fetch(pairs, sems)
    merge(mid_ref, (sum_1, sum_2, sum_3, sum_4))
    sums_ref[...] = jnp.zeros_like(sums_ref)
    for i, at in enumerate(PARTS):
        copies[2 * i].wait()
        middle = mid_ref[at, :] + x_held[at, :].astype(f32) + vec_ref[0:1, :]
        mid_ref[at, :] = middle
        unit, _ = normalize(middle)
        second = (unit * vec_ref[3:4, :] + vec_ref[4:5, :]).astype(bf16)
        second_ref[at, :] = second
        copies[2 * i + 1].wait()
        grad = g_held[at, :]
        sums_ref[1:2, :] += column_sum(grad.astype(f32))
        pre = dot_nn(second, w1_ref[...]) + vec_ref[7:8, :]
        upper = 0.5 + 0.5 * lax.erf(pre * (0.5**0.5))
        hidden_ref[at, :] = (pre * upper).astype(bf16)
        slope = upper + pre * (jnp.exp(-0.5 * pre * pre) * 0.3989422804014327)
        d_pre = (slope * dot_nn(grad, w2_ref[...])).astype(bf16)
        d_pre_ref[at, :] = d_pre
        sums_ref[0:1, :] += column_sum(d_pre.astype(f32))
        send_terms(at, d_pre, w1_ref, keep_ref, (send_1, send_2))


def mlp(sums, x, g, vec, w1, w2):
    (rows, width), hidden = x.shape, w1.shape[1]
    outs = [(x.shape, f32), (x.shape, bf16), ((rows, hidden), bf16), ((rows, hidden), bf16), ((8, width), f32)]
    outs += term_shapes(rows, width)
    scratch = [pltpu.VMEM(x.shape, bf16), pltpu.VMEM(x.shape, bf16), pltpu.SemaphoreType.DMA((4,))]
    return call(mlp_kernel, outs, 8, "mlp", scratch, (4, 5), VMEM_MLP)(*sums, x, g, vec, w1, w2)


def mlp_out_kernel(hidden_ref, w2_ref, keep_ref, *sends):
    for at in PARTS:
        send_terms(at, hidden_ref[at, :], w2_ref, keep_ref, sends)


def mlp_out(hidden, w2):
    return call(mlp_out_kernel, term_shapes(hidden.shape[0], w2.shape[0]), 2, "mlp_out")(hidden, w2)


def layer_out_kernel(sum_1, sum_2, sum_3, sum_4, mid_ref, vec_ref, out_ref, work_ref):
    merge(work_ref, (sum_1, sum_2, sum_3, sum_4))
    for at in PARTS:
        out_ref[at, :] = (mid_ref[at, :] + work_ref[at, :] + vec_ref[5:6, :]).astype(bf16)


def layer_out(sums, middle, vec):
    scratch = [pltpu.VMEM(middle.shape, f32)]
    return call(layer_out_kernel, [(middle.shape, bf16)], 2, "layer_out", scratch)(*sums, middle, vec)[0]


def spread(count, grads_ref, *outs):
    rows, sends = grads_ref.shape[0] // (2 * count), outs[count:]
    each = count // len(sends)
    for step in range(count):
        outs[step][...] = grads_ref[place(count, rows, step, 0), :]
        out, at = sends[len(sends) - 1 - step // each], (step % each) * rows
        out[at : at + rows, :] = grads_ref[place(count, rows, step, 1), :].astype(bf16)


def grad_1_kernel(count, left, right, *refs):
    outs, grads_ref = refs[:-1], refs[-1]
    grads_ref[...] = dot_tn(left[...], right[...])
    rows = grads_ref.shape[0] // (2 * count)
    for step, out in enumerate(outs):
        for side in range(2):
            out[side * rows : (side + 1) * rows, :] = grads_ref[place(count, rows, step, side), :].astype(out.dtype)


def grad_1(count, left, right):
    width, columns = left.shape[1], right.shape[1]
    scratch, shape = [pltpu.VMEM((width, columns), f32)], (width // count, columns)
    outs = [*[(shape, f32)] * (count - 1), (shape, bf16)]
    return call(functools.partial(grad_1_kernel, count), outs, 3, "grad_1", scratch)(left, right)


def grad_2_kernel(count, left, right, *refs):
    outs, grads_ref = refs[:-1], refs[-1]
    grads_ref[...] = dot_tn(left[...], right[...])
    spread(count, grads_ref, *outs)


def grad_a_kernel(count, normed, d_proj, low, mixture, *refs):
    outs, grads_ref = refs[:-1], refs[-1]
    grads_ref[:, : 3 * WIDTH] = dot_tn(normed[...], d_proj[...])
    grads_ref[:, 3 * WIDTH :] = dot_tn(low[...], mixture[...])
    spread(count, grads_ref, *outs)


def weight_grad(kernel, count, width, columns, micros, sends, *arrays):
    scratch = [pltpu.VMEM((width, columns), f32)]
    keep, send = ((width // 2 // count, columns), f32), ((width // 2 // sends, columns), bf16)
    results = call(functools.partial(kernel, count), [keep] * count + [send] * sends, micros, kernel.__name__, scratch)(*arrays)
    return results[:count], results[count:]


def norm2_back_kernel(
    sum_1, sum_2, sum_3, sum_4, mid_ref, g_ref, vec_ref, p_ref, mix_ref, lse_ref,
    low_ref, d_mix_ref, delta_ref, lse_out_ref, sums_ref, work_ref, both_ref,
):
    merge(work_ref, (sum_1, sum_2, sum_3, sum_4))
    sums_ref[...] = jnp.zeros_like(sums_ref)
    for at in PARTS:
        d_second = work_ref[at, :]
        unit, inverse = normalize(mid_ref[at, :])
        sums_ref[2:3, :] += column_sum(d_second * unit)
        sums_ref[3:4, :] += column_sum(d_second)
        d_middle = g_ref[at, :].astype(f32) + normalize_back(unit, inverse, d_second * vec_ref[3:4, :])
        low = d_middle.astype(bf16)
        low_ref[at, :] = low
        sums_ref[4:5, :] += column_sum(low.astype(f32))
        d_mix = dot_nn(low, p_ref[...]).astype(bf16)
        d_mix_ref[at, :] = d_mix
        both_ref[at, :] = d_mix.astype(f32) * mix_ref[at, :].astype(f32)
    head = lax.broadcasted_iota(jnp.int32, (8, WIDTH), 0)
    lane = lax.broadcasted_iota(jnp.int32, (8, WIDTH), 1)
    pick = (lane // HD == head).astype(f32)
    exact = dict(precision=lax.Precision.HIGHEST, preferred_element_type=f32)
    delta_ref[...] = lax.dot_general(pick, both_ref[...], (((1,), (1,)), ((), ())), **exact)
    one = (lane == head).astype(f32)[:, :128]
    lse_out_ref[...] = lax.dot_general(one, lse_ref[...], (((1,), (1,)), ((), ())), **exact)


def norm2_back(sums, middle, g, vec, proj_t, mixture, lse):
    rows, width = middle.shape
    outs = [((rows, width), bf16), ((rows, WIDTH), bf16), ((8, rows), f32), ((8, rows), f32), ((8, width), f32)]
    scratch = [pltpu.VMEM((rows, width), f32), pltpu.VMEM((rows, WIDTH), f32)]
    return call(norm2_back_kernel, outs, 6, "norm2_back", scratch)(*sums, middle, g, vec, proj_t, mixture, lse)


def bwd_kernel(heads, q_ref, k_ref, v_ref, do_ref, lse_ref, delta_ref, dkv_ref, dq_ref):
    rows, count = k_ref.shape[0], len(heads)
    for place, head in enumerate(heads):
        at = slice(head * HD, (head + 1) * HD)
        low, high = (slice(i * HD, (i + 1) * HD) for i in (place, count + place))
        keys, values, q, d_out = k_ref[:, at], v_ref[:, at], q_ref[:, at], do_ref[:, at]
        probs = jnp.exp(dot_nt(keys, q) - lse_ref[head : head + 1, :])
        d_probs = dot_nt(values, d_out)
        dkv_ref[:rows, high] = dot_nn(probs.astype(bf16), d_out).astype(dkv_ref.dtype)
        d_scores = (probs * (d_probs - delta_ref[head : head + 1, :])).astype(bf16)
        dkv_ref[:rows, low] = dot_nn(d_scores, q).astype(dkv_ref.dtype)
        dq_ref[low, :] = dot_tn(keys, d_scores)
    if dkv_ref.shape[0] > rows:
        dkv_ref[rows:, :] = jnp.zeros((dkv_ref.shape[0] - rows, dkv_ref.shape[1]), dkv_ref.dtype)


def attention_back(heads, dtype, more, q, k, v, d_out, lse, delta):
    rows = k.shape[0] + more
    outs = [((rows, 2 * len(heads) * HD), dtype), ((len(heads) * HD, q.shape[0]), f32)]
    kernel = functools.partial(bwd_kernel, heads)
    return call(kernel, outs, 3 * len(heads), "attention_back")(q, k, v, d_out, lse, delta)


def qkv_back_kernel(
    dq_one, dq_two, dq_here, dkv_here, back_one, back_two, w_ref, d_proj_ref, sums_ref, keep_ref, *sends
):
    rows, half = dkv_here.shape[0], WIDTH // 2
    sums_ref[...] = jnp.zeros_like(sums_ref)
    for place, (away, back) in enumerate(((dq_one, back_one), (dq_two, back_two))):
        at = slice(place * half, (place + 1) * half)
        d_query = ((away[...] + dq_here[at, :]).T * HD ** (-0.5)).astype(bf16)
        d_proj_ref[:, at] = d_query
        sums_ref[7:8, at] = column_sum(d_query.astype(f32))
        for part in range(2):
            here = slice(part * WIDTH + place * half, part * WIDTH + (place + 1) * half)
            there = slice(part * half, (part + 1) * half)
            value = (dkv_here[:, here] + back[:rows, there].astype(f32)).astype(bf16)
            out = slice(WIDTH + part * WIDTH + place * half, WIDTH + part * WIDTH + (place + 1) * half)
            d_proj_ref[:, out] = value
            if part:
                sums_ref[7:8, here] = column_sum(value.astype(f32))
    for at in PARTS:
        send_terms(at, d_proj_ref[at, :], w_ref, keep_ref, sends)


def qkv_back(dq_one, dq_two, dq_here, dkv_here, back_one, back_two, w):
    rows, width = dkv_here.shape[0], w.shape[0]
    outs = [((rows, 3 * WIDTH), bf16), ((8, width), f32), *term_shapes(rows, width)]
    return call(qkv_back_kernel, outs, 3, "qkv_back")(dq_one, dq_two, dq_here, dkv_here, back_one, back_two, w)


def norm1_back_kernel(
    sum_1, sum_2, sum_3, sum_4, low_ref, x_ref, vec_ref, sums_1, sums_2, sums_3, out_ref, sums_ref, work_ref, low_held, x_held, sems
):
    pairs = [pair for at in PARTS for pair in ((x_ref.at[at], x_held.at[at]), (low_ref.at[at], low_held.at[at]))]
    copies = fetch(pairs, sems)
    merge(work_ref, (sum_1, sum_2, sum_3, sum_4))
    sums_ref[...] = sums_1[...] + sums_2[...] + sums_3[...]
    for i, at in enumerate(PARTS):
        copies[2 * i].wait()
        unit, inverse = normalize(x_held[at, :].astype(f32))
        d_normed = work_ref[at, :]
        d_in = normalize_back(unit, inverse, d_normed * vec_ref[1:2, :])
        sums_ref[5:6, :] += column_sum(d_normed * unit)
        sums_ref[6:7, :] += column_sum(d_normed)
        copies[2 * i + 1].wait()
        out_ref[at, :] = (low_held[at, :].astype(f32) + d_in).astype(bf16)


def norm1_back(total, low, x, vec, *sums):
    scratch = [pltpu.VMEM(x.shape, f32), pltpu.VMEM(x.shape, bf16), pltpu.VMEM(x.shape, bf16)]
    outs, scratch = [(x.shape, bf16), (vec.shape, f32)], [*scratch, pltpu.SemaphoreType.DMA((4,))]
    return call(norm1_back_kernel, outs, 4, "norm1_back", scratch, (4, 5))(*total, low, x, vec, *sums)


def join_kernel(*refs):
    at = 0
    for ref in refs[:-1]:
        refs[-1][at : at + ref.shape[0], :] = ref[...]
        at += ref.shape[0]


def join(*pieces):
    rows = sum(piece.shape[0] for piece in pieces)
    return call(join_kernel, [((rows, pieces[0].shape[1]), bf16)], 1, "join")(*pieces)[0]


def layer(
    count,
    video_tokens,
    qkv_weight,
    q_bias,
    v_bias,
    proj_weight,
    proj_bias,
    norm1_gain,
    norm1_shift,
    norm2_gain,
    norm2_shift,
    fc1_weight,
    fc1_bias,
    fc2_weight,
    fc2_bias,
    out_grad,
):
    x, g = video_tokens[0], out_grad[0]
    tokens, width = x.shape
    hidden = fc1_bias.shape[0]
    order = Order()

    piece, piece_2 = order(pack, qkv_weight, proj_weight, fc2_weight)
    own_a, other_a = [piece], [ctx_swap(piece)]
    arrived_2 = ctx_swap(piece_2)
    qv_bias = jnp.concatenate([q_bias, v_bias, jnp.zeros((width - 2 * WIDTH,), bf16)])
    vec, normed = order(
        lambda x, *vectors: norm1(x, vectors),
        x, proj_bias, norm1_gain, norm1_shift, norm2_gain, norm2_shift, fc2_bias, qv_bias, fc1_bias,
    )
    pairs = []
    for step in range(1, count):
        before = own_a[-1]
        if step == 2:
            before = tie(before, other_a[0], normed)
        elif step > 2:
            before = tie(before, other_a[step - 2])
        if step == count - 1:
            pairs.append(order(join, piece_2, arrived_2))
            before = tie(before, pairs[0])
        own_a.append(ring_down(before, count))
        other_a.append(ctx_swap(own_a[-1]))
    half = count // 2

    own_1 = [tie(fc1_weight, own_a[-1], other_a[-2])]
    own_1.append(ring_down(own_1[-1], count))

    def next_1(until):
        while len(own_1) < until:
            own_1.append(ring_down(own_1[-1], count))

    def next_2(until):
        while len(pairs) < until:
            pairs.append(ring_down(pairs[-1], count))

    next_1(half)
    qkv_w, proj_t, queries, keys, values = order(
        lambda *values: qkv(count, values[: 2 * count], *values[2 * count :]), *own_a, *other_a, normed, vec
    )
    keys_far, values_far = ctx_swap(keys), ctx_swap(values)
    next_1(half + 1)
    next_2(half)
    partial = order(attention_near, queries, keys, values)
    both, each = order(join, own_1[-1], pairs[-1]), own_1[0].shape[0]
    while len(own_1) < count:
        both = ring_down(both, count)
        own_1.append(both[:each])
        pairs.append(both[each:])
    order.wait([keys_far, values_far])
    other_1 = [ctx_swap(order(join, *own_1[: half + 1]))]
    mixture, lse, *terms = order(attention_far, queries, keys_far, values_far, *partial, proj_t)
    attn = TpSum(order, False, *terms)
    attn.far()
    pairs[-1] = order(relay, pairs[-1])
    next_2(count)
    order.wait(other_1[0])
    other_1.append(ctx_swap(order(join, *own_1[half + 1 :])))
    w1 = order(lambda *pieces: assemble(pieces[:count], pieces[count:]), *own_1, *other_1)
    w2 = order(lambda *pieces: assemble_pairs(pieces), *pairs)
    attn.back()

    middle, second, hidden_b, d_pre, sums_1, *terms = order(lambda *values: mlp(values[:4], *values[4:]), *attn.result, x, g, vec, w1, w2)
    d_second = TpSum(order, False, *terms)
    d_second.far()
    blocks_2 = order(functools.partial(weight_grad, grad_2_kernel, count, width, hidden, 3, 1), g, hidden_b)
    blocks_1 = order(functools.partial(grad_1, count), second, d_pre)
    grads = PairScatter(order, count, blocks_1, *blocks_2)
    out_sum = TpSum(order, False, *order(mlp_out, hidden_b, w2))
    d_second.back()
    out_sum.far()
    low, d_mix, delta, lse_row, sums_2 = order(
        lambda *values: norm2_back(values[:4], *values[4:]), *d_second.result, middle, g, vec, proj_t, mixture, lse
    )

    grads.joint()
    state = (d_mix, lse_row, delta)
    first, second_pair = (0, 1), (2, 3)
    dkv_one, dq_one = order(functools.partial(attention_back, first, bf16, 16), queries, keys_far, values_far, *state)
    back_one = ctx_swap(dkv_one)
    dkv_two, dq_two = order(functools.partial(attention_back, second_pair, bf16, 0), queries, keys_far, values_far, *state)
    back_two = ctx_swap(dkv_two)
    dkv_here, dq_here = order(functools.partial(attention_back, (0, 1, 2, 3), f32, 0), queries, keys, values, *state)
    for _ in range(1, count - 2):
        grads.joint()
    order.wait(out_sum.arrived)
    d_proj, sums_3, *terms = order(qkv_back, dq_one, dq_two, dq_here, dkv_here, back_one, back_two, qkv_w)
    d_normed = TpSum(order, True, *terms)
    blocks_a = order(
        functools.partial(weight_grad, grad_a_kernel, count, width, 4 * WIDTH, 4, 2), normed, d_proj, low, mixture
    )
    grad_a = SwapScatter(order, count, *blocks_a)
    d_normed.far()
    order.wait(grads.arrived)
    grad_a.step()
    order.wait(grad_a.arrived)
    d_normed.back()
    for _ in range(1, half):
        grad_a.step()
    grads.ends()
    order.wait(grad_a.lower)
    input_grad, sums = order(
        lambda *values: norm1_back(values[:4], *values[4:]), *d_normed.result, low, x, vec, sums_1, sums_2, sums_3
    )
    out_sum.back()
    for _ in range(half, count - 1):
        grad_a.step()
    swaps = exchanges(count)
    sums = order(add, sums, swaps[0](sums))
    order.wait(grads.arrived)
    out_rows = order(lambda *values: layer_out(values[:4], *values[4:]), *out_sum.result, middle, vec)
    for swap in swaps[1:-1]:
        order.wait(grad_a.arrived)
        sums = order(add, sums, swap(sums))
    grad_a.step(finish_a)
    grads.last_second(finish_2)
    grads.last_first()
    grad_qkv, grad_proj = grad_a.result
    sums = order(finish_sums, sums, swaps[-1](sums))
    g_fc1_bias, g_fc2_bias, g_gain_two, g_shift_two, g_proj_bias, g_gain_one, g_shift_one, g_q_bias, g_v_bias = sums
    return (
        out_rows[None],
        input_grad[None],
        grad_qkv,
        g_q_bias,
        g_v_bias,
        grad_proj,
        g_proj_bias,
        g_gain_one,
        g_shift_one,
        g_gain_two,
        g_shift_two,
        grads.first,
        g_fc1_bias,
        grads.second,
        g_fc2_bias,
    )


def solution(mesh):
    split = ("shard", "ctx")
    tokens, rows, columns = P("shard", "ctx", None), P(split, "tp"), P("tp", split)
    stack = P(split, None, "tp")
    own, copied = P("tp"), P()
    in_specs = (
        tokens,
        stack,
        own,
        own,
        columns,
        copied,
        copied,
        copied,
        copied,
        copied,
        rows,
        own,
        columns,
        copied,
        tokens,
    )
    out_specs = (
        tokens,
        tokens,
        stack,
        own,
        own,
        columns,
        copied,
        copied,
        copied,
        copied,
        copied,
        rows,
        own,
        columns,
        copied,
    )
    return jax.shard_map(
        functools.partial(layer, mesh.shape["shard"]),
        mesh=mesh,
        in_specs=in_specs,
        out_specs=out_specs,
        check_vma=False,
    )
```

```python
import functools

import jax
import jax.numpy as jnp
from jax import lax
from jax.experimental import pallas as pl
from jax.experimental.pallas import tpu as pltpu
from jax.sharding import PartitionSpec as P

HD = 64
HEADS = 4
WIDTH = HEADS * HD

norm_eps = 1e-06
bf16, f32 = jnp.bfloat16, jnp.float32
VMEM_LIMIT, VMEM_MLP, VMEM_MOST = 24 * 1024 * 1024, 36 * 1024 * 1024, 58 * 1024 * 1024
PARTS = (slice(0, 784),)

CTX_PAIRS = [(0, 1), (1, 0)]
CORE_PAIRS = [(0, 1), (1, 0), (2, 3), (3, 2)]
FAR_PAIRS = [(0, 2), (2, 0), (1, 3), (3, 1)]


def cost(micros):
    return pl.CostEstimate(flops=int(micros * 1e5), bytes_accessed=1024, transcendentals=0)


class Order:
    def __init__(self):
        self.tokens = []

    def __call__(self, work, *values):
        CHAIN[:] = [self.tokens]
        result = work(*values)
        self.tokens = [CHAIN.pop()]
        return result

    def wait(self, value):
        self.tokens.extend(jax.tree.leaves(value))
        return value


CHAIN = []
WHOLE, PLACED = pl.BlockSpec(memory_space=pltpu.VMEM), pl.BlockSpec(memory_space=pl.ANY)
TOKEN = jax.ShapeDtypeStruct((8, 128), f32)


def launch(kernel, outs, micros, name, in_specs, out_specs, grid=(), scratch=(), limit=VMEM_LIMIT):
    def run(*values):
        tokens = [token for token in CHAIN.pop() if not any(token is value for value in values)]
        first, last = len(values), len(values) + len(tokens)
        end = last + len(outs)

        def ordered(*refs):
            kernel(*refs[:first], *refs[last:end], *refs[end + 1 :])
            refs[end][...] = jnp.zeros_like(refs[end])

        *results, token = pl.pallas_call(
            ordered,
            grid=grid,
            out_shape=[*(jax.ShapeDtypeStruct(shape, dtype) for shape, dtype in outs), TOKEN],
            in_specs=[*in_specs(len(values)), *[WHOLE] * len(tokens)],
            out_specs=[*out_specs, WHOLE],
            scratch_shapes=scratch,
            compiler_params=pltpu.CompilerParams(vmem_limit_bytes=limit),
            cost_estimate=cost(micros),
            name=name,
        )(*values, *tokens)
        CHAIN.append(token)
        return results

    return run


def call(kernel, outs, micros, name, scratch=(), far=(), limit=VMEM_LIMIT):
    def in_specs(count):
        return [PLACED if place in far else WHOLE for place in range(count)]

    return launch(kernel, outs, micros, name, in_specs, [WHOLE] * len(outs), (), scratch, limit)


def fetch(pairs, sems):
    copies = [pltpu.make_async_copy(source, target, sems.at[i]) for i, (source, target) in enumerate(pairs)]
    for copy in copies:
        copy.start()
    return copies


def dot_nn(left, right):
    return jnp.dot(left, right, preferred_element_type=f32)


def dot_tn(left, right):
    return lax.dot_general(left, right, (((0,), (0,)), ((), ())), preferred_element_type=f32)


def dot_nt(left, right):
    return lax.dot_general(left, right, (((1,), (1,)), ((), ())), preferred_element_type=f32)


def tie(value, *before):
    return lax.optimization_barrier((value, *before))[0]


def ctx_swap(value):
    return lax.ppermute(value, "ctx", CTX_PAIRS)


def core_swap(value):
    return lax.ppermute(value, "tp", CORE_PAIRS)


def far_swap(value):
    return lax.ppermute(value, "tp", FAR_PAIRS)


def ring_down(value, count):
    return lax.ppermute(value, "shard", [(i, (i - 1) % count) for i in range(count)])


def ring_up(value, count):
    return lax.ppermute(value, "shard", [(i, (i + 1) % count) for i in range(count)])


def relay(value):
    return call(relay_kernel, [(value.shape, value.dtype)], 1, "relay")(value)[0]


def relay_kernel(value_ref, out_ref):
    out_ref[...] = value_ref[...]


def add_kernel(left, *refs):
    out, at = refs[-1], 0
    for right in refs[:-1]:
        part = slice(at, at + right.shape[1])
        out[:, part] = (left[:, part].astype(f32) + right[...].astype(f32)).astype(out.dtype)
        at += right.shape[1]


def add(left, *rights):
    return call(add_kernel, [(left.shape, left.dtype)], 1, "add")(left, *rights)[0]


def add_apart_kernel(left, *refs):
    rights, outs = refs[: len(refs) // 2], refs[len(refs) // 2 :]
    for i, (right, out) in enumerate(zip(rights, outs)):
        part = slice(i * out.shape[1], (i + 1) * out.shape[1])
        out[...] = (left[:, part].astype(f32) + right[...].astype(f32)).astype(out.dtype)


def add_apart(left, *rights):
    return call(add_apart_kernel, [(right.shape, right.dtype) for right in rights], 1, "add_apart")(left, *rights)


def add_halves_kernel(left, right, *outs):
    for i, out in enumerate(outs):
        part = slice(i * out.shape[1], (i + 1) * out.shape[1])
        out[...] = (left[:, part].astype(f32) + right[:, part].astype(f32)).astype(out.dtype)


def add_halves(left, right):
    half = (left.shape[0], left.shape[1] // 2)
    return call(add_halves_kernel, [(half, left.dtype)] * 2, 1, "add_halves")(left, right)


class TpSum:
    def __init__(self, order, apart, keep, *sends):
        self.order, self.apart, self.keep = order, apart, keep
        self.arrived = [core_swap(send) for send in sends]

    def far(self):
        if self.apart:
            self.near = self.order(add_apart, self.keep, *self.arrived)
        else:
            self.near = [self.order(add, self.keep, *self.arrived)]
        self.arrived = [far_swap(piece) for piece in self.near]

    def back(self):
        if self.apart:
            total = [self.order(add, *pair) for pair in zip(self.near, self.arrived)]
        else:
            total = self.order(add_halves, *self.near, *self.arrived)
        self.result = [*total, *(core_swap(piece) for piece in total)]


class SwapScatter:
    def __init__(self, order, count, keep, sends):
        self.order, self.count, self.keep = order, count, keep
        self.other, self.later = ctx_swap(sends[0]), list(sends[1:])
        self.rows, self.first = keep[0].shape[0], (count // 2 if self.later else 0)
        self.at, self.arrived = count - 1, None

    def step(self, finish=None):
        at = self.at
        if at < self.first:
            self.other, self.first = self.lower, 0
        terms, places = [self.keep[at], self.other], [0, at - self.first]
        if self.arrived is not None:
            terms, places = [*terms, self.arrived], [*places, 0]
        if finish:
            self.result = self.order(finish, *(term[place * self.rows : (place + 1) * self.rows] for term, place in zip(terms, places)))
            return
        extra = self.later.pop() if self.later else None
        value, *copied = self.order(
            lambda *values: block_sum(values, self.rows, places, bf16 if at else f32, extra), *terms
        )
        if copied:
            self.lower = ctx_swap(copied[0])
        if at:
            self.arrived, self.at = ring_up(value, self.count), at - 1
        else:
            self.result = value


class PairScatter:
    def __init__(self, order, count, blocks, keep, sends):
        self.order, self.count, self.blocks, self.keep = order, count, blocks, keep
        self.other, self.rows, self.at = ctx_swap(sends[0]), keep[0].shape[0], count - 2
        self.arrived = ring_up(blocks[-1], count)

    def joint(self):
        at, rows = self.at, self.rows
        value = self.order(
            lambda *values: joint_sum(rows, at + 1, *values), self.blocks[at], self.arrived, self.keep[at + 1], self.other
        )
        self.arrived, self.at = ring_up(value, self.count), at - 1

    def ends(self):
        rows = self.rows
        self.own, other, value = self.order(
            lambda *values: ends_sum(rows, *values), self.blocks[0], self.arrived, self.keep[1], self.other
        )
        self.swapped, self.arrived = ctx_swap(other), ring_up(value, self.count)

    def last_second(self, finish):
        self.second = self.order(finish, self.keep[0], self.other[: self.rows], self.arrived)

    def last_first(self):
        self.first = self.order(lambda *values: block_sum(values, self.rows, [0, 0], f32), self.own, self.swapped)[0]


def joint_sum(rows, at, block, arrived, keep, other):
    def kernel(block_ref, arrived_ref, keep_ref, other_ref, out_ref):
        pair, third = slice(0, 2 * rows), slice(2 * rows, 3 * rows)
        out_ref[pair, :] = (block_ref[...] + arrived_ref[pair, :].astype(f32)).astype(bf16)
        value = keep_ref[...] + other_ref[at * rows : (at + 1) * rows, :].astype(f32)
        if arrived_ref.shape[0] > 2 * rows:
            value = value + arrived_ref[third, :].astype(f32)
        out_ref[third, :] = value.astype(bf16)

    return call(kernel, [((3 * rows, block.shape[1]), bf16)], 1, "joint_sum")(block, arrived, keep, other)[0]


def ends_sum(rows, block, arrived, keep, other):
    def kernel(block_ref, arrived_ref, keep_ref, other_ref, own_ref, away_ref, out_ref):
        own, away, third = slice(0, rows), slice(rows, 2 * rows), slice(2 * rows, 3 * rows)
        own_ref[...] = block_ref[own, :] + arrived_ref[own, :].astype(f32)
        away_ref[...] = (block_ref[away, :] + arrived_ref[away, :].astype(f32)).astype(bf16)
        value = keep_ref[...] + other_ref[away, :].astype(f32) + arrived_ref[third, :].astype(f32)
        out_ref[...] = value.astype(bf16)

    shape = (rows, block.shape[1])
    return call(kernel, [(shape, f32), (shape, bf16), (shape, bf16)], 1, "ends_sum")(block, arrived, keep, other)


def split_sum_kernel(left, right, own_ref, other_ref):
    side = own_ref.shape[0]
    own_ref[...] = left[:side, :].astype(f32) + right[:side, :].astype(f32)
    other_ref[...] = (left[side:, :].astype(f32) + right[side:, :].astype(f32)).astype(bf16)


def split_sum(left, right):
    shape = (left.shape[0] // 2, left.shape[1])
    return call(split_sum_kernel, [(shape, f32), (shape, bf16)], 1, "split_sum")(left, right)


def block_sum(terms, rows, at, dtype, extra=None):
    columns = terms[0].shape[1]

    def kernel(*refs):
        ins, outs = refs[: len(terms)], refs[-1 if extra is None else -2 :]
        outs[0][...] = sum(ref[...].astype(f32) for ref in ins).astype(dtype)
        if extra is not None:
            outs[1][...] = refs[len(terms)][...]

    def spec(place):
        return pl.BlockSpec((rows, columns), lambda i: (place, 0))

    specs, outs, out_specs = [spec(place) for place in at], [((rows, columns), dtype)], [spec(0)]
    values = list(terms)
    if extra is not None:
        whole = pl.BlockSpec(extra.shape, lambda i: (0, 0))
        specs, outs, out_specs = [*specs, whole], [*outs, (extra.shape, extra.dtype)], [*out_specs, whole]
        values.append(extra)
    return launch(kernel, outs, 1, "block_sum", lambda count: specs, out_specs, (1,))(*values)


def finish_a_kernel(one, two, three, qkv_ref, proj_ref):
    total = one[...] + two[...].astype(f32) + three[...].astype(f32)
    for i in range(3):
        qkv_ref[i] = total[:, i * WIDTH : (i + 1) * WIDTH]
    right = total[:, 3 * WIDTH :]
    proj_ref[...] = right.T if proj_ref.shape[0] == WIDTH else right


def finish_a(one, two, three):
    rows = one.shape[0]
    shape = (WIDTH, rows) if rows % 128 == 0 else (rows, WIDTH)
    qkv, proj = call(finish_a_kernel, [((3, rows, WIDTH), f32), (shape, f32)], 1, "finish_a")(one, two, three)
    return qkv.transpose(1, 0, 2), proj if rows % 128 == 0 else proj.T


def finish_2_kernel(one, two, three, out_ref):
    out_ref[...] = (one[...] + two[...].astype(f32) + three[...].astype(f32)).T


def finish_2(one, two, three):
    rows, columns = one.shape
    if rows % 128:
        return block_sum((one, two, three), rows, (0, 0, 0), f32)[0].T
    return call(finish_2_kernel, [((columns, rows), f32)], 1, "finish_2")(one, two, three)[0]


def finish_sums_kernel(left, right, *outs):
    for i, out in enumerate(outs):
        row, first = (i, 0) if i < 7 else (7, (i - 7) * WIDTH)
        for part in range(out.shape[0]):
            at = slice(first + part * 128, first + (part + 1) * 128)
            out[part : part + 1, :] = left[row : row + 1, at] + right[row : row + 1, at]


def finish_sums(left, right):
    lines = left.shape[1] // 128
    outs = [((lines, 128), f32)] * 7 + [((WIDTH // 128, 128), f32)] * 2
    return [out.reshape(-1) for out in call(finish_sums_kernel, outs, 1, "finish_sums")(left, right)]


def exchanges(count):
    steps = [1 << i for i in range(count.bit_length() - 1)]
    swaps = [lambda value, step=step: lax.ppermute(value, "shard", [(i, i ^ step) for i in range(count)]) for step in steps]
    return [ctx_swap, *swaps]


def place(count, rows, step, side):
    shard, ctx = lax.axis_index("shard"), lax.axis_index("ctx")
    owner = lax.rem(shard + step, count) * 2 + (ctx + side) % 2
    return pl.ds(pl.multiple_of(owner * rows, rows), rows)


def core_columns(width, side, piece=None):
    half = width // 2
    core = (lax.axis_index("tp") + side) % 2
    if piece is None:
        return pl.ds(pl.multiple_of(core * half, half), half)
    return pl.ds(pl.multiple_of(core * half + piece * (half // 2), half // 2), half // 2)


def send_terms(at, left, right_ref, keep_ref, sends):
    width = right_ref.shape[0]
    keep_ref[at, :] = dot_nt(left, right_ref[core_columns(width, 0), :]).astype(bf16)
    terms = dot_nt(left, right_ref[core_columns(width, 1), :]).astype(bf16)
    for piece, out in enumerate(sends):
        out[at, :] = terms[:, piece * width // 4 : (piece + 1) * width // 4]


def term_shapes(rows, width):
    return [((rows, width // 2), bf16), ((rows, width // 4), bf16), ((rows, width // 4), bf16)]


def normalize(values):
    centered = values - jnp.mean(values, axis=-1, keepdims=True)
    inverse = lax.rsqrt(jnp.mean(centered * centered, axis=-1, keepdims=True) + norm_eps)
    return centered * inverse, inverse


def normalize_back(unit, inverse, d_unit):
    mean = jnp.mean(d_unit, axis=-1, keepdims=True)
    along = jnp.mean(d_unit * unit, axis=-1, keepdims=True)
    return inverse * (d_unit - mean - unit * along)


def column_sum(values):
    return jnp.sum(values, axis=0, keepdims=True)


def assemble_kernel(count, rows, *refs):
    own, other, out = refs[:count], refs[count:-1], refs[-1]
    where = [(part, at) for part in other for at in range(0, part.shape[0], rows)]
    for step, (part, at) in enumerate(where):
        out[place(count, rows, step, 0), :] = own[step][...]
        out[place(count, rows, step, 1), :] = part[at : at + rows, :]


def assemble(own, other):
    count = len(own)
    rows, columns = own[0].shape
    shape = (2 * count * rows, columns)
    return call(functools.partial(assemble_kernel, count, rows), [(shape, bf16)], 1.5, "assemble")(*own, *other)[0]


def assemble_pairs_kernel(count, rows, *refs):
    pairs, out = refs[:count], refs[count]
    for step in range(count):
        for side in range(2):
            out[place(count, rows, step, side), :] = pairs[step][side * rows : (side + 1) * rows, :]


def assemble_pairs(pairs):
    count = len(pairs)
    rows, columns = pairs[0].shape[0] // 2, pairs[0].shape[1]
    shape = (2 * count * rows, columns)
    return call(functools.partial(assemble_pairs_kernel, count, rows), [(shape, bf16)], 1.5, "assemble_pairs")(*pairs)[0]


def norm1_kernel(x_hbm, *refs):
    sources, vec_ref, out_ref, x_ref, held, sems = refs[:8], *refs[8:]
    copies = fetch([(x_hbm, x_ref), *[(source, held.at[row]) for row, source in enumerate(sources)]], sems)
    for copy in copies[1:]:
        copy.wait()
    for row in range(8):
        for part in range(sources[0].shape[0]):
            vec_ref[row : row + 1, part * 128 : (part + 1) * 128] = held[row, part : part + 1, :].astype(f32)
    copies[0].wait()
    for at in PARTS:
        unit, _ = normalize(x_ref[at, :].astype(f32))
        out_ref[at, :] = (unit * vec_ref[1:2, :] + vec_ref[2:3, :]).astype(bf16)


def norm1(x, vectors):
    rows, width = x.shape
    vectors = [vector.reshape(-1, 128) for vector in vectors]
    outs = [((8, width), f32), ((rows, width), bf16)]
    scratch = [pltpu.VMEM((rows, width), bf16), pltpu.VMEM((8, *vectors[0].shape), bf16), pltpu.SemaphoreType.DMA((9,))]
    return call(norm1_kernel, outs, 3, "norm1", scratch, range(9), VMEM_MOST)(x, *vectors)


def pack_kernel(qkv_hbm, proj_hbm, fc2_hbm, a_ref, t_ref, qkv_ref, proj_ref, fc2_ref, sems):
    copies = fetch([(qkv_hbm, qkv_ref), (proj_hbm, proj_ref), (fc2_hbm, fc2_ref)], sems)
    copies[0].wait()
    for i in range(3):
        a_ref[:, i * WIDTH : (i + 1) * WIDTH] = qkv_ref[i]
    copies[1].wait()
    copies[2].wait()
    turned = proj_ref.shape[0] == WIDTH
    a_ref[:, 3 * WIDTH :] = proj_ref[...].T if turned else proj_ref[...]
    t_ref[...] = fc2_ref[...].T if turned else fc2_ref[...]


def pack(qkv_weight, proj_weight, fc2_weight):
    rows, hidden = fc2_weight.shape[1], fc2_weight.shape[0]
    outs = [((rows, 4 * WIDTH), bf16), ((rows, hidden), bf16)]
    if rows % 128:
        proj_weight, fc2_weight = proj_weight.T, fc2_weight.T
    scratch = [pltpu.VMEM((3, rows, WIDTH), bf16), pltpu.VMEM(proj_weight.shape, bf16), pltpu.VMEM(fc2_weight.shape, bf16)]
    scratch.append(pltpu.SemaphoreType.DMA((3,)))
    return call(pack_kernel, outs, 1, "pack", scratch, (0, 1, 2), VMEM_MOST)(qkv_weight.transpose(1, 0, 2), proj_weight, fc2_weight)


def qkv_kernel(count, rows, *refs):
    pieces = refs[: 2 * count]
    normed_hbm, vec_hbm, w_ref, p_ref, q_ref, k_ref, v_ref, normed_ref, vec_ref, sems = refs[2 * count :]
    pairs = [(normed_hbm, normed_ref), (vec_hbm, vec_ref)]
    for side in range(2):
        for step in range(count):
            at, index = place(count, rows, step, side), side * count + step
            pairs.append((pieces[index].at[:, pl.ds(0, 3 * WIDTH)], w_ref.at[at]))
            pairs.append((pieces[index].at[:, pl.ds(3 * WIDTH, WIDTH)], p_ref.at[at]))
    for copy in fetch(pairs, sems):
        copy.wait()
    for at in PARTS:
        projected = dot_nn(normed_ref[at, :], w_ref[...])
        queries = (projected[:, :WIDTH] + vec_ref[6:7, :WIDTH]).astype(bf16)
        q_ref[at, :] = (queries.astype(f32) * HD ** (-0.5)).astype(bf16)
        k_ref[at, :] = projected[:, WIDTH : 2 * WIDTH].astype(bf16)
        v_ref[at, :] = (projected[:, 2 * WIDTH :] + vec_ref[6:7, WIDTH : 2 * WIDTH]).astype(bf16)


def qkv(count, pieces, normed, vec):
    rows = pieces[0].shape[0]
    tokens, width = normed.shape
    outs = [((width, 3 * WIDTH), bf16), ((width, WIDTH), bf16), *[((tokens, WIDTH), bf16)] * 3]
    scratch = [pltpu.VMEM(normed.shape, bf16), pltpu.VMEM(vec.shape, f32), pltpu.SemaphoreType.DMA((4 * count + 2,))]
    kernel = functools.partial(qkv_kernel, count, rows)
    return call(kernel, outs, 4, "qkv", scratch, range(2 * count + 2))(*pieces, normed, vec)


def head_mask(shape, head):
    lane = lax.broadcasted_iota(jnp.int32, shape, len(shape) - 1)
    return (lane >= head * HD) & (lane < (head + 1) * HD)


def fwd_near_kernel(q_ref, k_ref, v_ref, o_ref, m_ref, l_ref):
    keys, values = k_ref[...], v_ref[...]
    for at in PARTS:
        q = q_ref[at, :]
        o, m, total = (jnp.zeros(q.shape, f32) for _ in range(3))
        for head in range(HEADS):
            mask = head_mask(q.shape, head)
            scores = dot_nt(jnp.where(mask, q, jnp.zeros_like(q)), keys)
            top = jnp.max(scores, axis=-1, keepdims=True)
            weights = jnp.exp(scores - top)
            row_sum = jnp.sum(weights, axis=-1, keepdims=True)
            mixed = dot_nn(weights.astype(bf16), values)
            o = jnp.where(mask, mixed, o)
            m = jnp.where(mask, top, m)
            total = jnp.where(mask, row_sum, total)
        o_ref[at, :] = o
        m_ref[at, :] = m
        l_ref[at, :] = total


def fwd_far_kernel(q_ref, k_ref, v_ref, o_ref, m_ref, l_ref, p_ref, mix_ref, lse_ref, keep_ref, *sends):
    keys, values = k_ref[...], v_ref[...]
    for at in PARTS:
        q = q_ref[at, :]
        o, m, total = o_ref[at, :], m_ref[at, :], l_ref[at, :]
        o_out = jnp.zeros(q.shape, f32)
        lse = jnp.zeros((q.shape[0], 128), f32)
        lane = lax.broadcasted_iota(jnp.int32, lse.shape, 1)
        for head in range(HEADS):
            mask = head_mask(q.shape, head)
            scores = dot_nt(jnp.where(mask, q, jnp.zeros_like(q)), keys)
            before = m[:, head * HD : head * HD + 1]
            top = jnp.maximum(jnp.max(scores, axis=-1, keepdims=True), before)
            weights = jnp.exp(scores - top)
            carry = jnp.exp(before - top)
            row_sum = jnp.sum(weights, axis=-1, keepdims=True) + carry * total[:, head * HD : head * HD + 1]
            mixed = dot_nn(weights.astype(bf16), values) + carry * o
            o_out = jnp.where(mask, mixed / row_sum, o_out)
            lse = jnp.where(lane == head, top + jnp.log(row_sum), lse)
        mixture = o_out.astype(bf16)
        mix_ref[at, :] = mixture
        lse_ref[at, :] = lse
        send_terms(at, mixture, p_ref, keep_ref, sends)


def attention_near(q, k, v):
    return call(fwd_near_kernel, [(q.shape, f32)] * 3, 6, "attention_near")(q, k, v)


def attention_far(q, k, v, o, m, total, proj_t):
    rows = q.shape[0]
    outs = [(q.shape, bf16), ((rows, 128), f32), *term_shapes(rows, proj_t.shape[0])]
    return call(fwd_far_kernel, outs, 8, "attention_far")(q, k, v, o, m, total, proj_t)


def merge(out, refs):
    width = out.shape[1]
    for i, ref in enumerate(refs):
        out[:, core_columns(width, i // 2, i % 2)] = ref[...].astype(out.dtype)


def mlp_kernel(
    sum_1, sum_2, sum_3, sum_4, x_ref, g_ref, vec_ref, w1_ref, w2_ref,
    mid_ref, second_ref, hidden_ref, d_pre_ref, sums_ref, keep_ref, send_1, send_2, x_held, g_held, sems,
):
    pairs = [pair for at in PARTS for pair in ((x_ref.at[at], x_held.at[at]), (g_ref.at[at], g_held.at[at]))]
    copies = fetch(pairs, sems)
    merge(mid_ref, (sum_1, sum_2, sum_3, sum_4))
    sums_ref[...] = jnp.zeros_like(sums_ref)
    for i, at in enumerate(PARTS):
        copies[2 * i].wait()
        middle = mid_ref[at, :] + x_held[at, :].astype(f32) + vec_ref[0:1, :]
        mid_ref[at, :] = middle
        unit, _ = normalize(middle)
        second = (unit * vec_ref[3:4, :] + vec_ref[4:5, :]).astype(bf16)
        second_ref[at, :] = second
        copies[2 * i + 1].wait()
        grad = g_held[at, :]
        sums_ref[1:2, :] += column_sum(grad.astype(f32))
        pre = dot_nn(second, w1_ref[...]) + vec_ref[7:8, :]
        upper = 0.5 + 0.5 * lax.erf(pre * (0.5**0.5))
        hidden_ref[at, :] = (pre * upper).astype(bf16)
        slope = upper + pre * (jnp.exp(-0.5 * pre * pre) * 0.3989422804014327)
        d_pre = (slope * dot_nn(grad, w2_ref[...])).astype(bf16)
        d_pre_ref[at, :] = d_pre
        sums_ref[0:1, :] += column_sum(d_pre.astype(f32))
        send_terms(at, d_pre, w1_ref, keep_ref, (send_1, send_2))


def mlp(sums, x, g, vec, w1, w2):
    (rows, width), hidden = x.shape, w1.shape[1]
    outs = [(x.shape, f32), (x.shape, bf16), ((rows, hidden), bf16), ((rows, hidden), bf16), ((8, width), f32)]
    outs += term_shapes(rows, width)
    scratch = [pltpu.VMEM(x.shape, bf16), pltpu.VMEM(x.shape, bf16), pltpu.SemaphoreType.DMA((4,))]
    return call(mlp_kernel, outs, 8, "mlp", scratch, (4, 5), VMEM_MLP)(*sums, x, g, vec, w1, w2)


def mlp_out_kernel(hidden_ref, w2_ref, keep_ref, *sends):
    for at in PARTS:
        send_terms(at, hidden_ref[at, :], w2_ref, keep_ref, sends)


def mlp_out(hidden, w2):
    return call(mlp_out_kernel, term_shapes(hidden.shape[0], w2.shape[0]), 2, "mlp_out")(hidden, w2)


def layer_out_kernel(sum_1, sum_2, sum_3, sum_4, mid_ref, vec_ref, out_ref, work_ref):
    merge(work_ref, (sum_1, sum_2, sum_3, sum_4))
    for at in PARTS:
        out_ref[at, :] = (mid_ref[at, :] + work_ref[at, :] + vec_ref[5:6, :]).astype(bf16)


def layer_out(sums, middle, vec):
    scratch = [pltpu.VMEM(middle.shape, f32)]
    return call(layer_out_kernel, [(middle.shape, bf16)], 2, "layer_out", scratch)(*sums, middle, vec)[0]


def spread(count, grads_ref, *outs):
    rows, sends = grads_ref.shape[0] // (2 * count), outs[count:]
    each = count // len(sends)
    for step in range(count):
        outs[step][...] = grads_ref[place(count, rows, step, 0), :]
        out, at = sends[len(sends) - 1 - step // each], (step % each) * rows
        out[at : at + rows, :] = grads_ref[place(count, rows, step, 1), :].astype(bf16)


def grad_1_kernel(count, left, right, *refs):
    outs, grads_ref = refs[:-1], refs[-1]
    grads_ref[...] = dot_tn(left[...], right[...])
    rows = grads_ref.shape[0] // (2 * count)
    for step, out in enumerate(outs):
        for side in range(2):
            out[side * rows : (side + 1) * rows, :] = grads_ref[place(count, rows, step, side), :].astype(out.dtype)


def grad_1(count, left, right):
    width, columns = left.shape[1], right.shape[1]
    scratch, shape = [pltpu.VMEM((width, columns), f32)], (width // count, columns)
    outs = [*[(shape, f32)] * (count - 1), (shape, bf16)]
    return call(functools.partial(grad_1_kernel, count), outs, 3, "grad_1", scratch)(left, right)


def grad_2_kernel(count, left, right, *refs):
    outs, grads_ref = refs[:-1], refs[-1]
    grads_ref[...] = dot_tn(left[...], right[...])
    spread(count, grads_ref, *outs)


def grad_a_kernel(count, normed, d_proj, low, mixture, *refs):
    outs, grads_ref = refs[:-1], refs[-1]
    grads_ref[:, : 3 * WIDTH] = dot_tn(normed[...], d_proj[...])
    grads_ref[:, 3 * WIDTH :] = dot_tn(low[...], mixture[...])
    spread(count, grads_ref, *outs)


def weight_grad(kernel, count, width, columns, micros, sends, *arrays):
    scratch = [pltpu.VMEM((width, columns), f32)]
    keep, send = ((width // 2 // count, columns), f32), ((width // 2 // sends, columns), bf16)
    results = call(functools.partial(kernel, count), [keep] * count + [send] * sends, micros, kernel.__name__, scratch)(*arrays)
    return results[:count], results[count:]


def picked_rows(pick, values, terms):
    total = 0.0
    for _ in range(terms):
        part = values.astype(bf16)
        total = total + dot_nt(pick.astype(bf16), part)
        values = values - part.astype(f32)
    return total


def norm2_back_kernel(
    sum_1, sum_2, sum_3, sum_4, mid_ref, g_ref, vec_ref, p_ref, mix_ref, lse_ref,
    low_ref, d_mix_ref, delta_ref, lse_out_ref, sums_ref, work_ref, both_ref,
):
    merge(work_ref, (sum_1, sum_2, sum_3, sum_4))
    sums_ref[...] = jnp.zeros_like(sums_ref)
    for at in PARTS:
        d_second = work_ref[at, :]
        unit, inverse = normalize(mid_ref[at, :])
        sums_ref[2:3, :] += column_sum(d_second * unit)
        sums_ref[3:4, :] += column_sum(d_second)
        d_middle = g_ref[at, :].astype(f32) + normalize_back(unit, inverse, d_second * vec_ref[3:4, :])
        low = d_middle.astype(bf16)
        low_ref[at, :] = low
        sums_ref[4:5, :] += column_sum(low.astype(f32))
        d_mix = dot_nn(low, p_ref[...]).astype(bf16)
        d_mix_ref[at, :] = d_mix
        both_ref[at, :] = d_mix.astype(f32) * mix_ref[at, :].astype(f32)
    head = lax.broadcasted_iota(jnp.int32, (8, WIDTH), 0)
    lane = lax.broadcasted_iota(jnp.int32, (8, WIDTH), 1)
    pick, one = (lane // HD == head).astype(f32), (lane == head).astype(f32)[:, :128]
    delta_ref[...] = picked_rows(pick, both_ref[...], 2)
    lse_out_ref[...] = picked_rows(one, lse_ref[...], 3)


def norm2_back(sums, middle, g, vec, proj_t, mixture, lse):
    rows, width = middle.shape
    outs = [((rows, width), bf16), ((rows, WIDTH), bf16), ((8, rows), f32), ((8, rows), f32), ((8, width), f32)]
    scratch = [pltpu.VMEM((rows, width), f32), pltpu.VMEM((rows, WIDTH), f32)]
    return call(norm2_back_kernel, outs, 6, "norm2_back", scratch)(*sums, middle, g, vec, proj_t, mixture, lse)


def bwd_kernel(heads, q_ref, k_ref, v_ref, do_ref, lse_ref, delta_ref, dkv_ref, dq_ref):
    rows, count = k_ref.shape[0], len(heads)
    for place, head in enumerate(heads):
        at = slice(head * HD, (head + 1) * HD)
        low, high = (slice(i * HD, (i + 1) * HD) for i in (place, count + place))
        keys, values, q, d_out = k_ref[:, at], v_ref[:, at], q_ref[:, at], do_ref[:, at]
        probs = jnp.exp(dot_nt(keys, q) - lse_ref[head : head + 1, :])
        d_probs = dot_nt(values, d_out)
        dkv_ref[:rows, high] = dot_nn(probs.astype(bf16), d_out).astype(dkv_ref.dtype)
        d_scores = (probs * (d_probs - delta_ref[head : head + 1, :])).astype(bf16)
        dkv_ref[:rows, low] = dot_nn(d_scores, q).astype(dkv_ref.dtype)
        dq_ref[low, :] = dot_tn(keys, d_scores)
    if dkv_ref.shape[0] > rows:
        dkv_ref[rows:, :] = jnp.zeros((dkv_ref.shape[0] - rows, dkv_ref.shape[1]), dkv_ref.dtype)


def attention_back(heads, dtype, more, q, k, v, d_out, lse, delta):
    rows = k.shape[0] + more
    outs = [((rows, 2 * len(heads) * HD), dtype), ((len(heads) * HD, q.shape[0]), f32)]
    kernel = functools.partial(bwd_kernel, heads)
    return call(kernel, outs, 3 * len(heads), "attention_back")(q, k, v, d_out, lse, delta)


def qkv_back_kernel(
    dq_one, dq_two, dq_here, dkv_here, back_one, back_two, w_ref, d_proj_ref, sums_ref, keep_ref, *sends
):
    rows, half = dkv_here.shape[0], WIDTH // 2
    sums_ref[...] = jnp.zeros_like(sums_ref)
    for place, (away, back) in enumerate(((dq_one, back_one), (dq_two, back_two))):
        at = slice(place * half, (place + 1) * half)
        d_query = ((away[...] + dq_here[at, :]).T * HD ** (-0.5)).astype(bf16)
        d_proj_ref[:, at] = d_query
        sums_ref[7:8, at] = column_sum(d_query.astype(f32))
        for part in range(2):
            here = slice(part * WIDTH + place * half, part * WIDTH + (place + 1) * half)
            there = slice(part * half, (part + 1) * half)
            value = (dkv_here[:, here] + back[:rows, there].astype(f32)).astype(bf16)
            out = slice(WIDTH + part * WIDTH + place * half, WIDTH + part * WIDTH + (place + 1) * half)
            d_proj_ref[:, out] = value
            if part:
                sums_ref[7:8, here] = column_sum(value.astype(f32))
    for at in PARTS:
        send_terms(at, d_proj_ref[at, :], w_ref, keep_ref, sends)


def qkv_back(dq_one, dq_two, dq_here, dkv_here, back_one, back_two, w):
    rows, width = dkv_here.shape[0], w.shape[0]
    outs = [((rows, 3 * WIDTH), bf16), ((8, width), f32), *term_shapes(rows, width)]
    return call(qkv_back_kernel, outs, 3, "qkv_back")(dq_one, dq_two, dq_here, dkv_here, back_one, back_two, w)


def norm1_back_kernel(
    sum_1, sum_2, sum_3, sum_4, low_ref, x_ref, vec_ref, sums_1, sums_2, sums_3, out_ref, sums_ref, work_ref, low_held, x_held, sems
):
    pairs = [pair for at in PARTS for pair in ((x_ref.at[at], x_held.at[at]), (low_ref.at[at], low_held.at[at]))]
    copies = fetch(pairs, sems)
    merge(work_ref, (sum_1, sum_2, sum_3, sum_4))
    sums_ref[...] = sums_1[...] + sums_2[...] + sums_3[...]
    for i, at in enumerate(PARTS):
        copies[2 * i].wait()
        unit, inverse = normalize(x_held[at, :].astype(f32))
        d_normed = work_ref[at, :]
        d_in = normalize_back(unit, inverse, d_normed * vec_ref[1:2, :])
        sums_ref[5:6, :] += column_sum(d_normed * unit)
        sums_ref[6:7, :] += column_sum(d_normed)
        copies[2 * i + 1].wait()
        out_ref[at, :] = (low_held[at, :].astype(f32) + d_in).astype(bf16)


def norm1_back(total, low, x, vec, *sums):
    scratch = [pltpu.VMEM(x.shape, f32), pltpu.VMEM(x.shape, bf16), pltpu.VMEM(x.shape, bf16)]
    outs, scratch = [(x.shape, bf16), (vec.shape, f32)], [*scratch, pltpu.SemaphoreType.DMA((4,))]
    return call(norm1_back_kernel, outs, 4, "norm1_back", scratch, (4, 5))(*total, low, x, vec, *sums)


def join_kernel(*refs):
    at = 0
    for ref in refs[:-1]:
        refs[-1][at : at + ref.shape[0], :] = ref[...]
        at += ref.shape[0]


def join(*pieces):
    rows = sum(piece.shape[0] for piece in pieces)
    return call(join_kernel, [((rows, pieces[0].shape[1]), bf16)], 1, "join")(*pieces)[0]


def layer(
    count,
    video_tokens,
    qkv_weight,
    q_bias,
    v_bias,
    proj_weight,
    proj_bias,
    norm1_gain,
    norm1_shift,
    norm2_gain,
    norm2_shift,
    fc1_weight,
    fc1_bias,
    fc2_weight,
    fc2_bias,
    out_grad,
):
    x, g = video_tokens[0], out_grad[0]
    tokens, width = x.shape
    hidden = fc1_bias.shape[0]
    order = Order()

    piece, piece_2 = order(pack, qkv_weight, proj_weight, fc2_weight)
    own_a, other_a = [piece], [ctx_swap(piece)]
    arrived_2 = ctx_swap(piece_2)
    qv_bias = jnp.concatenate([q_bias, v_bias, jnp.zeros((width - 2 * WIDTH,), bf16)])
    vec, normed = order(
        lambda x, *vectors: norm1(x, vectors),
        x, proj_bias, norm1_gain, norm1_shift, norm2_gain, norm2_shift, fc2_bias, qv_bias, fc1_bias,
    )
    pairs = []
    for step in range(1, count):
        before = own_a[-1]
        if step == 2:
            before = tie(before, other_a[0], normed)
        elif step > 2:
            before = tie(before, other_a[step - 2])
        if step == count - 1:
            pairs.append(order(join, piece_2, arrived_2))
            before = tie(before, pairs[0])
        own_a.append(ring_down(before, count))
        other_a.append(ctx_swap(own_a[-1]))
    half = count // 2

    own_1 = [tie(fc1_weight, own_a[-1], other_a[-2])]
    own_1.append(ring_down(own_1[-1], count))

    def next_1(until):
        while len(own_1) < until:
            own_1.append(ring_down(own_1[-1], count))

    def next_2(until):
        while len(pairs) < until:
            pairs.append(ring_down(pairs[-1], count))

    next_1(half)
    qkv_w, proj_t, queries, keys, values = order(
        lambda *values: qkv(count, values[: 2 * count], *values[2 * count :]), *own_a, *other_a, normed, vec
    )
    keys_far, values_far = ctx_swap(keys), ctx_swap(values)
    next_1(half + 1)
    next_2(half)
    partial = order(attention_near, queries, keys, values)
    both, each = order(join, own_1[-1], pairs[-1]), own_1[0].shape[0]
    while len(own_1) < count:
        both = ring_down(both, count)
        own_1.append(both[:each])
        pairs.append(both[each:])
    order.wait([keys_far, values_far])
    other_1 = [ctx_swap(order(join, *own_1[: half + 1]))]
    mixture, lse, *terms = order(attention_far, queries, keys_far, values_far, *partial, proj_t)
    attn = TpSum(order, False, *terms)
    attn.far()
    pairs[-1] = order(relay, pairs[-1])
    next_2(count)
    order.wait(other_1[0])
    other_1.append(ctx_swap(order(join, *own_1[half + 1 :])))
    w1 = order(lambda *pieces: assemble(pieces[:count], pieces[count:]), *own_1, *other_1)
    w2 = order(lambda *pieces: assemble_pairs(pieces), *pairs)
    attn.back()

    middle, second, hidden_b, d_pre, sums_1, *terms = order(lambda *values: mlp(values[:4], *values[4:]), *attn.result, x, g, vec, w1, w2)
    d_second = TpSum(order, False, *terms)
    d_second.far()
    blocks_2 = order(functools.partial(weight_grad, grad_2_kernel, count, width, hidden, 3, 1), g, hidden_b)
    blocks_1 = order(functools.partial(grad_1, count), second, d_pre)
    grads = PairScatter(order, count, blocks_1, *blocks_2)
    out_sum = TpSum(order, False, *order(mlp_out, hidden_b, w2))
    d_second.back()
    out_sum.far()
    low, d_mix, delta, lse_row, sums_2 = order(
        lambda *values: norm2_back(values[:4], *values[4:]), *d_second.result, middle, g, vec, proj_t, mixture, lse
    )

    grads.joint()
    state = (d_mix, lse_row, delta)
    first, second_pair = (0, 1), (2, 3)
    dkv_one, dq_one = order(functools.partial(attention_back, first, bf16, 16), queries, keys_far, values_far, *state)
    back_one = ctx_swap(dkv_one)
    dkv_two, dq_two = order(functools.partial(attention_back, second_pair, bf16, 0), queries, keys_far, values_far, *state)
    back_two = ctx_swap(dkv_two)
    dkv_here, dq_here = order(functools.partial(attention_back, (0, 1, 2, 3), f32, 0), queries, keys, values, *state)
    for _ in range(1, count - 2):
        grads.joint()
    order.wait(out_sum.arrived)
    d_proj, sums_3, *terms = order(qkv_back, dq_one, dq_two, dq_here, dkv_here, back_one, back_two, qkv_w)
    d_normed = TpSum(order, True, *terms)
    blocks_a = order(
        functools.partial(weight_grad, grad_a_kernel, count, width, 4 * WIDTH, 4, 2), normed, d_proj, low, mixture
    )
    grad_a = SwapScatter(order, count, *blocks_a)
    d_normed.far()
    order.wait(grads.arrived)
    grad_a.step()
    order.wait(grad_a.arrived)
    d_normed.back()
    for _ in range(1, half):
        grad_a.step()
    grads.ends()
    order.wait(grad_a.lower)
    input_grad, sums = order(
        lambda *values: norm1_back(values[:4], *values[4:]), *d_normed.result, low, x, vec, sums_1, sums_2, sums_3
    )
    out_sum.back()
    for _ in range(half, count - 1):
        grad_a.step()
    swaps = exchanges(count)
    sums = order(add, sums, swaps[0](sums))
    order.wait(grads.arrived)
    out_rows = order(lambda *values: layer_out(values[:4], *values[4:]), *out_sum.result, middle, vec)
    for swap in swaps[1:-1]:
        order.wait(grad_a.arrived)
        sums = order(add, sums, swap(sums))
    grad_a.step(finish_a)
    grads.last_second(finish_2)
    grads.last_first()
    grad_qkv, grad_proj = grad_a.result
    sums = order(finish_sums, sums, swaps[-1](sums))
    g_fc1_bias, g_fc2_bias, g_gain_two, g_shift_two, g_proj_bias, g_gain_one, g_shift_one, g_q_bias, g_v_bias = sums
    return (
        out_rows[None],
        input_grad[None],
        grad_qkv,
        g_q_bias,
        g_v_bias,
        grad_proj,
        g_proj_bias,
        g_gain_one,
        g_shift_one,
        g_gain_two,
        g_shift_two,
        grads.first,
        g_fc1_bias,
        grads.second,
        g_fc2_bias,
    )


def solution(mesh):
    split = ("shard", "ctx")
    tokens, rows, columns = P("shard", "ctx", None), P(split, "tp"), P("tp", split)
    stack = P(split, None, "tp")
    own, copied = P("tp"), P()
    in_specs = (
        tokens,
        stack,
        own,
        own,
        columns,
        copied,
        copied,
        copied,
        copied,
        copied,
        rows,
        own,
        columns,
        copied,
        tokens,
    )
    out_specs = (
        tokens,
        tokens,
        stack,
        own,
        own,
        columns,
        copied,
        copied,
        copied,
        copied,
        copied,
        rows,
        own,
        columns,
        copied,
    )
    return jax.shard_map(
        functools.partial(layer, mesh.shape["shard"]),
        mesh=mesh,
        in_specs=in_specs,
        out_specs=out_specs,
        check_vma=False,
    )
```

```python
import functools

import jax
import jax.numpy as jnp
from jax import lax
from jax.experimental import pallas as pl
from jax.experimental.pallas import tpu as pltpu
from jax.sharding import PartitionSpec as P

HD = 64
HEADS = 4
WIDTH = HEADS * HD

norm_eps = 1e-06
bf16, f32 = jnp.bfloat16, jnp.float32
VMEM_LIMIT, VMEM_MLP, VMEM_MOST = 24 * 1024 * 1024, 36 * 1024 * 1024, 58 * 1024 * 1024
PARTS = (slice(0, 784),)

CTX_PAIRS = [(0, 1), (1, 0)]
CORE_PAIRS = [(0, 1), (1, 0), (2, 3), (3, 2)]
FAR_PAIRS = [(0, 2), (2, 0), (1, 3), (3, 1)]


def cost(micros):
    return pl.CostEstimate(flops=int(micros * 1e5), bytes_accessed=1024, transcendentals=0)


class Order:
    def __init__(self):
        self.tokens = []

    def __call__(self, work, *values):
        CHAIN[:] = [self.tokens]
        result = work(*values)
        self.tokens = [CHAIN.pop()]
        return result

    def wait(self, value):
        self.tokens.extend(jax.tree.leaves(value))
        return value


CHAIN = []
WHOLE, PLACED = pl.BlockSpec(memory_space=pltpu.VMEM), pl.BlockSpec(memory_space=pl.ANY)
TOKEN = jax.ShapeDtypeStruct((8, 128), f32)


def launch(kernel, outs, micros, name, in_specs, out_specs, grid=(), scratch=(), limit=VMEM_LIMIT):
    def run(*values):
        tokens = [token for token in CHAIN.pop() if not any(token is value for value in values)]
        first, last = len(values), len(values) + len(tokens)
        end = last + len(outs)

        def ordered(*refs):
            kernel(*refs[:first], *refs[last:end], *refs[end + 1 :])
            refs[end][...] = jnp.zeros_like(refs[end])

        *results, token = pl.pallas_call(
            ordered,
            grid=grid,
            out_shape=[*(jax.ShapeDtypeStruct(shape, dtype) for shape, dtype in outs), TOKEN],
            in_specs=[*in_specs(len(values)), *[WHOLE] * len(tokens)],
            out_specs=[*out_specs, WHOLE],
            scratch_shapes=scratch,
            compiler_params=pltpu.CompilerParams(vmem_limit_bytes=limit),
            cost_estimate=cost(micros),
            name=name,
        )(*values, *tokens)
        CHAIN.append(token)
        return results

    return run


def call(kernel, outs, micros, name, scratch=(), far=(), limit=VMEM_LIMIT):
    def in_specs(count):
        return [PLACED if place in far else WHOLE for place in range(count)]

    return launch(kernel, outs, micros, name, in_specs, [WHOLE] * len(outs), (), scratch, limit)


def fetch(pairs, sems):
    copies = [pltpu.make_async_copy(source, target, sems.at[i]) for i, (source, target) in enumerate(pairs)]
    for copy in copies:
        copy.start()
    return copies


def dot_nn(left, right):
    return jnp.dot(left, right, preferred_element_type=f32)


def dot_tn(left, right):
    return lax.dot_general(left, right, (((0,), (0,)), ((), ())), preferred_element_type=f32)


def dot_nt(left, right):
    return lax.dot_general(left, right, (((1,), (1,)), ((), ())), preferred_element_type=f32)


def tie(value, *before):
    return lax.optimization_barrier((value, *before))[0]


def ctx_swap(value):
    return lax.ppermute(value, "ctx", CTX_PAIRS)


def core_swap(value):
    return lax.ppermute(value, "tp", CORE_PAIRS)


def far_swap(value):
    return lax.ppermute(value, "tp", FAR_PAIRS)


def ring_down(value, count):
    return lax.ppermute(value, "shard", [(i, (i - 1) % count) for i in range(count)])


def ring_up(value, count):
    return lax.ppermute(value, "shard", [(i, (i + 1) % count) for i in range(count)])


def relay(value):
    return call(relay_kernel, [(value.shape, value.dtype)], 1, "relay")(value)[0]


def relay_kernel(value_ref, out_ref):
    out_ref[...] = value_ref[...]


def add_kernel(left, *refs):
    out, at = refs[-1], 0
    for right in refs[:-1]:
        part = slice(at, at + right.shape[1])
        out[:, part] = (left[:, part].astype(f32) + right[...].astype(f32)).astype(out.dtype)
        at += right.shape[1]


def add(left, *rights):
    return call(add_kernel, [(left.shape, left.dtype)], 1, "add")(left, *rights)[0]


def add_apart_kernel(left, *refs):
    rights, outs = refs[: len(refs) // 2], refs[len(refs) // 2 :]
    for i, (right, out) in enumerate(zip(rights, outs)):
        part = slice(i * out.shape[1], (i + 1) * out.shape[1])
        out[...] = (left[:, part].astype(f32) + right[...].astype(f32)).astype(out.dtype)


def add_apart(left, *rights):
    return call(add_apart_kernel, [(right.shape, right.dtype) for right in rights], 1, "add_apart")(left, *rights)


def add_halves_kernel(left, right, *outs):
    for i, out in enumerate(outs):
        part = slice(i * out.shape[1], (i + 1) * out.shape[1])
        out[...] = (left[:, part].astype(f32) + right[:, part].astype(f32)).astype(out.dtype)


def add_halves(left, right):
    half = (left.shape[0], left.shape[1] // 2)
    return call(add_halves_kernel, [(half, left.dtype)] * 2, 1, "add_halves")(left, right)


class TpSum:
    def __init__(self, order, apart, keep, *sends):
        self.order, self.apart, self.keep = order, apart, keep
        self.arrived = [core_swap(send) for send in sends]

    def far(self):
        if self.apart:
            self.near = self.order(add_apart, self.keep, *self.arrived)
        else:
            self.near = [self.order(add, self.keep, *self.arrived)]
        self.arrived = [far_swap(piece) for piece in self.near]

    def back(self):
        if self.apart:
            total = [self.order(add, *pair) for pair in zip(self.near, self.arrived)]
        else:
            total = self.order(add_halves, *self.near, *self.arrived)
        self.result = [*total, *(core_swap(piece) for piece in total)]


class SwapScatter:
    def __init__(self, order, count, keep, sends):
        self.order, self.count, self.keep = order, count, keep
        self.other, self.later = ctx_swap(sends[0]), list(sends[1:])
        self.rows, self.first = keep[0].shape[0], (count // 2 if self.later else 0)
        self.at, self.arrived = count - 1, None

    def step(self, finish=None):
        at = self.at
        if at < self.first:
            self.other, self.first = self.lower, 0
        terms, places = [self.keep[at], self.other], [0, at - self.first]
        if self.arrived is not None:
            terms, places = [*terms, self.arrived], [*places, 0]
        if finish:
            self.result = self.order(finish, *(term[place * self.rows : (place + 1) * self.rows] for term, place in zip(terms, places)))
            return
        extra = self.later.pop() if self.later else None
        value, *copied = self.order(
            lambda *values: block_sum(values, self.rows, places, bf16 if at else f32, extra), *terms
        )
        if copied:
            self.lower = ctx_swap(copied[0])
        if at:
            self.arrived, self.at = ring_up(value, self.count), at - 1
        else:
            self.result = value


class PairScatter:
    def __init__(self, order, count, blocks, keep, sends):
        self.order, self.count, self.blocks, self.keep = order, count, blocks, keep
        self.other, self.rows, self.at = ctx_swap(sends[0]), keep[0].shape[0], count - 2
        self.arrived = ring_up(blocks[-1], count)

    def joint(self):
        at, rows = self.at, self.rows
        value = self.order(
            lambda *values: joint_sum(rows, at + 1, *values), self.blocks[at], self.arrived, self.keep[at + 1], self.other
        )
        self.arrived, self.at = ring_up(value, self.count), at - 1

    def ends(self):
        rows = self.rows
        self.own, other, value = self.order(
            lambda *values: ends_sum(rows, *values), self.blocks[0], self.arrived, self.keep[1], self.other
        )
        self.swapped, self.arrived = ctx_swap(other), ring_up(value, self.count)

    def last_second(self, finish):
        self.second = self.order(finish, self.keep[0], self.other[: self.rows], self.arrived)

    def last_first(self):
        self.first = self.order(lambda *values: block_sum(values, self.rows, [0, 0], f32), self.own, self.swapped)[0]


def joint_sum(rows, at, block, arrived, keep, other):
    def kernel(block_ref, arrived_ref, keep_ref, other_ref, out_ref):
        pair, third = slice(0, 2 * rows), slice(2 * rows, 3 * rows)
        out_ref[pair, :] = (block_ref[...] + arrived_ref[pair, :].astype(f32)).astype(bf16)
        value = keep_ref[...] + other_ref[at * rows : (at + 1) * rows, :].astype(f32)
        if arrived_ref.shape[0] > 2 * rows:
            value = value + arrived_ref[third, :].astype(f32)
        out_ref[third, :] = value.astype(bf16)

    return call(kernel, [((3 * rows, block.shape[1]), bf16)], 1, "joint_sum")(block, arrived, keep, other)[0]


def ends_sum(rows, block, arrived, keep, other):
    def kernel(block_ref, arrived_ref, keep_ref, other_ref, own_ref, away_ref, out_ref):
        own, away, third = slice(0, rows), slice(rows, 2 * rows), slice(2 * rows, 3 * rows)
        own_ref[...] = block_ref[own, :] + arrived_ref[own, :].astype(f32)
        away_ref[...] = (block_ref[away, :] + arrived_ref[away, :].astype(f32)).astype(bf16)
        value = keep_ref[...] + other_ref[away, :].astype(f32) + arrived_ref[third, :].astype(f32)
        out_ref[...] = value.astype(bf16)

    shape = (rows, block.shape[1])
    return call(kernel, [(shape, f32), (shape, bf16), (shape, bf16)], 1, "ends_sum")(block, arrived, keep, other)


def split_sum_kernel(left, right, own_ref, other_ref):
    side = own_ref.shape[0]
    own_ref[...] = left[:side, :].astype(f32) + right[:side, :].astype(f32)
    other_ref[...] = (left[side:, :].astype(f32) + right[side:, :].astype(f32)).astype(bf16)


def split_sum(left, right):
    shape = (left.shape[0] // 2, left.shape[1])
    return call(split_sum_kernel, [(shape, f32), (shape, bf16)], 1, "split_sum")(left, right)


def block_sum(terms, rows, at, dtype, extra=None):
    columns = terms[0].shape[1]

    def kernel(*refs):
        ins, outs = refs[: len(terms)], refs[-1 if extra is None else -2 :]
        outs[0][...] = sum(ref[...].astype(f32) for ref in ins).astype(dtype)
        if extra is not None:
            outs[1][...] = refs[len(terms)][...]

    def spec(place):
        return pl.BlockSpec((rows, columns), lambda i: (place, 0))

    specs, outs, out_specs = [spec(place) for place in at], [((rows, columns), dtype)], [spec(0)]
    values = list(terms)
    if extra is not None:
        whole = pl.BlockSpec(extra.shape, lambda i: (0, 0))
        specs, outs, out_specs = [*specs, whole], [*outs, (extra.shape, extra.dtype)], [*out_specs, whole]
        values.append(extra)
    return launch(kernel, outs, 1, "block_sum", lambda count: specs, out_specs, (1,))(*values)


def finish_a_kernel(one, two, three, qkv_ref, proj_ref):
    total = one[...] + two[...].astype(f32) + three[...].astype(f32)
    for i in range(3):
        qkv_ref[i] = total[:, i * WIDTH : (i + 1) * WIDTH]
    right = total[:, 3 * WIDTH :]
    proj_ref[...] = right.T if proj_ref.shape[0] == WIDTH else right


def finish_a(one, two, three):
    rows = one.shape[0]
    shape = (WIDTH, rows) if rows % 128 == 0 else (rows, WIDTH)
    qkv, proj = call(finish_a_kernel, [((3, rows, WIDTH), f32), (shape, f32)], 1, "finish_a")(one, two, three)
    return qkv.transpose(1, 0, 2), proj if rows % 128 == 0 else proj.T


def finish_2_kernel(one, two, three, out_ref):
    out_ref[...] = (one[...] + two[...].astype(f32) + three[...].astype(f32)).T


def finish_2(one, two, three):
    rows, columns = one.shape
    if rows % 128:
        return block_sum((one, two, three), rows, (0, 0, 0), f32)[0].T
    return call(finish_2_kernel, [((columns, rows), f32)], 1, "finish_2")(one, two, three)[0]


def finish_sums_kernel(left, right, *outs):
    for i, out in enumerate(outs):
        row, first = (i, 0) if i < 7 else (7, (i - 7) * WIDTH)
        for part in range(out.shape[0]):
            at = slice(first + part * 128, first + (part + 1) * 128)
            out[part : part + 1, :] = left[row : row + 1, at] + right[row : row + 1, at]


def finish_sums(left, right):
    lines = left.shape[1] // 128
    outs = [((lines, 128), f32)] * 7 + [((WIDTH // 128, 128), f32)] * 2
    return [out.reshape(-1) for out in call(finish_sums_kernel, outs, 1, "finish_sums")(left, right)]


def exchanges(count):
    steps = [1 << i for i in range(count.bit_length() - 1)]
    swaps = [lambda value, step=step: lax.ppermute(value, "shard", [(i, i ^ step) for i in range(count)]) for step in steps]
    return [ctx_swap, *swaps]


def place(count, rows, step, side):
    shard, ctx = lax.axis_index("shard"), lax.axis_index("ctx")
    owner = lax.rem(shard + step, count) * 2 + (ctx + side) % 2
    return pl.ds(pl.multiple_of(owner * rows, rows), rows)


def core_columns(width, side, piece=None):
    half = width // 2
    core = (lax.axis_index("tp") + side) % 2
    if piece is None:
        return pl.ds(pl.multiple_of(core * half, half), half)
    return pl.ds(pl.multiple_of(core * half + piece * (half // 2), half // 2), half // 2)


def send_terms(at, left, right_ref, keep_ref, sends):
    width = right_ref.shape[0]
    keep_ref[at, :] = dot_nt(left, right_ref[core_columns(width, 0), :]).astype(bf16)
    terms = dot_nt(left, right_ref[core_columns(width, 1), :]).astype(bf16)
    for piece, out in enumerate(sends):
        out[at, :] = terms[:, piece * width // 4 : (piece + 1) * width // 4]


def term_shapes(rows, width):
    return [((rows, width // 2), bf16), ((rows, width // 4), bf16), ((rows, width // 4), bf16)]


def normalize(values):
    centered = values - jnp.mean(values, axis=-1, keepdims=True)
    inverse = lax.rsqrt(jnp.mean(centered * centered, axis=-1, keepdims=True) + norm_eps)
    return centered * inverse, inverse


def normalize_back(unit, inverse, d_unit):
    mean = jnp.mean(d_unit, axis=-1, keepdims=True)
    along = jnp.mean(d_unit * unit, axis=-1, keepdims=True)
    return inverse * (d_unit - mean - unit * along)


def column_sum(values):
    return jnp.sum(values, axis=0, keepdims=True)


def assemble_kernel(count, rows, *refs):
    own, other, out = refs[:count], refs[count:-1], refs[-1]
    where = [(part, at) for part in other for at in range(0, part.shape[0], rows)]
    for step, (part, at) in enumerate(where):
        out[place(count, rows, step, 0), :] = own[step][...]
        out[place(count, rows, step, 1), :] = part[at : at + rows, :]


def assemble(own, other):
    count = len(own)
    rows, columns = own[0].shape
    shape = (2 * count * rows, columns)
    return call(functools.partial(assemble_kernel, count, rows), [(shape, bf16)], 1.5, "assemble")(*own, *other)[0]


def assemble_pairs_kernel(count, rows, *refs):
    pairs, out = refs[:count], refs[count]
    for step in range(count):
        for side in range(2):
            out[place(count, rows, step, side), :] = pairs[step][side * rows : (side + 1) * rows, :]


def assemble_pairs(pairs):
    count = len(pairs)
    rows, columns = pairs[0].shape[0] // 2, pairs[0].shape[1]
    shape = (2 * count * rows, columns)
    return call(functools.partial(assemble_pairs_kernel, count, rows), [(shape, bf16)], 1.5, "assemble_pairs")(*pairs)[0]


def norm1_kernel(x_hbm, *refs):
    sources, vec_ref, out_ref, x_ref, held, sems = refs[:8], *refs[8:]
    copies = fetch([(x_hbm, x_ref), *[(source, held.at[row]) for row, source in enumerate(sources)]], sems)
    for copy in copies[1:]:
        copy.wait()
    for row in range(8):
        for part in range(sources[0].shape[0]):
            vec_ref[row : row + 1, part * 128 : (part + 1) * 128] = held[row, part : part + 1, :].astype(f32)
    copies[0].wait()
    for at in PARTS:
        unit, _ = normalize(x_ref[at, :].astype(f32))
        out_ref[at, :] = (unit * vec_ref[1:2, :] + vec_ref[2:3, :]).astype(bf16)


def norm1(x, vectors):
    rows, width = x.shape
    vectors = [vector.reshape(-1, 128) for vector in vectors]
    outs = [((8, width), f32), ((rows, width), bf16)]
    scratch = [pltpu.VMEM((rows, width), bf16), pltpu.VMEM((8, *vectors[0].shape), bf16), pltpu.SemaphoreType.DMA((9,))]
    return call(norm1_kernel, outs, 3, "norm1", scratch, range(9), VMEM_MOST)(x, *vectors)


def pack_kernel(qkv_hbm, proj_hbm, fc2_hbm, a_ref, t_ref, qkv_ref, proj_ref, fc2_ref, sems):
    copies = fetch([(qkv_hbm, qkv_ref), (proj_hbm, proj_ref), (fc2_hbm, fc2_ref)], sems)
    copies[0].wait()
    for i in range(3):
        a_ref[:, i * WIDTH : (i + 1) * WIDTH] = qkv_ref[i]
    copies[1].wait()
    copies[2].wait()
    turned = proj_ref.shape[0] == WIDTH
    a_ref[:, 3 * WIDTH :] = proj_ref[...].T if turned else proj_ref[...]
    t_ref[...] = fc2_ref[...].T if turned else fc2_ref[...]


def pack(qkv_weight, proj_weight, fc2_weight):
    rows, hidden = fc2_weight.shape[1], fc2_weight.shape[0]
    outs = [((rows, 4 * WIDTH), bf16), ((rows, hidden), bf16)]
    if rows % 128:
        proj_weight, fc2_weight = proj_weight.T, fc2_weight.T
    scratch = [pltpu.VMEM((3, rows, WIDTH), bf16), pltpu.VMEM(proj_weight.shape, bf16), pltpu.VMEM(fc2_weight.shape, bf16)]
    scratch.append(pltpu.SemaphoreType.DMA((3,)))
    return call(pack_kernel, outs, 1, "pack", scratch, (0, 1, 2), VMEM_MOST)(qkv_weight.transpose(1, 0, 2), proj_weight, fc2_weight)


def qkv_kernel(count, rows, *refs):
    pieces = refs[: 2 * count]
    normed_hbm, vec_hbm, w_ref, p_ref, q_ref, k_ref, v_ref, normed_ref, vec_ref, sems = refs[2 * count :]
    pairs = [(normed_hbm, normed_ref), (vec_hbm, vec_ref)]
    for side in range(2):
        for step in range(count):
            at, index = place(count, rows, step, side), side * count + step
            pairs.append((pieces[index].at[:, pl.ds(0, 3 * WIDTH)], w_ref.at[at]))
            pairs.append((pieces[index].at[:, pl.ds(3 * WIDTH, WIDTH)], p_ref.at[at]))
    for copy in fetch(pairs, sems):
        copy.wait()
    for at in PARTS:
        projected = dot_nn(normed_ref[at, :], w_ref[...])
        queries = (projected[:, :WIDTH] + vec_ref[6:7, :WIDTH]).astype(bf16)
        q_ref[at, :] = (queries.astype(f32) * HD ** (-0.5)).astype(bf16)
        k_ref[at, :] = projected[:, WIDTH : 2 * WIDTH].astype(bf16)
        v_ref[at, :] = (projected[:, 2 * WIDTH :] + vec_ref[6:7, WIDTH : 2 * WIDTH]).astype(bf16)


def qkv(count, pieces, normed, vec):
    rows = pieces[0].shape[0]
    tokens, width = normed.shape
    outs = [((width, 3 * WIDTH), bf16), ((width, WIDTH), bf16), *[((tokens, WIDTH), bf16)] * 3]
    scratch = [pltpu.VMEM(normed.shape, bf16), pltpu.VMEM(vec.shape, f32), pltpu.SemaphoreType.DMA((4 * count + 2,))]
    kernel = functools.partial(qkv_kernel, count, rows)
    return call(kernel, outs, 4, "qkv", scratch, range(2 * count + 2))(*pieces, normed, vec)


def head_mask(shape, head):
    lane = lax.broadcasted_iota(jnp.int32, shape, len(shape) - 1)
    return (lane >= head * HD) & (lane < (head + 1) * HD)


def fwd_near_kernel(q_ref, k_ref, v_ref, o_ref, m_ref, l_ref):
    keys, values = k_ref[...], v_ref[...]
    for at in PARTS:
        q = q_ref[at, :]
        o, m, total = (jnp.zeros(q.shape, f32) for _ in range(3))
        for head in range(HEADS):
            mask = head_mask(q.shape, head)
            scores = dot_nt(jnp.where(mask, q, jnp.zeros_like(q)), keys)
            top = jnp.max(scores, axis=-1, keepdims=True)
            weights = jnp.exp(scores - top)
            row_sum = jnp.sum(weights, axis=-1, keepdims=True)
            mixed = dot_nn(weights.astype(bf16), values)
            o = jnp.where(mask, mixed, o)
            m = jnp.where(mask, top, m)
            total = jnp.where(mask, row_sum, total)
        o_ref[at, :] = o
        m_ref[at, :] = m
        l_ref[at, :] = total


def fwd_far_kernel(q_ref, k_ref, v_ref, o_ref, m_ref, l_ref, p_ref, mix_ref, lse_ref, keep_ref, *sends):
    keys, values = k_ref[...], v_ref[...]
    for at in PARTS:
        q = q_ref[at, :]
        o, m, total = o_ref[at, :], m_ref[at, :], l_ref[at, :]
        o_out = jnp.zeros(q.shape, f32)
        lse = jnp.zeros((q.shape[0], 128), f32)
        lane = lax.broadcasted_iota(jnp.int32, lse.shape, 1)
        for head in range(HEADS):
            mask = head_mask(q.shape, head)
            scores = dot_nt(jnp.where(mask, q, jnp.zeros_like(q)), keys)
            before = m[:, head * HD : head * HD + 1]
            top = jnp.maximum(jnp.max(scores, axis=-1, keepdims=True), before)
            weights = jnp.exp(scores - top)
            carry = jnp.exp(before - top)
            row_sum = jnp.sum(weights, axis=-1, keepdims=True) + carry * total[:, head * HD : head * HD + 1]
            mixed = dot_nn(weights.astype(bf16), values) + carry * o
            o_out = jnp.where(mask, mixed / row_sum, o_out)
            lse = jnp.where(lane == head, top + jnp.log(row_sum), lse)
        mixture = o_out.astype(bf16)
        mix_ref[at, :] = mixture
        lse_ref[at, :] = lse
        send_terms(at, mixture, p_ref, keep_ref, sends)


def attention_near(q, k, v):
    return call(fwd_near_kernel, [(q.shape, f32)] * 3, 6, "attention_near")(q, k, v)


def attention_far(q, k, v, o, m, total, proj_t):
    rows = q.shape[0]
    outs = [(q.shape, bf16), ((rows, 128), f32), *term_shapes(rows, proj_t.shape[0])]
    return call(fwd_far_kernel, outs, 8, "attention_far")(q, k, v, o, m, total, proj_t)


def merge(out, refs):
    width = out.shape[1]
    for i, ref in enumerate(refs):
        out[:, core_columns(width, i // 2, i % 2)] = ref[...].astype(out.dtype)


def mlp_kernel(
    sum_1, sum_2, sum_3, sum_4, x_ref, g_ref, vec_ref, w1_ref, w2_ref,
    mid_ref, second_ref, hidden_ref, d_pre_ref, sums_ref, keep_ref, send_1, send_2, x_held, g_held, sems,
):
    pairs = [pair for at in PARTS for pair in ((x_ref.at[at], x_held.at[at]), (g_ref.at[at], g_held.at[at]))]
    copies = fetch(pairs, sems)
    merge(mid_ref, (sum_1, sum_2, sum_3, sum_4))
    sums_ref[...] = jnp.zeros_like(sums_ref)
    for i, at in enumerate(PARTS):
        copies[2 * i].wait()
        middle = mid_ref[at, :] + x_held[at, :].astype(f32) + vec_ref[0:1, :]
        mid_ref[at, :] = middle
        unit, _ = normalize(middle)
        second = (unit * vec_ref[3:4, :] + vec_ref[4:5, :]).astype(bf16)
        second_ref[at, :] = second
        copies[2 * i + 1].wait()
        grad = g_held[at, :]
        sums_ref[1:2, :] += column_sum(grad.astype(f32))
        pre = dot_nn(second, w1_ref[...]) + vec_ref[7:8, :]
        upper = 0.5 + 0.5 * lax.erf(pre * (0.5**0.5))
        hidden_ref[at, :] = (pre * upper).astype(bf16)
        slope = upper + pre * (jnp.exp(-0.5 * pre * pre) * 0.3989422804014327)
        d_pre = (slope * dot_nn(grad, w2_ref[...])).astype(bf16)
        d_pre_ref[at, :] = d_pre
        sums_ref[0:1, :] += column_sum(d_pre.astype(f32))
        send_terms(at, d_pre, w1_ref, keep_ref, (send_1, send_2))


def mlp(sums, x, g, vec, w1, w2):
    (rows, width), hidden = x.shape, w1.shape[1]
    outs = [(x.shape, f32), (x.shape, bf16), ((rows, hidden), bf16), ((rows, hidden), bf16), ((8, width), f32)]
    outs += term_shapes(rows, width)
    scratch = [pltpu.VMEM(x.shape, bf16), pltpu.VMEM(x.shape, bf16), pltpu.SemaphoreType.DMA((4,))]
    return call(mlp_kernel, outs, 8, "mlp", scratch, (4, 5), VMEM_MLP)(*sums, x, g, vec, w1, w2)


def mlp_out_kernel(hidden_ref, w2_ref, keep_ref, *sends):
    for at in PARTS:
        send_terms(at, hidden_ref[at, :], w2_ref, keep_ref, sends)


def mlp_out(hidden, w2):
    return call(mlp_out_kernel, term_shapes(hidden.shape[0], w2.shape[0]), 2, "mlp_out")(hidden, w2)


def layer_out_kernel(sum_1, sum_2, sum_3, sum_4, mid_ref, vec_ref, out_ref, work_ref):
    merge(work_ref, (sum_1, sum_2, sum_3, sum_4))
    for at in PARTS:
        out_ref[at, :] = (mid_ref[at, :] + work_ref[at, :] + vec_ref[5:6, :]).astype(bf16)


def layer_out(sums, middle, vec):
    scratch = [pltpu.VMEM(middle.shape, f32)]
    return call(layer_out_kernel, [(middle.shape, bf16)], 2, "layer_out", scratch)(*sums, middle, vec)[0]


def spread(count, grads_ref, *outs):
    rows, sends = grads_ref.shape[0] // (2 * count), outs[count:]
    each = count // len(sends)
    for step in range(count):
        outs[step][...] = grads_ref[place(count, rows, step, 0), :]
        out, at = sends[len(sends) - 1 - step // each], (step % each) * rows
        out[at : at + rows, :] = grads_ref[place(count, rows, step, 1), :].astype(bf16)


def grad_1_kernel(count, left, right, *refs):
    outs, grads_ref = refs[:-1], refs[-1]
    grads_ref[...] = dot_tn(left[...], right[...])
    rows = grads_ref.shape[0] // (2 * count)
    for step, out in enumerate(outs):
        for side in range(2):
            out[side * rows : (side + 1) * rows, :] = grads_ref[place(count, rows, step, side), :].astype(out.dtype)


def grad_1(count, left, right):
    width, columns = left.shape[1], right.shape[1]
    scratch, shape = [pltpu.VMEM((width, columns), f32)], (width // count, columns)
    outs = [*[(shape, f32)] * (count - 1), (shape, bf16)]
    return call(functools.partial(grad_1_kernel, count), outs, 3, "grad_1", scratch)(left, right)


def grad_2_kernel(count, left, right, *refs):
    outs, grads_ref = refs[:-1], refs[-1]
    grads_ref[...] = dot_tn(left[...], right[...])
    spread(count, grads_ref, *outs)


def grad_proj_kernel(low, mixture, out_ref):
    out_ref[...] = dot_tn(low[...], mixture[...])


def grad_a_kernel(count, normed, d_proj, proj_grad, *refs):
    outs, grads_ref = refs[:-1], refs[-1]
    grads_ref[:, : 3 * WIDTH] = dot_tn(normed[...], d_proj[...])
    grads_ref[:, 3 * WIDTH :] = proj_grad[...]
    spread(count, grads_ref, *outs)


def weight_grad(kernel, count, width, columns, micros, sends, *arrays):
    scratch = [pltpu.VMEM((width, columns), f32)]
    keep, send = ((width // 2 // count, columns), f32), ((width // 2 // sends, columns), bf16)
    results = call(functools.partial(kernel, count), [keep] * count + [send] * sends, micros, kernel.__name__, scratch)(*arrays)
    return results[:count], results[count:]


def picked_rows(pick, values, terms):
    total = 0.0
    for _ in range(terms):
        part = values.astype(bf16)
        total = total + dot_nt(pick.astype(bf16), part)
        values = values - part.astype(f32)
    return total


def norm2_back_kernel(
    sum_1, sum_2, sum_3, sum_4, mid_ref, g_ref, vec_ref, p_ref, mix_ref, lse_ref,
    low_ref, d_mix_ref, delta_ref, lse_out_ref, sums_ref, work_ref, both_ref,
):
    merge(work_ref, (sum_1, sum_2, sum_3, sum_4))
    sums_ref[...] = jnp.zeros_like(sums_ref)
    for at in PARTS:
        d_second = work_ref[at, :]
        unit, inverse = normalize(mid_ref[at, :])
        sums_ref[2:3, :] += column_sum(d_second * unit)
        sums_ref[3:4, :] += column_sum(d_second)
        d_middle = g_ref[at, :].astype(f32) + normalize_back(unit, inverse, d_second * vec_ref[3:4, :])
        low = d_middle.astype(bf16)
        low_ref[at, :] = low
        sums_ref[4:5, :] += column_sum(low.astype(f32))
        d_mix = dot_nn(low, p_ref[...]).astype(bf16)
        d_mix_ref[at, :] = d_mix
        both_ref[at, :] = d_mix.astype(f32) * mix_ref[at, :].astype(f32)
    head = lax.broadcasted_iota(jnp.int32, (8, WIDTH), 0)
    lane = lax.broadcasted_iota(jnp.int32, (8, WIDTH), 1)
    pick, one = (lane // HD == head).astype(f32), (lane == head).astype(f32)[:, :128]
    delta_ref[...] = picked_rows(pick, both_ref[...], 2)
    lse_out_ref[...] = picked_rows(one, lse_ref[...], 3)


def norm2_back(sums, middle, g, vec, proj_t, mixture, lse):
    rows, width = middle.shape
    outs = [((rows, width), bf16), ((rows, WIDTH), bf16), ((8, rows), f32), ((8, rows), f32), ((8, width), f32)]
    scratch = [pltpu.VMEM((rows, width), f32), pltpu.VMEM((rows, WIDTH), f32)]
    return call(norm2_back_kernel, outs, 6, "norm2_back", scratch)(*sums, middle, g, vec, proj_t, mixture, lse)


def bwd_kernel(heads, q_ref, k_ref, v_ref, do_ref, lse_ref, delta_ref, dkv_ref, dq_ref):
    rows, count = k_ref.shape[0], len(heads)
    for place, head in enumerate(heads):
        at = slice(head * HD, (head + 1) * HD)
        low, high = (slice(i * HD, (i + 1) * HD) for i in (place, count + place))
        keys, values, q, d_out = k_ref[:, at], v_ref[:, at], q_ref[:, at], do_ref[:, at]
        probs = jnp.exp(dot_nt(keys, q) - lse_ref[head : head + 1, :])
        d_probs = dot_nt(values, d_out)
        dkv_ref[:rows, high] = dot_nn(probs.astype(bf16), d_out).astype(dkv_ref.dtype)
        d_scores = (probs * (d_probs - delta_ref[head : head + 1, :])).astype(bf16)
        dkv_ref[:rows, low] = dot_nn(d_scores, q).astype(dkv_ref.dtype)
        dq_ref[low, :] = dot_tn(keys, d_scores)
    if dkv_ref.shape[0] > rows:
        dkv_ref[rows:, :] = jnp.zeros((dkv_ref.shape[0] - rows, dkv_ref.shape[1]), dkv_ref.dtype)


def attention_back(heads, dtype, more, q, k, v, d_out, lse, delta):
    rows = k.shape[0] + more
    outs = [((rows, 2 * len(heads) * HD), dtype), ((len(heads) * HD, q.shape[0]), f32)]
    kernel = functools.partial(bwd_kernel, heads)
    return call(kernel, outs, 3 * len(heads), "attention_back")(q, k, v, d_out, lse, delta)


def qkv_back_kernel(
    dq_one, dq_two, dq_here, dkv_here, back_one, back_two, w_ref, d_proj_ref, sums_ref, keep_ref, *sends
):
    rows, half = dkv_here.shape[0], WIDTH // 2
    sums_ref[...] = jnp.zeros_like(sums_ref)
    for place, (away, back) in enumerate(((dq_one, back_one), (dq_two, back_two))):
        at = slice(place * half, (place + 1) * half)
        d_query = ((away[...] + dq_here[at, :]).T * HD ** (-0.5)).astype(bf16)
        d_proj_ref[:, at] = d_query
        sums_ref[7:8, at] = column_sum(d_query.astype(f32))
        for part in range(2):
            here = slice(part * WIDTH + place * half, part * WIDTH + (place + 1) * half)
            there = slice(part * half, (part + 1) * half)
            value = (dkv_here[:, here] + back[:rows, there].astype(f32)).astype(bf16)
            out = slice(WIDTH + part * WIDTH + place * half, WIDTH + part * WIDTH + (place + 1) * half)
            d_proj_ref[:, out] = value
            if part:
                sums_ref[7:8, here] = column_sum(value.astype(f32))
    for at in PARTS:
        send_terms(at, d_proj_ref[at, :], w_ref, keep_ref, sends)


def qkv_back(dq_one, dq_two, dq_here, dkv_here, back_one, back_two, w):
    rows, width = dkv_here.shape[0], w.shape[0]
    outs = [((rows, 3 * WIDTH), bf16), ((8, width), f32), *term_shapes(rows, width)]
    return call(qkv_back_kernel, outs, 3, "qkv_back")(dq_one, dq_two, dq_here, dkv_here, back_one, back_two, w)


def norm1_back_kernel(
    sum_1, sum_2, sum_3, sum_4, low_ref, x_ref, vec_ref, sums_1, sums_2, sums_3, out_ref, sums_ref, work_ref, low_held, x_held, sems
):
    pairs = [pair for at in PARTS for pair in ((x_ref.at[at], x_held.at[at]), (low_ref.at[at], low_held.at[at]))]
    copies = fetch(pairs, sems)
    merge(work_ref, (sum_1, sum_2, sum_3, sum_4))
    sums_ref[...] = sums_1[...] + sums_2[...] + sums_3[...]
    for i, at in enumerate(PARTS):
        copies[2 * i].wait()
        unit, inverse = normalize(x_held[at, :].astype(f32))
        d_normed = work_ref[at, :]
        d_in = normalize_back(unit, inverse, d_normed * vec_ref[1:2, :])
        sums_ref[5:6, :] += column_sum(d_normed * unit)
        sums_ref[6:7, :] += column_sum(d_normed)
        copies[2 * i + 1].wait()
        out_ref[at, :] = (low_held[at, :].astype(f32) + d_in).astype(bf16)


def norm1_back(total, low, x, vec, *sums):
    scratch = [pltpu.VMEM(x.shape, f32), pltpu.VMEM(x.shape, bf16), pltpu.VMEM(x.shape, bf16)]
    outs, scratch = [(x.shape, bf16), (vec.shape, f32)], [*scratch, pltpu.SemaphoreType.DMA((4,))]
    return call(norm1_back_kernel, outs, 4, "norm1_back", scratch, (4, 5))(*total, low, x, vec, *sums)


def join_kernel(*refs):
    at = 0
    for ref in refs[:-1]:
        refs[-1][at : at + ref.shape[0], :] = ref[...]
        at += ref.shape[0]


def join(*pieces):
    rows = sum(piece.shape[0] for piece in pieces)
    return call(join_kernel, [((rows, pieces[0].shape[1]), bf16)], 1, "join")(*pieces)[0]


def layer(
    count,
    video_tokens,
    qkv_weight,
    q_bias,
    v_bias,
    proj_weight,
    proj_bias,
    norm1_gain,
    norm1_shift,
    norm2_gain,
    norm2_shift,
    fc1_weight,
    fc1_bias,
    fc2_weight,
    fc2_bias,
    out_grad,
):
    x, g = video_tokens[0], out_grad[0]
    tokens, width = x.shape
    hidden = fc1_bias.shape[0]
    order = Order()

    piece, piece_2 = order(pack, qkv_weight, proj_weight, fc2_weight)
    own_a, other_a = [piece], [ctx_swap(piece)]
    arrived_2 = ctx_swap(piece_2)
    qv_bias = jnp.concatenate([q_bias, v_bias, jnp.zeros((width - 2 * WIDTH,), bf16)])
    vec, normed = order(
        lambda x, *vectors: norm1(x, vectors),
        x, proj_bias, norm1_gain, norm1_shift, norm2_gain, norm2_shift, fc2_bias, qv_bias, fc1_bias,
    )
    pairs = []
    for step in range(1, count):
        before = own_a[-1]
        if step == 2:
            before = tie(before, other_a[0], normed)
        elif step > 2:
            before = tie(before, other_a[step - 2])
        if step == count - 1:
            pairs.append(order(join, piece_2, arrived_2))
            before = tie(before, pairs[0])
        own_a.append(ring_down(before, count))
        other_a.append(ctx_swap(own_a[-1]))
    half = count // 2

    own_1 = [tie(fc1_weight, own_a[-1], other_a[-2])]
    own_1.append(ring_down(own_1[-1], count))

    def next_1(until):
        while len(own_1) < until:
            own_1.append(ring_down(own_1[-1], count))

    def next_2(until):
        while len(pairs) < until:
            pairs.append(ring_down(pairs[-1], count))

    next_1(half)
    qkv_w, proj_t, queries, keys, values = order(
        lambda *values: qkv(count, values[: 2 * count], *values[2 * count :]), *own_a, *other_a, normed, vec
    )
    keys_far, values_far = ctx_swap(keys), ctx_swap(values)
    next_1(half + 1)
    next_2(half)
    partial = order(attention_near, queries, keys, values)
    both, each = order(join, own_1[-1], pairs[-1]), own_1[0].shape[0]
    while len(own_1) < count:
        both = ring_down(both, count)
        own_1.append(both[:each])
        pairs.append(both[each:])
    order.wait([keys_far, values_far])
    other_1 = [ctx_swap(order(join, *own_1[: half + 1]))]
    mixture, lse, *terms = order(attention_far, queries, keys_far, values_far, *partial, proj_t)
    attn = TpSum(order, False, *terms)
    attn.far()
    pairs[-1] = order(relay, pairs[-1])
    next_2(count)
    order.wait(other_1[0])
    other_1.append(ctx_swap(order(join, *own_1[half + 1 :])))
    w1 = order(lambda *pieces: assemble(pieces[:count], pieces[count:]), *own_1, *other_1)
    w2 = order(lambda *pieces: assemble_pairs(pieces), *pairs)
    attn.back()

    middle, second, hidden_b, d_pre, sums_1, *terms = order(lambda *values: mlp(values[:4], *values[4:]), *attn.result, x, g, vec, w1, w2)
    d_second = TpSum(order, False, *terms)
    blocks_2 = order(functools.partial(weight_grad, grad_2_kernel, count, width, hidden, 3, 1), g, hidden_b)
    d_second.far()
    blocks_1 = order(functools.partial(grad_1, count), second, d_pre)
    grads = PairScatter(order, count, blocks_1, *blocks_2)
    out_sum = TpSum(order, False, *order(mlp_out, hidden_b, w2))
    d_second.back()
    out_sum.far()
    low, d_mix, delta, lse_row, sums_2 = order(
        lambda *values: norm2_back(values[:4], *values[4:]), *d_second.result, middle, g, vec, proj_t, mixture, lse
    )

    grads.joint()
    state = (d_mix, lse_row, delta)
    first, second_pair = (0, 1), (2, 3)
    dkv_one, dq_one = order(functools.partial(attention_back, first, bf16, 16), queries, keys_far, values_far, *state)
    back_one = ctx_swap(dkv_one)
    dkv_two, dq_two = order(functools.partial(attention_back, second_pair, bf16, 0), queries, keys_far, values_far, *state)
    back_two = ctx_swap(dkv_two)
    dkv_here, dq_here = order(functools.partial(attention_back, (0, 1, 2, 3), f32, 0), queries, keys, values, *state)
    for _ in range(1, count - 2):
        grads.joint()
    proj_grad = order(call(grad_proj_kernel, [((width, WIDTH), f32)], 1, "grad_proj"), low, mixture)[0]
    order.wait(out_sum.arrived)
    d_proj, sums_3, *terms = order(qkv_back, dq_one, dq_two, dq_here, dkv_here, back_one, back_two, qkv_w)
    d_normed = TpSum(order, True, *terms)
    blocks_a = order(
        functools.partial(weight_grad, grad_a_kernel, count, width, 4 * WIDTH, 4, 2), normed, d_proj, proj_grad
    )
    grad_a = SwapScatter(order, count, *blocks_a)
    d_normed.far()
    order.wait(grads.arrived)
    grad_a.step()
    order.wait(grad_a.arrived)
    d_normed.back()
    for _ in range(1, half):
        grad_a.step()
    grads.ends()
    order.wait(grad_a.lower)
    input_grad, sums = order(
        lambda *values: norm1_back(values[:4], *values[4:]), *d_normed.result, low, x, vec, sums_1, sums_2, sums_3
    )
    out_sum.back()
    for _ in range(half, count - 1):
        grad_a.step()
    swaps = exchanges(count)
    sums = order(add, sums, swaps[0](sums))
    order.wait(grads.arrived)
    out_rows = order(lambda *values: layer_out(values[:4], *values[4:]), *out_sum.result, middle, vec)
    for swap in swaps[1:-1]:
        order.wait(grad_a.arrived)
        sums = order(add, sums, swap(sums))
    grad_a.step(finish_a)
    grads.last_second(finish_2)
    grads.last_first()
    grad_qkv, grad_proj = grad_a.result
    sums = order(finish_sums, sums, swaps[-1](sums))
    g_fc1_bias, g_fc2_bias, g_gain_two, g_shift_two, g_proj_bias, g_gain_one, g_shift_one, g_q_bias, g_v_bias = sums
    return (
        out_rows[None],
        input_grad[None],
        grad_qkv,
        g_q_bias,
        g_v_bias,
        grad_proj,
        g_proj_bias,
        g_gain_one,
        g_shift_one,
        g_gain_two,
        g_shift_two,
        grads.first,
        g_fc1_bias,
        grads.second,
        g_fc2_bias,
    )


def solution(mesh):
    split = ("shard", "ctx")
    tokens, rows, columns = P("shard", "ctx", None), P(split, "tp"), P("tp", split)
    stack = P(split, None, "tp")
    own, copied = P("tp"), P()
    in_specs = (
        tokens,
        stack,
        own,
        own,
        columns,
        copied,
        copied,
        copied,
        copied,
        copied,
        rows,
        own,
        columns,
        copied,
        tokens,
    )
    out_specs = (
        tokens,
        tokens,
        stack,
        own,
        own,
        columns,
        copied,
        copied,
        copied,
        copied,
        copied,
        rows,
        own,
        columns,
        copied,
    )
    return jax.shard_map(
        functools.partial(layer, mesh.shape["shard"]),
        mesh=mesh,
        in_specs=in_specs,
        out_specs=out_specs,
        check_vma=False,
    )
```
